128 devices in a mesh: dp: 2 (over x_lo), seq: 16 (over x_hi, z, core), mp: 4 (over y).
Axes of the slice: x: 4 (x_hi: 2, x_lo: 2; x = x_hi * 2 + x_lo), y: 4, z: 4, core: 2. Of those that a mesh axis runs over, the one named last changes fastest.
Arguments:
- enc_out: bfloat16 [2, 4096, 4096], P('dp', 'seq'), may hold values from -6 to 6
- dec_query: bfloat16 [2, 4096, 2048], P('dp', 'seq', 'mp'), may hold values from -64 to 64
- ctx_grad: bfloat16 [2, 4096, 2048], P('dp', 'seq', 'mp'), may hold values from -6 to 6
- kv_weight: bfloat16 [2, 4096, 2048], P(None, ('dp', 'seq'), 'mp'), may hold values from -0.09375 to 0.09375
- enc_seg: int32 [2, 4096], P('dp'), may hold values from 0 to 3, never falling along the last dimension, each value on 1 to 2048 neighbouring positions
- dec_seg: int32 [2, 4096], P('dp', 'seq'), may hold values from 0 to 3, never falling along the last dimension, each value on 1 to 2048 neighbouring positions
Outputs:
- enc_grad: bfloat16 [2, 4096, 4096], P('dp', 'seq', 'mp')
- query_grad: bfloat16 [2, 4096, 2048], P('dp', 'seq', 'mp')
- kv_weight_grad: float32 [2, 4096, 2048], P(None, ('dp', 'seq'), 'mp')
The draws below stay inside these ranges and needn't reach their ends.
Inputs may be any that keep to these rules, and one draw needn't show every extreme that they name: `enc_seg`: each replica's ids never fall along the positions, every id appears, and each pair covers at most 2048 positions. `dec_seg`: each replica's ids never fall along the positions, every id appears, and each pair covers at most 2048 positions.
All inputs are finite; a program needn't handle non-finite values.
Results may differ from the reference program's by a relative error of at most 0.034.
The reference program's roundings to bfloat16 on the way count: a program that leaves them out, or rounds other values in their place, can miss the bound.
Values may be sent and summed in bfloat16 or wider, within the bound.
A program may use at most 128 MiB of HBM per device.

```python
import math
import jax
import jax.numpy as jnp
import numpy as np
from jax import lax

D = 4096
HEADS = 32
DH = 64
TOK_DEV = 256
SEGS = 4
SEQ_LEN = 4096
INNER = 2048
N_DP = 2
N_SEQ = 16
N_MP = 4


def draw_dec_query(key, part):
    key = jax.random.fold_in(key, 7)
    base_key = jax.random.fold_in(key, 0)
    values = jax.random.normal(base_key, (N_DP, SEQ_LEN, HEADS * DH), jnp.float32)
    values = jnp.clip(values, -8.0, 8.0)
    return values.astype(jnp.bfloat16)


def steps_of(key, extent, pieces, least, largest):
    level, own = 1.0, jax.random.fold_in(key, 6)
    for position, shards_of in pieces:
        draws = jnp.exp(jax.random.uniform(jax.random.fold_in(own, position), (shards_of,), jnp.float32, least / len(pieces), largest / len(pieces)))
        level = level * jnp.repeat(draws, extent[position] // shards_of).reshape([-1 if axis == position else 1 for axis in range(len(extent))])
    return level


def split_up(count, total, most, lean):
    portions = [(1 << 20) // math.isqrt(grade ** lean) + 1 for grade in range(2, count + 1)]
    surplus, counts = total - most - (count - 1), [1] * (count - 1)
    while surplus > 0:
        free = [i for i in range(count - 1) if counts[i] < most]
        mass, remaining = sum([portions[i] for i in free]), surplus
        for i in free:
            more = min(most - counts[i], max(1, remaining * portions[i] // mass), surplus)
            counts[i] = counts[i] + more
            surplus = surplus - more
    return np.array([most] + counts)


def uneven_parts(stream_key, number_of, total, limit, slope):
    if number_of == 2:
        one = jax.random.randint(stream_key, (), max(1, total - limit), min(limit, total - 1) + 1)
        return jnp.stack([one, total - one])
    lengths = jnp.asarray(split_up(number_of, total, limit, slope), jnp.int32)
    twos = (number_of - 1) // 2
    donor, sink = lengths[1:1 + 2 * twos:2], lengths[2:2 + 2 * twos:2]
    slack = jnp.minimum(donor - 1, limit - sink)
    passed = jax.random.randint(jax.random.fold_in(stream_key, 1), (twos,), 0, 1 << 20) % (slack + 1)
    lengths = lengths.at[1:1 + 2 * twos:2].set(donor - passed).at[2:2 + 2 * twos:2].set(sink + passed)
    return lengths[jax.random.permutation(jax.random.fold_in(stream_key, 2), number_of)]


def noise(own_key, dims, scale, bound, cuts=(), kind=jnp.bfloat16):
    entries = jax.random.normal(own_key, dims, jnp.float32) * scale
    if len(cuts) > 0:
        entries = steps_of(own_key, dims, cuts, -0.22, 0.18) * entries
    return jnp.clip(entries, min=-bound, max=bound).astype(kind)


def setup_inputs(seed: int = 0) -> dict:
    arg_keys = jax.random.split(jax.random.key(seed), 7)
    return {
        "enc_out": noise(arg_keys[0], (N_DP, SEQ_LEN, D), 1.0, 6.0, ((0, 2), (1, 16))),
        "dec_query": draw_dec_query(jax.random.fold_in(arg_keys[6], 71), 0),
        "ctx_grad": noise(arg_keys[2], (N_DP, SEQ_LEN, INNER), 1.0, 6.0, ((0, 2), (1, 16), (2, 4))),
        "kv_weight": noise(arg_keys[3], (2, D, INNER), D ** -0.5, 0.09375, ((1, 32), (2, 4))),
        "enc_seg": jax.vmap(lambda own: jnp.searchsorted(jnp.cumsum(uneven_parts(own, SEGS, SEQ_LEN, SEQ_LEN // 2, 0)), jnp.arange(SEQ_LEN), side="right"))(jax.random.split(arg_keys[4], N_DP)).reshape((N_DP, SEQ_LEN)).astype(jnp.int32),
        "dec_seg": jax.vmap(lambda own: jnp.searchsorted(jnp.cumsum(uneven_parts(own, SEGS, SEQ_LEN, SEQ_LEN // 2, 0)), jnp.arange(SEQ_LEN), side="right"))(jax.random.split(arg_keys[5], N_DP)).reshape((N_DP, SEQ_LEN)).astype(jnp.int32),
    }


SCALE = 0.125
NEG = -1e30


def head_backward(query, grad_out, keys, values, mask):
    scores = jnp.where(mask, jnp.dot(query, keys.T, preferred_element_type=jnp.float32) * SCALE, NEG)
    top = jnp.max(scores, axis=-1, keepdims=True)
    weights = jnp.exp(scores - top)
    probs = weights / jnp.sum(weights, axis=-1, keepdims=True)
    probs_low = probs.astype(jnp.bfloat16)
    context = jnp.dot(probs_low, values, preferred_element_type=jnp.float32)
    delta = jnp.sum(grad_out.astype(jnp.float32) * context, axis=-1, keepdims=True)
    dprobs = jnp.dot(grad_out, values.T, preferred_element_type=jnp.float32)
    dscores = (probs * (dprobs - delta) * SCALE).astype(jnp.bfloat16)
    return probs_low, dscores, jnp.dot(dscores, keys, preferred_element_type=jnp.float32)


def block_sum(left, right):
    left_blocks = left.reshape(N_SEQ, TOK_DEV, left.shape[1]).astype(jnp.float32)
    right_blocks = right.reshape(N_SEQ, TOK_DEV, right.shape[1]).astype(jnp.float32)
    parts = jnp.einsum("nqk,nqd->nkd", left_blocks, right_blocks).astype(jnp.bfloat16)
    parts = lax.optimization_barrier(parts)
    return jnp.sum(parts.astype(jnp.float32), axis=0)


def split_heads(array):
    return array.reshape(array.shape[0], HEADS, DH).transpose(1, 0, 2)


def join_heads(array):
    return array.transpose(1, 0, 2).reshape(array.shape[1], HEADS * DH)


def reference(enc_out, dec_query, ctx_grad, kv_weight, enc_seg, dec_seg):
    enc_list = []
    query_list = []
    weight_total = jnp.zeros((2, D, HEADS * DH), jnp.float32)
    for replica in range(N_DP):
        encoder = enc_out[replica]
        projected = jnp.einsum("td,cdh->cth", encoder.astype(jnp.float32), kv_weight.astype(jnp.float32)).astype(jnp.bfloat16)
        mask = dec_seg[replica][:, None] == enc_seg[replica][None, :]

        def one_head(items):
            query, grad_out, keys, values = items
            probs_low, dscores, dquery = head_backward(query, grad_out, keys, values, mask)
            return dquery, block_sum(dscores, query), block_sum(probs_low, grad_out)

        dquery, dkeys, dvalues = lax.map(one_head, (split_heads(dec_query[replica]), split_heads(ctx_grad[replica]), split_heads(projected[0]), split_heads(projected[1])))
        query_list.append(join_heads(dquery).astype(jnp.bfloat16))
        kv_grads = jnp.stack([join_heads(dkeys), join_heads(dvalues)]).astype(jnp.bfloat16)
        group_cols = HEADS * DH // N_MP
        grads_grouped = kv_grads.reshape(2, SEQ_LEN, N_MP, group_cols).transpose(2, 0, 1, 3)
        weights_grouped = kv_weight.reshape(2, D, N_MP, group_cols).transpose(2, 0, 1, 3)

        def one_group(items):
            grad_part, weight_part = items
            return jnp.einsum("cth,cdh->td", grad_part.astype(jnp.float32), weight_part.astype(jnp.float32)).astype(jnp.bfloat16)

        parts = lax.optimization_barrier(lax.map(one_group, (grads_grouped, weights_grouped)))
        enc_list.append(jnp.sum(parts.astype(jnp.float32), axis=0).astype(jnp.bfloat16))
        weight_total = weight_total + jnp.einsum("td,cth->cdh", encoder.astype(jnp.float32), kv_grads.astype(jnp.float32))
    return jnp.stack(enc_list), jnp.stack(query_list), weight_total
```

```python
import functools

import jax
import jax.numpy as jnp
from jax import lax
from jax.experimental import pallas as pl
from jax.experimental.pallas import tpu as pltpu
from jax.sharding import PartitionSpec as P

MESH = pl.DeviceIdType.MESH
BF = jnp.bfloat16
F32 = jnp.float32
NEG = -1e30
KB = 256
RING = (2, 1, 3)


def coords():
    dp, seq, y = lax.axis_index("dp"), lax.axis_index("seq"), lax.axis_index("mp")
    xh = seq // 8
    return xh * 2 + dp, xh, (seq // 2) % 4, seq % 2, y


def dev(x, z, core, y):
    return (x % 2, (x // 2) * 8 + z * 2 + core, y)


def row_group(x):
    return (x % 2) * 2 + x // 2


def mod4(v):
    return (v + 4) % 4


def remote(src, dst, send, recv, device):
    return pltpu.make_async_remote_copy(
        src_ref=src, dst_ref=dst, send_sem=send, recv_sem=recv, device_id=device, device_id_type=MESH
    )


def arrived(dst, sem):
    pltpu.make_async_copy(dst, dst, sem).wait()


def greet(peers):
    barrier = pltpu.get_barrier_semaphore()
    for peer in peers:
        pl.semaphore_signal(barrier, inc=1, device_id=peer, device_id_type=MESH)
    pl.semaphore_wait(barrier, len(peers))


def lanes_of(shape):
    return lax.broadcasted_iota(jnp.int32, shape, 1)


def halves(first, second, shift_first, shift_second):
    first = pltpu.roll(first, 64, 1) if shift_first else first
    second = pltpu.roll(second, 64, 1) if shift_second else second
    return jnp.where(lanes_of(first.shape) < 64, first, second)


def front(
    enc, q, do, w, dseg, eseg,
    wg_out, kvx, kvt, xt, xs, dec_out,
    encv, wg, acc, kvs, kvb, qs, qb,
    loc, sib_s, sib_r, ws, wr, qsend, qrecv, ksend, krecv,
):
    x, xh, z, c, y = coords()
    me = row_group(x)
    t = xh * 4 + z
    sibling = dev(x, z, 1 - c, y)
    peers = [sibling]
    for dx in range(4):
        for dz in range(4):
            if dx == 0 and dz == 0:
                continue
            if dx in (0, 2) or dz == 0:
                peers.append(dev(mod4(x + dx), mod4(z + dz), c, y))
            if dx in (0, 2):
                peers.append(dev(mod4(x + dx), mod4(z + dz), 1 - c, y))
    greet(peers)

    own = pl.multiple_of(c * 256, 256)
    other = pl.multiple_of((1 - c) * 256, 256)
    rows = pl.ds(pl.multiple_of(c * 128, 128), 128)
    w_sib = remote(w.at[:, :, pl.ds(other, 256)], wg.at[:, me, z, rows], sib_s.at[0], sib_r.at[0], sibling)
    w_sib.start()
    w_loc = pltpu.make_async_copy(w.at[:, :, pl.ds(own, 256)], wg.at[:, me, z, rows], loc.at[0])
    w_loc.start()
    e_sib = remote(enc, encv.at[c], sib_s.at[1], sib_r.at[1], sibling)
    e_sib.start()
    e_loc = pltpu.make_async_copy(enc, encv.at[c], loc.at[1])
    e_loc.start()
    w_loc.wait()
    w_sib.wait()

    def to(a, dx, dz, step_x, step_z):
        bx, bz = mod4(x - (dx - step_x)), mod4(z - (dz - step_z))
        block = wg.at[a, row_group(bx), bz]
        copy = remote(
            block, block, ws.at[a, dx, dz], wr.at[a, dx, dz], dev(mod4(x + step_x), mod4(z + step_z), c, y)
        )
        copy.start()
        return copy

    sent = []
    for d in RING:
        sent.append(to(0, d, 0, d, 0))
        sent.append(to(1, 0, d, 0, d))
    for d in RING:
        sent.append(to(0, 0, d, 0, d))
        sent.append(to(1, d, 0, d, 0))

    for h in range(8):
        tile = pl.ds((h // 2) * 128, 128)
        odd = h % 2 == 1
        qs[h, 0:256, :] = halves(q[:, tile].astype(F32), do[:, tile].astype(F32), odd, not odd).astype(BF)
        qs[h, 256:272, :] = dseg[...].astype(BF)
    q_sent = []
    for dxh in (1, 0):
        for dz in (2, 1, 3, 0):
            if dxh == 0 and dz == 0:
                continue
            hx, hz = (xh + dxh) % 2, mod4(z + dz)
            copy = remote(
                qs.at[hx * 4 + hz], qb.at[t], qsend.at[dxh, dz], qrecv.at[dxh, dz],
                dev(mod4(x + 2 * dxh), hz, c, y),
            )
            copy.start()
            q_sent.append(copy)
    q_loc = pltpu.make_async_copy(qs.at[t], qb.at[t], loc.at[2])
    q_loc.start()

    def block_at(a, dx, dz):
        return wg.at[a, row_group(mod4(x - dx)), mod4(z - dz)]

    for d in (1, 3, 2):
        arrived(block_at(0, d, 0), wr.at[0, d, 0])
        for e in RING:
            sent.append(to(0, d, e, 0, e))
        arrived(block_at(1, 0, d), wr.at[1, 0, d])
        for e in RING:
            sent.append(to(1, e, d, e, 0))

    e_loc.wait()
    e_sib.wait()
    q_loc.wait()
    for dxh in range(2):
        for dz in range(4):
            if dxh or dz:
                src = ((xh + dxh) % 2) * 4 + mod4(z - dz)
                arrived(qb.at[src], qrecv.at[dxh, dz])

    def prepare(b, _):
        block = qb[b, 0:256, :]
        low = lanes_of((256, 128)) < 64
        zero = jnp.zeros_like(block)
        xs[b, 0:256, :] = jnp.where(low, block, zero)
        xs[b, 256:512, :] = jnp.where(low, zero, block)
        turned = block.T
        xt[b, 0:64, 0:256] = turned[0:64] * jnp.asarray(0.125, BF)
        xt[b, 64:128, 256:512] = turned[64:128]
        xt[b, 0:64, 256:512] = jnp.zeros((64, 256), BF)
        xt[b, 64:128, 0:256] = jnp.zeros((64, 256), BF)
        xt[b, 128:256, :] = jnp.zeros((128, 512), BF)
        ids = qb[b, 256:272, :].astype(F32)
        ids = jnp.concatenate([ids[0:1], ids[1:2]], axis=1)
        row = lax.broadcasted_iota(jnp.int32, (16, 256), 0)
        differs = (row < 4) & (row.astype(F32) != ids)
        xt[b, 128:144, 0:256] = jnp.where(differs, NEG, 0.0).astype(BF)
        dec_out[b] = jnp.broadcast_to(ids, (8, 256))
        return 0

    lax.fori_loop(0, 8, prepare, 0)

    def one_hot(i, _):
        seg = eseg[pl.ds(i, 1), :].astype(F32)
        row = lax.broadcasted_iota(jnp.int32, (128, 128), 0).astype(F32)
        hot = jnp.where(row == seg, 1.0, 0.0)
        kvx[pl.ds(pl.multiple_of(i * 128, 128), 128), 128:256] = hot.T.astype(BF)
        return 0

    lax.fori_loop(0, 32, one_hot, 0)

    def multiply(a, dx, dz, first):
        bx, bz = mod4(x - dx), mod4(z - dz)
        columns = pl.ds(pl.multiple_of((row_group(bx) * 4 + bz) * 256, 256), 256)
        for half in range(2):
            term = jnp.dot(encv[half, :, columns], wg[a, row_group(bx), bz], preferred_element_type=F32)
            if first:
                acc[a, pl.ds(half * 256, 256), :] = term
            else:
                acc[a, pl.ds(half * 256, 256), :] += term

    multiply(0, 0, 0, True)
    multiply(1, 0, 0, True)
    for d in (1, 3, 2):
        multiply(0, d, 0, False)
        multiply(1, 0, d, False)
    for d in (1, 3, 2):
        arrived(block_at(0, 0, d), wr.at[0, 0, d])
        multiply(0, 0, d, False)
        arrived(block_at(1, d, 0), wr.at[1, d, 0])
        multiply(1, d, 0, False)
    for d in (1, 3, 2):
        for e in (1, 3, 2):
            arrived(block_at(0, d, e), wr.at[0, d, e])
            multiply(0, d, e, False)
            arrived(block_at(1, e, d), wr.at[1, e, d])
            multiply(1, e, d, False)

    for j in range(4):
        tile = pl.ds((j // 2) * 128, 128)
        odd = j % 2 == 1
        kvs[j] = halves(acc[0, :, tile], acc[1, :, tile], odd, not odd).astype(BF)

    w_save = pltpu.make_async_copy(wg, wg_out, loc.at[3])
    w_save.start()
    ex = (c + 2 - xh) % 2
    tx = c * 2 + x % 2
    here = c == xh

    def kv_copy(dz, dc):
        hz = mod4(z + dz)
        return remote(
            kvs.at[hz], kvb.at[t], ksend.at[dz, dc], krecv.at[ex, dz], dev(tx, hz, (c + dc) % 2, y)
        )

    kv_loc = pltpu.make_async_copy(kvs.at[z], kvb.at[t], loc.at[4])
    k_sent = [kv_copy(dz, dc) for dz in (2, 1, 3) for dc in range(2)]
    for copy in k_sent:
        copy.start()
    kv_copy(0, 1).start()

    @pl.when(here)
    def _():
        kv_loc.start()

    @pl.when(jnp.logical_not(here))
    def _():
        kv_copy(0, 0).start()

    for e in (0, 1):
        for dz in (0, 1, 3, 2):
            src = ((xh + e) % 2) * 4 + mod4(z - dz)
            if e == 0 and dz == 0:

                @pl.when(here)
                def _():
                    kv_loc.wait()

                @pl.when(jnp.logical_not(here))
                def _():
                    arrived(kvb.at[t], krecv.at[0, 0])
            else:
                arrived(kvb.at[src], krecv.at[e, dz])
            block = kvb[src]
            span = pl.ds(pl.multiple_of(src * 512, 512), 512)
            kvx[span, 0:128] = block
            kvt[:, span] = block.T

    for copy in sent + q_sent + k_sent:
        copy.wait_send()
    kv_copy(0, 1).wait_send()

    @pl.when(jnp.logical_not(here))
    def _():
        kv_copy(0, 0).wait_send()

    w_save.wait()


def attend(kvx, kvt, xt, xs, dec, eseg, dkv_out, dq_out, tt, yy, dkv):
    dkv[...] = jnp.zeros_like(dkv)
    seg = eseg[...].astype(F32)

    def one_block(b, _):
        ids = dec[b]
        low, high = jnp.min(ids), jnp.max(ids)
        begin = jnp.sum(jnp.where(seg < low, 1.0, 0.0)).astype(jnp.int32)
        end = jnp.sum(jnp.where(seg <= high, 1.0, 0.0)).astype(jnp.int32)
        j0, j1 = begin // KB, (end + KB - 1) // KB

        def at(j):
            return pl.ds(pl.multiple_of(j * KB, KB), KB)

        def fold(op, v):
            return op(v.reshape(KB // 8, 8, 256), axis=0)

        def scores(j, top):
            both = jnp.dot(kvx[at(j), :], xt[b], preferred_element_type=F32)
            tt[at(j), :] = both
            return jnp.maximum(top, fold(jnp.max, both[:, 0:256]))

        top = lax.fori_loop(j0, j1, scores, jnp.full((8, 256), -3e38, F32))
        top = jnp.max(top, axis=0, keepdims=True)

        def weigh(j, total):
            e = jnp.exp(tt[at(j), 0:256] - top)
            tt[at(j), 0:256] = e
            return total + fold(jnp.sum, e)

        total = lax.fori_loop(j0, j1, weigh, jnp.zeros((8, 256), F32))
        inv = 1.0 / jnp.sum(total, axis=0, keepdims=True)

        def deltas(j, delta):
            low_p = (tt[at(j), 0:256] * inv).astype(BF)
            yy[at(j), 256:512] = low_p
            return delta + fold(jnp.sum, low_p.astype(F32) * tt[at(j), 256:512])

        delta = lax.fori_loop(j0, j1, deltas, jnp.zeros((8, 256), F32))
        delta = jnp.sum(delta, axis=0, keepdims=True)
        inv8 = inv * 0.125

        def grads(j, dq):
            ds = ((tt[at(j), 0:256] * inv8) * (tt[at(j), 256:512] - delta)).astype(BF)
            yy[at(j), 0:256] = ds
            dkv[at(j), :] += jnp.dot(yy[at(j), :], xs[b], preferred_element_type=F32)
            return dq + jnp.dot(kvt[0:64, at(j)], ds, preferred_element_type=F32)

        dq = lax.fori_loop(j0, j1, grads, jnp.zeros((64, 256), F32))
        dq_out[b] = jnp.concatenate([dq[:, 0:128], dq[:, 128:256]], axis=0).T.astype(BF)
        return 0

    lax.fori_loop(0, 8, one_block, 0)
    dkv_out[...] = dkv[...].astype(BF).reshape(dkv_out.shape)


def back(
    dkvp, dqp, enc, w,
    enc_out, q_out, w_out,
    encv, wv, rb, gt, gs, qg, sa, ra, s2, r2, oa, ys, yr, fin, fsib,
    loc, sib_s, sib_r, dsend, drecv, qsend, qrecv, asend, arecv, bsend, brecv, ysend, yrecv,
):
    x, xh, z, c, y = coords()
    me = row_group(x)
    sibling = dev(x, z, 1 - c, y)
    peers = [sibling]
    for dx in range(4):
        for dz in range(4):
            if dx == 0 and dz == 0:
                continue
            if dx in (0, 2) or dz == 0:
                peers.append(dev(mod4(x + dx), mod4(z + dz), c, y))
            if dx in (0, 2):
                peers.append(dev(mod4(x + dx), mod4(z + dz), 1 - c, y))
    for dy in range(1, 4):
        peers.append(dev(x, z, c, mod4(y + dy)))
    greet(peers)

    here = c == xh

    def d_copy(dxh, dz):
        tx, tz = (xh + dxh) % 2, mod4(z + dz)
        return remote(
            dkvp.at[tx * 4 + tz], rb.at[z, c], dsend.at[dxh, dz], drecv.at[dz, c],
            dev(tx * 2 + x % 2, tz, xh, y),
        )

    d_sent = [d_copy(dxh, dz) for dxh in (1, 0) for dz in (2, 1, 3, 0) if dxh or dz]
    for copy in d_sent:
        copy.start()
    d_loc = pltpu.make_async_copy(dkvp.at[xh * 4 + z], rb.at[z, c], loc.at[0])

    @pl.when(here)
    def _():
        d_loc.start()

    @pl.when(jnp.logical_not(here))
    def _():
        d_copy(0, 0).start()

    e_sib = remote(enc, encv.at[c], sib_s.at[0], sib_r.at[0], sibling)
    e_sib.start()
    e_loc = pltpu.make_async_copy(enc, encv.at[c], loc.at[1])
    e_loc.start()
    w_sib = remote(w, wv.at[c], sib_s.at[1], sib_r.at[1], sibling)
    w_sib.start()
    w_loc = pltpu.make_async_copy(w, wv.at[c], loc.at[2])
    w_loc.start()
    q_sent = []
    for dxh in (1, 0):
        for dz in (2, 1, 3, 0):
            if dxh or dz:
                tx, tz = (xh + dxh) % 2, mod4(z + dz)
                copy = remote(
                    dqp.at[tx * 4 + tz], qg.at[xh * 4 + z], qsend.at[dxh, dz], qrecv.at[dxh, dz],
                    dev(tx * 2 + x % 2, tz, c, y),
                )
                copy.start()
                q_sent.append(copy)
    q_loc = pltpu.make_async_copy(dqp.at[xh * 4 + z], qg.at[xh * 4 + z], loc.at[3])
    q_loc.start()

    for dz in (0, 1, 3, 2):
        j = mod4(z - dz)
        for s in range(2):
            if dz == 0:
                local = jnp.logical_and(here, c == s)

                @pl.when(local)
                def _():
                    d_loc.wait()

                @pl.when(jnp.logical_not(local))
                def _():
                    arrived(rb.at[j, s], drecv.at[0, s])
            else:
                arrived(rb.at[j, s], drecv.at[dz, s])
        turned = (rb[j, 0].astype(F32) + rb[j, 1].astype(F32)).astype(BF).T
        keys = pl.ds(pl.multiple_of(j * 64, 64), 64)
        gt[0, keys, :] = turned[0:64]
        gt[1, keys, :] = turned[64:128]

    own_tok = pl.ds(pl.multiple_of(c * 256, 256), 256)
    sib_tok = pl.ds(pl.multiple_of((1 - c) * 256, 256), 256)
    g_sib = remote(gt.at[:, :, sib_tok], gs.at[c], sib_s.at[2], sib_r.at[2], sibling)
    g_sib.start()
    gs_own = pltpu.make_async_copy(gt.at[:, :, own_tok], gs.at[c], loc.at[4])
    gs_own.start()
    e_loc.wait()
    e_sib.wait()

    def product(a, dx, dz):
        bx, bz = mod4(x + dx), mod4(z + dz)
        columns = pl.ds(pl.multiple_of((row_group(bx) * 4 + bz) * 256, 256), 256)
        return jnp.dot(gt[a, :, 0:256], encv[0, :, columns], preferred_element_type=F32) + jnp.dot(
            gt[a, :, 256:512], encv[1, :, columns], preferred_element_type=F32
        )

    a_sent = []

    def first_hop(far):
        for d in RING:
            for a in range(2):
                dx, dz = (far, d) if a == 0 else (d, far)
                sa[a, d - 1, far] = product(a, dx, dz).astype(BF)
                step_x, step_z = (0, d) if a == 0 else (d, 0)
                copy = remote(
                    sa.at[a, d - 1, far], ra.at[a, d - 1, far], asend.at[a, d - 1, far], arecv.at[a, d - 1, far],
                    dev(mod4(x + step_x), mod4(z + step_z), c, y),
                )
                copy.start()
                a_sent.append(copy)

    def enc_term(dy, r):
        group = mod4(y + dy)
        total = None
        for half in range(2):
            for a in range(2):
                term = jnp.dot(wv[half, a, group, r], gs[half, a], preferred_element_type=F32)
                total = term if total is None else total + term
        return total

    y_sent = []

    def to_group(dy):
        for r in range(4):
            ys[dy - 1, pl.ds(r * 256, 256), :] = enc_term(dy, r).astype(BF)
        copy = remote(
            ys.at[dy - 1], yr.at[dy - 1], ysend.at[dy - 1], yrecv.at[dy - 1], dev(x, z, c, mod4(y + dy))
        )
        copy.start()
        y_sent.append(copy)

    first_hop(2)
    w_loc.wait()
    w_sib.wait()
    gs_own.wait()
    g_sib.wait()
    to_group(2)
    first_hop(1)
    to_group(1)
    first_hop(3)
    to_group(3)
    first_hop(0)
    for far in (2, 1, 3, 0):
        for a in range(2):
            dx, dz = (far, 0) if a == 0 else (0, far)
            oa[a, far] = product(a, dx, dz)

    b_sent = []
    for far in (2, 1, 3, 0):
        for a in range(2):
            total = oa[a, far]
            for d in RING:
                arrived(ra.at[a, d - 1, far], arecv.at[a, d - 1, far])
                total = total + ra[a, d - 1, far].astype(F32)
            if far == 0:
                oa[a, 0] = total
            else:
                s2[a, far - 1] = total.astype(BF)
                step_x, step_z = (far, 0) if a == 0 else (0, far)
                copy = remote(
                    s2.at[a, far - 1], r2.at[a, far - 1], bsend.at[a, far - 1], brecv.at[a, far - 1],
                    dev(mod4(x + step_x), mod4(z + step_z), c, y),
                )
                copy.start()
                b_sent.append(copy)

    q_loc.wait()
    for dxh in range(2):
        for dz in range(4):
            if dxh or dz:
                src = ((xh + dxh) % 2) * 4 + mod4(z - dz)
                arrived(qg.at[src], qrecv.at[dxh, dz])
    for i in range(4):
        tile = pl.ds(i * 128, 128)
        even, odd = qg[2 * i].astype(F32), qg[2 * i + 1].astype(F32)
        q_out[0:128, tile] = halves(even, odd, False, True).astype(BF)
        q_out[128:256, tile] = halves(even, odd, True, False).astype(BF)

    for a in range(2):
        total = oa[a, 0]
        for d in RING:
            arrived(r2.at[a, d - 1], brecv.at[a, d - 1])
            total = total + r2[a, d - 1].astype(F32)
        fin[a] = total
    mine = pl.ds(pl.multiple_of(c * 128, 128), 128)
    theirs = pl.ds(pl.multiple_of((1 - c) * 128, 128), 128)
    f_sib = remote(fin.at[:, :, theirs], fsib.at[c], sib_s.at[3], sib_r.at[3], sibling)
    f_sib.start()
    w_out[:, pl.ds(pl.multiple_of(c * 256, 256), 256), :] = fin[:, :, mine]

    for r in range(4):
        part = pl.ds(r * 256, 256)
        total = enc_term(0, r).astype(BF).astype(F32)
        if r == 0:
            for dy in RING:
                arrived(yr.at[dy - 1], yrecv.at[dy - 1])
        for dy in RING:
            total = total + yr[dy - 1, part, :].astype(F32)
        enc_out[part, :] = total.astype(BF)

    f_sib.wait()
    w_out[:, pl.ds(pl.multiple_of((1 - c) * 256, 256), 256), :] = fsib[1 - c]

    for copy in d_sent + q_sent + a_sent + b_sent + y_sent:
        copy.wait_send()

    @pl.when(jnp.logical_not(here))
    def _():
        d_copy(0, 0).wait_send()


VM = pl.BlockSpec(memory_space=pltpu.VMEM)
ANY = pl.BlockSpec(memory_space=pl.ANY)
DMA = pltpu.SemaphoreType.DMA


def params(collective_id=None):
    if collective_id is None:
        return pltpu.CompilerParams(vmem_limit_bytes=60 << 20)
    return pltpu.CompilerParams(
        collective_id=collective_id, has_side_effects=True, vmem_limit_bytes=60 << 20
    )


def body(enc_out, dec_query, ctx_grad, kv_weight, enc_seg, dec_seg):
    enc = enc_out[0]
    eseg = enc_seg.reshape(32, 128)
    dseg = jnp.pad(dec_seg.reshape(2, 128), ((0, 14), (0, 0)))
    shape = jax.ShapeDtypeStruct
    wg, kvx, kvt, xt, xs, dec = pl.pallas_call(
        front,
        out_shape=(
            shape((2, 4, 4, 256, 256), BF),
            shape((4096, 256), BF),
            shape((128, 4096), BF),
            shape((8, 256, 512), BF),
            shape((8, 512, 128), BF),
            shape((8, 8, 256), F32),
        ),
        in_specs=[ANY, VM, VM, ANY, VM, VM],
        out_specs=(ANY, VM, VM, VM, VM, VM),
        scratch_shapes=[
            pltpu.VMEM((2, 256, 4096), BF),
            pltpu.VMEM((2, 4, 4, 256, 256), BF),
            pltpu.VMEM((2, 512, 256), F32),
            pltpu.VMEM((4, 512, 128), BF),
            pltpu.VMEM((8, 512, 128), BF),
            pltpu.VMEM((8, 272, 128), BF),
            pltpu.VMEM((8, 272, 128), BF),
            DMA((5,)), DMA((2,)), DMA((2,)),
            DMA((2, 4, 4)), DMA((2, 4, 4)),
            DMA((2, 4)), DMA((2, 4)),
            DMA((4, 2)), DMA((2, 4)),
        ],
        compiler_params=params(1),
        name="front",
    )(enc, dec_query[0], ctx_grad[0], kv_weight, dseg, eseg)

    dkvp, dqp = pl.pallas_call(
        attend,
        out_shape=(shape((8, 512, 128), BF), shape((8, 128, 128), BF)),
        in_specs=[VM] * 6,
        out_specs=(VM, VM),
        scratch_shapes=[
            pltpu.VMEM((4096, 512), F32),
            pltpu.VMEM((4096, 512), BF),
            pltpu.VMEM((4096, 128), F32),
        ],
        compiler_params=params(),
        name="attend",
    )(kvx, kvt, xt, xs, dec, eseg)

    enc_t, q_grad, w_t = pl.pallas_call(
        back,
        out_shape=(shape((1024, 256), BF), shape((256, 512), BF), shape((2, 512, 128), F32)),
        in_specs=[ANY, ANY, ANY, ANY],
        out_specs=(VM, VM, VM),
        scratch_shapes=[
            pltpu.VMEM((2, 256, 4096), BF),
            pltpu.VMEM((2, 2, 4, 4, 256, 256), BF),
            pltpu.VMEM((4, 2, 512, 128), BF),
            pltpu.VMEM((2, 256, 512), BF),
            pltpu.VMEM((2, 2, 256, 256), BF),
            pltpu.VMEM((8, 128, 128), BF),
            pltpu.VMEM((2, 3, 4, 256, 256), BF),
            pltpu.VMEM((2, 3, 4, 256, 256), BF),
            pltpu.VMEM((2, 3, 256, 256), BF),
            pltpu.VMEM((2, 3, 256, 256), BF),
            pltpu.VMEM((2, 4, 256, 256), F32),
            pltpu.VMEM((3, 1024, 256), BF),
            pltpu.VMEM((3, 1024, 256), BF),
            pltpu.VMEM((2, 256, 256), F32),
            pltpu.VMEM((2, 2, 256, 128), F32),
            DMA((5,)), DMA((4,)), DMA((4,)),
            DMA((2, 4)), DMA((4, 2)),
            DMA((2, 4)), DMA((2, 4)),
            DMA((2, 3, 4)), DMA((2, 3, 4)),
            DMA((2, 3)), DMA((2, 3)),
            DMA((3,)), DMA((3,)),
        ],
        compiler_params=params(2),
        name="back",
    )(dkvp, dqp, enc, wg)
    return enc_t.T[None], q_grad[None], w_t.transpose(0, 2, 1)


def solution(mesh):
    placed = (
        P("dp", "seq", None),
        P("dp", "seq", "mp"),
        P("dp", "seq", "mp"),
        P(None, ("dp", "seq"), "mp"),
        P("dp", None),
        P("dp", "seq"),
    )
    return jax.shard_map(
        body,
        mesh=mesh,
        in_specs=placed,
        out_specs=(P("dp", "seq", "mp"), P("dp", "seq", "mp"), P(None, ("dp", "seq"), "mp")),
        check_vma=False,
    )
```

```python
import functools

import jax
import jax.numpy as jnp
from jax import lax
from jax.experimental import pallas as pl
from jax.experimental.pallas import tpu as pltpu
from jax.sharding import PartitionSpec as P

MESH = pl.DeviceIdType.MESH
BF = jnp.bfloat16
F32 = jnp.float32
NEG = -1e30
KB = 512


def coords():
    dp, seq, y = lax.axis_index("dp"), lax.axis_index("seq"), lax.axis_index("mp")
    xh = seq // 8
    return xh * 2 + dp, xh, (seq // 2) % 4, seq % 2, y


def dev(x, z, core, y):
    return (x % 2, (x // 2) * 8 + z * 2 + core, y)


def row_group(x):
    return (x % 2) * 2 + x // 2


def mod4(v):
    return (v + 4) % 4


def remote(src, dst, send, recv, device):
    return pltpu.make_async_remote_copy(
        src_ref=src, dst_ref=dst, send_sem=send, recv_sem=recv, device_id=device, device_id_type=MESH
    )


def arrived(dst, sem):
    pltpu.make_async_copy(dst, dst, sem).wait()


def greet(peers):
    for peer in peers:
        pl.semaphore_signal(pltpu.get_barrier_semaphore(), inc=1, device_id=peer, device_id_type=MESH)


def greeted(peers):
    pl.semaphore_wait(pltpu.get_barrier_semaphore(), len(peers))


def plane_peers(x, z, c, y):
    peers = [dev(x, z, 1 - c, y), dev(mod4(x + 1), z, c, y), dev(mod4(x + 3), z, c, y)]
    for dx in (0, 2):
        for dz in range(4):
            if dx or dz:
                peers += [dev(mod4(x + dx), mod4(z + dz), core, y) for core in range(2)]
    return peers


def lanes_of(shape):
    return lax.broadcasted_iota(jnp.int32, shape, 1)


def halves(first, second, shift_first, shift_second):
    first = pltpu.roll(first, 64, 1) if shift_first else first
    second = pltpu.roll(second, 64, 1) if shift_second else second
    return jnp.where(lanes_of(first.shape) < 64, first, second)


def front(
    enc, q, do, w, dseg, eseg,
    wg_out, kvx, kvt, xt, xs, dec_out,
    encv, wg, acc, kvs, kvb, qs, qb,
    loc, sib_s, sib_r, ws, wr, qsend, qrecv, ksend, krecv, fsend, frecv,
):
    x, xh, z, c, y = coords()
    me = row_group(x)
    t = xh * 4 + z
    sibling = dev(x, z, 1 - c, y)
    peers = plane_peers(x, z, c, y)
    greet(peers)

    own = pl.multiple_of(c * 256, 256)
    other = pl.multiple_of((1 - c) * 256, 256)
    rows = pl.ds(pl.multiple_of(c * 128, 128), 128)
    w_loc = pltpu.make_async_copy(w.at[:, :, pl.ds(own, 256)], wg.at[:, me, z, rows], loc.at[0])
    w_loc.start()
    e_loc = pltpu.make_async_copy(enc, encv.at[c], loc.at[1])
    e_loc.start()

    ids = dseg[...].astype(F32)
    row = lax.broadcasted_iota(jnp.int32, (16, 128), 0)
    id_rows = jnp.where(row == 0, ids[0:1], jnp.where(row == 1, ids[1:2], 0.0)).astype(BF)
    for h in range(8):
        tile = pl.ds((h // 2) * 128, 128)
        odd = h % 2 == 1
        qs[h, 0:256, :] = halves(q[:, tile].astype(F32), do[:, tile].astype(F32), odd, not odd).astype(BF)
        qs[h, 256:272, :] = id_rows
    q_loc = pltpu.make_async_copy(qs.at[t], qb.at[t], loc.at[2])
    q_loc.start()
    greeted(peers)

    w_sib = remote(w.at[:, :, pl.ds(other, 256)], wg.at[:, me, z, rows], sib_s.at[0], sib_r.at[0], sibling)
    w_sib.start()
    q_sent = []
    for dxh in (1, 0):
        for dz in (2, 1, 3, 0):
            if dxh == 0 and dz == 0:
                continue
            hx, hz = (xh + dxh) % 2, mod4(z + dz)
            copy = remote(
                qs.at[hx * 4 + hz], qb.at[t], qsend.at[dxh, dz], qrecv.at[dxh, dz],
                dev(mod4(x + 2 * dxh), hz, c, y),
            )
            copy.start()
            q_sent.append(copy)
    e_sib = remote(enc, encv.at[c], sib_s.at[1], sib_r.at[1], sibling)
    e_sib.start()
    w_loc.wait()
    w_sib.wait()

    def place(a, first, second):
        bx, bz = (first, second) if a == 0 else (second, first)
        return row_group(mod4(x - bx)), mod4(z - bz)

    def block_of(a, first, second, half=None):
        group, bz = place(a, first, second)
        block = wg.at[a, group, bz]
        return block if half is None else block.at[pl.ds(half * 128, 128)]

    sent = []

    def pass_on(a, first, second, ring, step, half=None):
        block = block_of(a, first, second, half)
        to_first, to_second = (first + step) % 4 if ring == 0 else first, (second + step) % 4 if ring else second
        sem = (a, to_first, to_second, half or 0)
        along_x = (a == 0) == (ring == 0)
        target = dev(mod4(x + step), z, c, y) if along_x else dev(x, mod4(z + step), c, y)
        copy = remote(block, block, ws.at[sem], wr.at[sem], target)
        copy.start()
        sent.append(copy)

    def take(a, first, second):
        if second == 2 or (first == 2 and second == 0):
            for half in range(2):
                arrived(block_of(a, first, second, half), wr.at[a, first, second, half])
        else:
            arrived(block_of(a, first, second), wr.at[a, first, second, 0])

    def multiply(a, first, second, fresh=False):
        group, bz = place(a, first, second)
        columns = pl.ds(pl.multiple_of((group * 4 + bz) * 256, 256), 256)
        for half in range(2):
            term = jnp.dot(encv[half, :, columns], wg[a, group, bz], preferred_element_type=F32)
            if fresh:
                acc[a, pl.ds(half * 256, 256), :] = term
            else:
                acc[a, pl.ds(half * 256, 256), :] += term

    def both_ways(a, first):
        pass_on(a, first, 0, 1, 1)
        pass_on(a, first, 0, 1, -1)

    for step in (1, -1):
        for a in range(2):
            pass_on(a, 0, 0, 0, step)
    for a in range(2):
        both_ways(a, 0)

    def one_hot(i, _):
        seg = eseg[pl.ds(i, 1), :].astype(F32)
        row = lax.broadcasted_iota(jnp.int32, (128, 128), 0).astype(F32)
        hot = jnp.where(row == seg, 1.0, 0.0)
        kvx[pl.ds(pl.multiple_of(i * 128, 128), 128), 128:256] = hot.T.astype(BF)
        return 0

    lax.fori_loop(0, 32, one_hot, 0)

    for a in range(2):
        take(a, 1, 0)
        pass_on(a, 1, 0, 0, 1, 0)
        take(a, 3, 0)
        pass_on(a, 3, 0, 0, -1, 1)
    for a in range(2):
        both_ways(a, 1)
        both_ways(a, 3)
    for a in range(2):
        take(a, 0, 1)
        pass_on(a, 0, 1, 1, 1, 0)
        take(a, 0, 3)
        pass_on(a, 0, 3, 1, -1, 1)
    for a in range(2):
        take(a, 2, 0)
        both_ways(a, 2)
    e_loc.wait()
    e_sib.wait()
    for a in range(2):
        multiply(a, 0, 0, True)
        for first, second in ((1, 0), (3, 0), (0, 1), (0, 3), (2, 0)):
            multiply(a, first, second)

    q_loc.wait()
    for dxh in range(2):
        for dz in range(4):
            if dxh or dz:
                src = ((xh + dxh) % 2) * 4 + mod4(z - dz)
                arrived(qb.at[src], qrecv.at[dxh, dz])

    def prepare(b, _):
        block = qb[b, 0:256, :]
        low = lanes_of((256, 128)) < 64
        zero = jnp.zeros_like(block)
        xs[b, 0:256, :] = jnp.where(low, block, zero)
        xs[b, 256:512, :] = jnp.where(low, zero, block)
        turned = block.T
        xt[b, 0:64, 0:256] = turned[0:64] * jnp.asarray(0.125, BF)
        xt[b, 64:128, 256:512] = turned[64:128]
        xt[b, 0:64, 256:512] = jnp.zeros((64, 256), BF)
        xt[b, 64:128, 0:256] = jnp.zeros((64, 256), BF)
        xt[b, 128:256, :] = jnp.zeros((128, 512), BF)
        ids = qb[b, 256:272, :].astype(F32)
        ids = jnp.concatenate([ids[0:1], ids[1:2]], axis=1)
        row = lax.broadcasted_iota(jnp.int32, (16, 256), 0)
        differs = (row < 4) & (row.astype(F32) != ids)
        xt[b, 128:144, 0:256] = jnp.where(differs, NEG, 0.0).astype(BF)
        dec_out[b] = jnp.broadcast_to(ids, (8, 256))
        return 0

    for first in (1, 3, 2):
        for a in range(2):
            take(a, first, 1)
            pass_on(a, first, 1, 1, 1, 0)
            take(a, first, 3)
            pass_on(a, first, 3, 1, -1, 1)
            multiply(a, first, 1)
            multiply(a, first, 3)
        if first != 2:
            lax.fori_loop(0 if first == 1 else 4, 4 if first == 1 else 8, prepare, 0)
    for first in (0, 1, 3, 2):
        for a in range(2):
            take(a, first, 2)
            multiply(a, first, 2)

    for j in range(4):
        tile = pl.ds((j // 2) * 128, 128)
        odd = j % 2 == 1
        kvs[j] = halves(acc[0, :, tile], acc[1, :, tile], odd, not odd).astype(BF)

    ex = (c + 2 - xh) % 2
    tx = c * 2 + x % 2
    here = c == xh

    def kv_copy(dz, core):
        hz = mod4(z + dz)
        part = pl.ds(core * 256, 256)
        return remote(
            kvs.at[hz, part], kvb.at[t, part], ksend.at[dz, core], krecv.at[ex, dz], dev(tx, hz, core, y)
        )

    def kv_local(core):
        part = pl.ds(core * 256, 256)
        return pltpu.make_async_copy(kvs.at[z, part], kvb.at[t, part], loc.at[4])

    k_sent = [kv_copy(dz, core) for dz in (2, 1, 3) for core in range(2)]
    for copy in k_sent:
        copy.start()
    for core in range(2):
        local = jnp.logical_and(here, c == core)

        @pl.when(local)
        def _():
            kv_local(core).start()

        @pl.when(jnp.logical_not(local))
        def _():
            kv_copy(0, core).start()

    w_save = pltpu.make_async_copy(wg, wg_out, loc.at[3])
    w_save.start()

    mine = pl.ds(pl.multiple_of(c * 256, 256), 256)
    theirs = pl.ds(pl.multiple_of((1 - c) * 256, 256), 256)

    def source(e, dz):
        return ((xh + e) % 2) * 4 + mod4(z - dz)

    f_sent = []

    def hand_over(e, dz):
        src = source(e, dz)
        if e == 0 and dz == 0:

            @pl.when(here)
            def _():
                for core in range(2):

                    @pl.when(c == core)
                    def _():
                        kv_local(core).wait()

            @pl.when(jnp.logical_not(here))
            def _():
                arrived(kvb.at[src, mine], krecv.at[0, 0])
        else:
            arrived(kvb.at[src, mine], krecv.at[e, dz])
        copy = remote(kvb.at[src, mine], kvb.at[src, mine], fsend.at[e, dz], frecv.at[e, dz], sibling)
        copy.start()
        f_sent.append(copy)

    def use(e, dz):
        src = source(e, dz)
        arrived(kvb.at[src, theirs], frecv.at[e, dz])
        block = kvb[src]
        span = pl.ds(pl.multiple_of(src * 512, 512), 512)
        kvx[span, 0:128] = block
        kvt[:, span] = block.T

    order = [(e, dz) for dz in (0, 1, 3, 2) for e in (0, 1)]
    for i, at in enumerate(order):
        hand_over(*at)
        if i:
            use(*order[i - 1])
    use(*order[-1])

    for copy in sent + q_sent + k_sent + f_sent:
        copy.wait_send()
    for core in range(2):

        @pl.when(jnp.logical_not(jnp.logical_and(here, c == core)))
        def _():
            kv_copy(0, core).wait_send()

    w_save.wait()


def attend(kvx, kvt, xt, xs, dec, eseg, dkv_out, dq_out, tt, yy, dkv):
    dkv[...] = jnp.zeros_like(dkv)
    seg = eseg[...].astype(F32)

    def one_block(b, _):
        ids = dec[b]
        low, high = jnp.min(ids), jnp.max(ids)
        begin = jnp.sum(jnp.where(seg < low, 1.0, 0.0)).astype(jnp.int32)
        end = jnp.sum(jnp.where(seg <= high, 1.0, 0.0)).astype(jnp.int32)
        j0, j1 = begin // KB, (end + KB - 1) // KB

        def at(j):
            return pl.ds(pl.multiple_of(j * KB, KB), KB)

        def fold(op, v):
            return op(v.reshape(KB // 8, 8, 256), axis=0)

        def scores(j, top):
            both = jnp.dot(kvx[at(j), :], xt[b], preferred_element_type=F32)
            tt[at(j), :] = both
            return jnp.maximum(top, fold(jnp.max, both[:, 0:256]))

        top = lax.fori_loop(j0, j1, scores, jnp.full((8, 256), -3e38, F32))
        top = jnp.max(top, axis=0, keepdims=True)

        def weigh(j, total):
            e = jnp.exp(tt[at(j), 0:256] - top)
            tt[at(j), 0:256] = e
            return total + fold(jnp.sum, e)

        total = lax.fori_loop(j0, j1, weigh, jnp.zeros((8, 256), F32))
        inv = 1.0 / jnp.sum(total, axis=0, keepdims=True)

        def deltas(j, delta):
            low_p = (tt[at(j), 0:256] * inv).astype(BF)
            yy[at(j), 256:512] = low_p
            return delta + fold(jnp.sum, low_p.astype(F32) * tt[at(j), 256:512])

        delta = lax.fori_loop(j0, j1, deltas, jnp.zeros((8, 256), F32))
        delta = jnp.sum(delta, axis=0, keepdims=True)
        inv8 = inv * 0.125

        def grads(j, dq):
            ds = ((tt[at(j), 0:256] * inv8) * (tt[at(j), 256:512] - delta)).astype(BF)
            yy[at(j), 0:256] = ds
            dkv[at(j), :] += jnp.dot(yy[at(j), :], xs[b], preferred_element_type=F32)
            return dq + jnp.dot(kvt[0:64, at(j)], ds, preferred_element_type=F32)

        dq = lax.fori_loop(j0, j1, grads, jnp.zeros((64, 256), F32))
        dq_out[b] = jnp.concatenate([dq[:, 0:128], dq[:, 128:256]], axis=0).T.astype(BF)
        return 0

    lax.fori_loop(0, 8, one_block, 0)
    dkv_out[...] = dkv[...].astype(BF).reshape(dkv_out.shape)


def back(
    dkvp, dqp, enc, w,
    enc_out, q_out, w_out,
    encv, wv, po, pb, ps, rb, gt, gs, qg, cs, cr, ms, mr, keep, fin, fsib, ycs, ycr, yms, ymr,
    loc, sib_s, sib_r, dsend, drecv, qsend, qrecv, csend, crecv, msend, mrecv, ysend, yrecv,
):
    x, xh, z, c, y = coords()
    sibling = dev(x, z, 1 - c, y)
    peers = plane_peers(x, z, c, y) + [dev(x, z, c, mod4(y + 1)), dev(x, z, c, mod4(y + 3))]
    greet(peers)
    p_loc = pltpu.make_async_copy(dkvp.at[pl.ds(c * 4, 4)], po, loc.at[0])
    p_loc.start()
    e_loc = pltpu.make_async_copy(enc, encv.at[c], loc.at[1])
    e_loc.start()
    w_loc = pltpu.make_async_copy(w, wv.at[c], loc.at[2])
    w_loc.start()
    q_loc = pltpu.make_async_copy(dqp.at[xh * 4 + z], qg.at[xh * 4 + z], loc.at[3])
    q_loc.start()
    greeted(peers)

    here = c == xh
    p_sib = remote(dkvp.at[pl.ds((1 - c) * 4, 4)], pb, sib_s.at[0], sib_r.at[0], sibling)
    p_sib.start()
    e_sib = remote(enc, encv.at[c], sib_s.at[1], sib_r.at[1], sibling)
    e_sib.start()
    w_sib = remote(w, wv.at[c], sib_s.at[2], sib_r.at[2], sibling)
    w_sib.start()

    def d_copy(dz):
        tz = mod4(z + dz)
        return remote(ps.at[tz], rb.at[z], dsend.at[dz], drecv.at[dz], dev(c * 2 + x % 2, tz, xh, y))

    p_loc.wait()
    p_sib.wait()
    for dz in (2, 1, 3, 0):
        tz = mod4(z + dz)
        ps[tz] = (po[tz].astype(F32) + pb[tz].astype(F32)).astype(BF)
        if dz:
            d_copy(dz).start()
    d_loc = pltpu.make_async_copy(ps.at[z], rb.at[z], loc.at[4])

    @pl.when(here)
    def _():
        d_loc.start()

    @pl.when(jnp.logical_not(here))
    def _():
        d_copy(0).start()

    q_sent = []
    for dxh in (1, 0):
        for dz in (2, 1, 3, 0):
            if dxh or dz:
                tx, tz = (xh + dxh) % 2, mod4(z + dz)
                copy = remote(
                    dqp.at[tx * 4 + tz], qg.at[xh * 4 + z], qsend.at[dxh, dz], qrecv.at[dxh, dz],
                    dev(tx * 2 + x % 2, tz, c, y),
                )
                copy.start()
                q_sent.append(copy)

    for dz in (0, 1, 3, 2):
        j = mod4(z - dz)
        if dz == 0:

            @pl.when(here)
            def _():
                d_loc.wait()

            @pl.when(jnp.logical_not(here))
            def _():
                arrived(rb.at[j], drecv.at[0])
        else:
            arrived(rb.at[j], drecv.at[dz])
        turned = rb[j].T
        keys = pl.ds(pl.multiple_of(j * 64, 64), 64)
        gt[0, keys, :] = turned[0:64]
        gt[1, keys, :] = turned[64:128]

    own_tok = pl.ds(pl.multiple_of(c * 256, 256), 256)
    sib_tok = pl.ds(pl.multiple_of((1 - c) * 256, 256), 256)
    g_sib = remote(gt.at[:, :, sib_tok], gs.at[c], sib_s.at[3], sib_r.at[3], sibling)
    g_sib.start()
    gs_own = pltpu.make_async_copy(gt.at[:, :, own_tok], gs.at[c], loc.at[5])
    gs_own.start()
    e_loc.wait()
    e_sib.wait()

    def product(a, first, second):
        bx, bz = (second, first) if a == 0 else (first, second)
        columns = pl.ds(pl.multiple_of((row_group(mod4(x + bx)) * 4 + mod4(z + bz)) * 256, 256), 256)
        return jnp.dot(gt[a, :, 0:256], encv[0, :, columns], preferred_element_type=F32) + jnp.dot(
            gt[a, :, 256:512], encv[1, :, columns], preferred_element_type=F32
        )

    sent = []

    def neighbour(a, ring, step):
        along_x = (a == 1) == (ring == 0)
        return dev(mod4(x + step), z, c, y) if along_x else dev(x, mod4(z + step), c, y)

    def send_far(a, slot, ring, value):
        for half in range(2):
            cs[a, slot, half] = value[half * 128 : half * 128 + 128].astype(BF)
            at = (a, slot, half)
            copy = remote(cs.at[at], cr.at[at], csend.at[at], crecv.at[at], neighbour(a, ring, 1 - 2 * half))
            copy.start()
            sent.append(copy)

    def send_near(a, slot, ring, values):
        for half in range(2):
            value = values[half]()
            at = (a, slot, half)
            arrived(cr.at[at], crecv.at[at])
            keep_half = pl.ds(half * 128, 128)
            rest = slice(128, 256) if half == 0 else slice(0, 128)
            this = slice(0, 128) if half == 0 else slice(128, 256)
            ms[a, slot, half, pl.ds((1 - half) * 128, 128), :] = value[rest].astype(BF)
            ms[a, slot, half, keep_half, :] = (value[this] + cr[a, slot, half].astype(F32)).astype(BF)
            copy = remote(ms.at[at], mr.at[at], msend.at[at], mrecv.at[at], neighbour(a, ring, 1 - 2 * half))
            copy.start()
            sent.append(copy)

    def collect(a, slot, value):
        for half in range(2):
            at = (a, slot, half)
            arrived(mr.at[at], mrecv.at[at])
            value = value + mr[a, slot, half].astype(F32)
        return value

    def far(slot):
        for a in range(2):
            send_far(a, slot, 0, product(a, 2, slot))

    def near(slot):
        for a in range(2):
            send_near(a, slot, 0, [lambda a=a: product(a, 1, slot), lambda a=a: product(a, 3, slot)])

    def ahead(slot):
        for a in range(2):
            keep[a, slot] = product(a, 0, slot)

    def enc_rows(dy, r):
        group = mod4(y + dy)
        total = None
        for half in range(2):
            for a in range(2):
                term = jnp.dot(wv[half, a, group, r], gs[half, a], preferred_element_type=F32)
                total = term if total is None else total + term
        return total

    def y_send(src, dst, i, step):
        copy = remote(src, dst, ysend.at[i], yrecv.at[i], dev(x, z, c, mod4(y + step)))
        copy.start()
        sent.append(copy)

    def y_far():
        for half in range(2):
            for r in range(2):
                ycs[half, r] = enc_rows(2, 2 * half + r).astype(BF)
            y_send(ycs.at[half], ycr.at[half], half, 1 - 2 * half)

    def y_free():
        for half in range(2):
            for r in range(2):
                yms[half, 1 - half, r] = enc_rows(1 + 2 * half, 2 * (1 - half) + r).astype(BF)
            y_send(yms.at[half, 1 - half], ymr.at[half, 1 - half], 2 + half, 1 - 2 * half)

    def y_near():
        for half in range(2):
            for r in range(2):
                value = enc_rows(1 + 2 * half, 2 * half + r)
                if r == 0:
                    arrived(ycr.at[half], yrecv.at[half])
                yms[half, half, r] = (value + ycr[half, r].astype(F32)).astype(BF)
            y_send(yms.at[half, half], ymr.at[half, half], 4 + half, 1 - 2 * half)

    far(2)
    gs_own.wait()
    g_sib.wait()
    w_loc.wait()
    w_sib.wait()
    y_far()
    far(1)
    near(2)
    y_free()
    far(3)
    near(1)
    ahead(2)
    far(0)
    near(3)
    y_near()
    for a in range(2):
        send_far(a, 4, 1, collect(a, 2, keep[a, 2]))
    near(0)
    ahead(1)
    ahead(3)
    ahead(0)

    q_loc.wait()
    for dxh in range(2):
        for dz in range(4):
            if dxh or dz:
                src = ((xh + dxh) % 2) * 4 + mod4(z - dz)
                arrived(qg.at[src], qrecv.at[dxh, dz])
    q_out[...] = qg[...]

    for a in range(2):
        for slot in (1, 3):
            keep[a, slot] = collect(a, slot, keep[a, slot])
    for a in range(2):
        send_near(a, 4, 1, [lambda a=a: keep[a, 1], lambda a=a: keep[a, 3]])

    for r in range(4):
        total = enc_rows(0, r).astype(BF).astype(F32)
        for half in range(2):
            if r == 0:
                arrived(ymr.at[half, 1 - half], yrecv.at[2 + half])
                arrived(ymr.at[half, half], yrecv.at[4 + half])
            total = total + ymr[half, r // 2, r % 2].astype(F32)
        enc_out[pl.ds(r * 256, 256), :] = total.astype(BF)

    for a in range(2):
        fin[a] = collect(a, 4, collect(a, 0, keep[a, 0]))
    mine = pl.ds(pl.multiple_of(c * 128, 128), 128)
    theirs = pl.ds(pl.multiple_of((1 - c) * 128, 128), 128)
    f_sib = remote(fin.at[:, :, theirs], fsib, sib_s.at[4], sib_r.at[4], sibling)
    f_sib.start()
    w_out[:, pl.ds(pl.multiple_of(c * 256, 256), 256), :] = fin[:, :, mine]
    for copy in q_sent + sent + [d_copy(dz) for dz in (1, 2, 3)]:
        copy.wait_send()

    @pl.when(jnp.logical_not(here))
    def _():
        d_copy(0).wait_send()

    f_sib.wait()
    w_out[:, pl.ds(pl.multiple_of((1 - c) * 256, 256), 256), :] = fsib[...]


def finish(enc_t, qg, w_t, enc_out, q_out, w_out):
    enc_out[...] = enc_t[...].T
    for i in range(4):
        tile = pl.ds(i * 128, 128)
        even, odd = qg[2 * i].astype(F32), qg[2 * i + 1].astype(F32)
        q_out[0:128, tile] = halves(even, odd, False, True).astype(BF)
        q_out[128:256, tile] = halves(even, odd, True, False).astype(BF)
    for a in range(2):
        w_out[a] = w_t[a].T


VM = pl.BlockSpec(memory_space=pltpu.VMEM)
ANY = pl.BlockSpec(memory_space=pl.ANY)
DMA = pltpu.SemaphoreType.DMA


def params(collective_id=None):
    if collective_id is None:
        return pltpu.CompilerParams(vmem_limit_bytes=60 << 20)
    return pltpu.CompilerParams(
        collective_id=collective_id, has_side_effects=True, vmem_limit_bytes=60 << 20
    )


def body(enc_out, dec_query, ctx_grad, kv_weight, enc_seg, dec_seg):
    enc = enc_out[0]
    eseg = enc_seg.reshape(32, 128)
    dseg = dec_seg.reshape(2, 128)
    shape = jax.ShapeDtypeStruct
    wg, kvx, kvt, xt, xs, dec = pl.pallas_call(
        front,
        out_shape=(
            shape((2, 4, 4, 256, 256), BF),
            shape((4096, 256), BF),
            shape((128, 4096), BF),
            shape((8, 256, 512), BF),
            shape((8, 512, 128), BF),
            shape((8, 8, 256), F32),
        ),
        in_specs=[ANY, VM, VM, ANY, VM, VM],
        out_specs=(ANY, VM, VM, VM, VM, VM),
        scratch_shapes=[
            pltpu.VMEM((2, 256, 4096), BF),
            pltpu.VMEM((2, 4, 4, 256, 256), BF),
            pltpu.VMEM((2, 512, 256), F32),
            pltpu.VMEM((4, 512, 128), BF),
            pltpu.VMEM((8, 512, 128), BF),
            pltpu.VMEM((8, 272, 128), BF),
            pltpu.VMEM((8, 272, 128), BF),
            DMA((5,)), DMA((2,)), DMA((2,)),
            DMA((2, 4, 4, 2)), DMA((2, 4, 4, 2)),
            DMA((2, 4)), DMA((2, 4)),
            DMA((4, 2)), DMA((2, 4)),
            DMA((2, 4)), DMA((2, 4)),
        ],
        compiler_params=params(1),
        name="front",
    )(enc, dec_query[0], ctx_grad[0], kv_weight, dseg, eseg)

    dkvp, dqp = pl.pallas_call(
        attend,
        out_shape=(shape((8, 512, 128), BF), shape((8, 128, 128), BF)),
        in_specs=[VM] * 6,
        out_specs=(VM, VM),
        scratch_shapes=[
            pltpu.VMEM((4096, 512), F32),
            pltpu.VMEM((4096, 512), BF),
            pltpu.VMEM((4096, 128), F32),
        ],
        compiler_params=params(),
        name="attend",
    )(kvx, kvt, xt, xs, dec, eseg)

    enc_t, qg, w_t = pl.pallas_call(
        back,
        out_shape=(shape((1024, 256), BF), shape((8, 128, 128), BF), shape((2, 512, 128), F32)),
        in_specs=[ANY, ANY, ANY, ANY],
        out_specs=(VM, VM, VM),
        scratch_shapes=[
            pltpu.VMEM((2, 256, 4096), BF),
            pltpu.VMEM((2, 2, 4, 4, 256, 256), BF),
            pltpu.VMEM((4, 512, 128), BF),
            pltpu.VMEM((4, 512, 128), BF),
            pltpu.VMEM((4, 512, 128), BF),
            pltpu.VMEM((4, 512, 128), BF),
            pltpu.VMEM((2, 256, 512), BF),
            pltpu.VMEM((2, 2, 256, 256), BF),
            pltpu.VMEM((8, 128, 128), BF),
            pltpu.VMEM((2, 5, 2, 128, 256), BF),
            pltpu.VMEM((2, 5, 2, 128, 256), BF),
            pltpu.VMEM((2, 5, 2, 256, 256), BF),
            pltpu.VMEM((2, 5, 2, 256, 256), BF),
            pltpu.VMEM((2, 4, 256, 256), F32),
            pltpu.VMEM((2, 256, 256), F32),
            pltpu.VMEM((2, 256, 128), F32),
            pltpu.VMEM((2, 2, 256, 256), BF),
            pltpu.VMEM((2, 2, 256, 256), BF),
            pltpu.VMEM((2, 2, 2, 256, 256), BF),
            pltpu.VMEM((2, 2, 2, 256, 256), BF),
            DMA((6,)), DMA((5,)), DMA((5,)),
            DMA((4,)), DMA((4,)),
            DMA((2, 4)), DMA((2, 4)),
            DMA((2, 5, 2)), DMA((2, 5, 2)),
            DMA((2, 5, 2)), DMA((2, 5, 2)),
            DMA((6,)), DMA((6,)),
        ],
        compiler_params=params(2),
        name="back",
    )(dkvp, dqp, enc, wg)

    enc_grad, q_grad, w_grad = pl.pallas_call(
        finish,
        out_shape=(shape((256, 1024), BF), shape((256, 512), BF), shape((2, 128, 512), F32)),
        in_specs=[VM] * 3,
        out_specs=(VM, VM, VM),
        compiler_params=params(),
        name="finish",
    )(enc_t, qg, w_t)
    return enc_grad[None], q_grad[None], w_grad


def solution(mesh):
    placed = (
        P("dp", "seq", None),
        P("dp", "seq", "mp"),
        P("dp", "seq", "mp"),
        P(None, ("dp", "seq"), "mp"),
        P("dp", None),
        P("dp", "seq"),
    )
    return jax.shard_map(
        body,
        mesh=mesh,
        in_specs=placed,
        out_specs=(P("dp", "seq", "mp"), P("dp", "seq", "mp"), P(None, ("dp", "seq"), "mp")),
        check_vma=False,
    )
```

```python
import functools

import jax
import jax.numpy as jnp
from jax import lax
from jax.experimental import pallas as pl
from jax.experimental.pallas import tpu as pltpu
from jax.sharding import PartitionSpec as P

MESH = pl.DeviceIdType.MESH
BF = jnp.bfloat16
F32 = jnp.float32
NEG = -1e30
KB = 256


def coords():
    dp, seq, y = lax.axis_index("dp"), lax.axis_index("seq"), lax.axis_index("mp")
    xh = seq // 8
    return xh * 2 + dp, xh, (seq // 2) % 4, seq % 2, y


def dev(x, z, core, y):
    return (x % 2, (x // 2) * 8 + z * 2 + core, y)


def row_group(x):
    return (x % 2) * 2 + x // 2


def mod4(v):
    return (v + 4) % 4


def remote(src, dst, send, recv, device):
    return pltpu.make_async_remote_copy(
        src_ref=src, dst_ref=dst, send_sem=send, recv_sem=recv, device_id=device, device_id_type=MESH
    )


def arrived(dst, sem):
    pltpu.make_async_copy(dst, dst, sem).wait()


def greet(peers):
    for peer in peers:
        pl.semaphore_signal(pltpu.get_barrier_semaphore(), inc=1, device_id=peer, device_id_type=MESH)


def greeted(peers):
    pl.semaphore_wait(pltpu.get_barrier_semaphore(), len(peers))


def plane_peers(x, z, c, y):
    peers = [dev(x, z, 1 - c, y), dev(mod4(x + 1), z, c, y), dev(mod4(x + 3), z, c, y)]
    for dx in (0, 2):
        for dz in range(4):
            if dx or dz:
                peers += [dev(mod4(x + dx), mod4(z + dz), core, y) for core in range(2)]
    return peers


def lanes_of(shape):
    return lax.broadcasted_iota(jnp.int32, shape, 1)


def halves(first, second, shift_first, shift_second):
    first = pltpu.roll(first, 64, 1) if shift_first else first
    second = pltpu.roll(second, 64, 1) if shift_second else second
    return jnp.where(lanes_of(first.shape) < 64, first, second)


def front(
    enc, q, do, w, dseg, eseg,
    wg_out, kvx_out, kvt_out, xt_out, xs_out, spans,
    encv, wg, acc, kvs, kvb, qs, qb, kvx, kvt, xt, xs,
    loc, save, sib_s, sib_r, ws, wr, qsend, qrecv, ksend, krecv, fsend, frecv,
):
    x, xh, z, c, y = coords()
    me = row_group(x)
    t = xh * 4 + z
    sibling = dev(x, z, 1 - c, y)
    peers = plane_peers(x, z, c, y)
    greet(peers)

    own = pl.multiple_of(c * 256, 256)
    other = pl.multiple_of((1 - c) * 256, 256)
    rows = pl.ds(pl.multiple_of(c * 128, 128), 128)
    w_loc = pltpu.make_async_copy(w.at[:, :, pl.ds(own, 256)], wg.at[:, me, z, rows], loc.at[0])
    w_loc.start()
    e_loc = pltpu.make_async_copy(enc, encv.at[c], loc.at[1])
    e_loc.start()

    ids = dseg[...].astype(F32)
    row = lax.broadcasted_iota(jnp.int32, (16, 128), 0)
    id_rows = jnp.where(row == 0, ids[0:1], jnp.where(row == 1, ids[1:2], 0.0)).astype(BF)
    for h in range(8):
        tile = pl.ds((h // 2) * 128, 128)
        odd = h % 2 == 1
        qs[h, 0:256, :] = halves(q[:, tile].astype(F32), do[:, tile].astype(F32), odd, not odd).astype(BF)
        qs[h, 256:272, :] = id_rows
    q_loc = pltpu.make_async_copy(qs.at[t], qb.at[t], loc.at[2])
    q_loc.start()
    greeted(peers)

    w_sib = remote(w.at[:, :, pl.ds(other, 256)], wg.at[:, me, z, rows], sib_s.at[0], sib_r.at[0], sibling)
    w_sib.start()
    q_sent = []
    for dxh in (1, 0):
        for dz in (2, 1, 3, 0):
            if dxh == 0 and dz == 0:
                continue
            hx, hz = (xh + dxh) % 2, mod4(z + dz)
            copy = remote(
                qs.at[hx * 4 + hz], qb.at[t], qsend.at[dxh, dz], qrecv.at[dxh, dz],
                dev(mod4(x + 2 * dxh), hz, c, y),
            )
            copy.start()
            q_sent.append(copy)
    e_sib = remote(enc, encv.at[c], sib_s.at[1], sib_r.at[1], sibling)
    e_sib.start()
    w_loc.wait()
    w_sib.wait()

    def place(a, first, second):
        bx, bz = (first, second) if a == 0 else (second, first)
        return row_group(mod4(x - bx)), mod4(z - bz)

    def block_of(a, first, second, half=None):
        group, bz = place(a, first, second)
        block = wg.at[a, group, bz]
        return block if half is None else block.at[pl.ds(half * 128, 128)]

    sent = []

    def pass_on(a, first, second, ring, step, half=None):
        block = block_of(a, first, second, half)
        to_first, to_second = (first + step) % 4 if ring == 0 else first, (second + step) % 4 if ring else second
        sem = (a, to_first, to_second, half or 0)
        along_x = (a == 0) == (ring == 0)
        target = dev(mod4(x + step), z, c, y) if along_x else dev(x, mod4(z + step), c, y)
        copy = remote(block, block, ws.at[sem], wr.at[sem], target)
        copy.start()
        sent.append(copy)

    def take(a, first, second):
        if second == 2 or (first == 2 and second == 0):
            for half in range(2):
                arrived(block_of(a, first, second, half), wr.at[a, first, second, half])
        else:
            arrived(block_of(a, first, second), wr.at[a, first, second, 0])

    def multiply(a, first, second, fresh=False):
        group, bz = place(a, first, second)
        columns = pl.ds(pl.multiple_of((group * 4 + bz) * 256, 256), 256)
        for half in range(2):
            term = jnp.dot(encv[half, :, columns], wg[a, group, bz], preferred_element_type=F32)
            if fresh:
                acc[a, pl.ds(half * 256, 256), :] = term
            else:
                acc[a, pl.ds(half * 256, 256), :] += term

    def both_ways(a, first):
        pass_on(a, first, 0, 1, 1)
        pass_on(a, first, 0, 1, -1)

    for step in (1, -1):
        for a in range(2):
            pass_on(a, 0, 0, 0, step)
    for a in range(2):
        both_ways(a, 0)

    def one_hot(i, _):
        seg = eseg[pl.ds(i, 1), :].astype(F32)
        row = lax.broadcasted_iota(jnp.int32, (128, 128), 0).astype(F32)
        hot = jnp.where(row == seg, 1.0, 0.0)
        kvx[pl.ds(pl.multiple_of(i * 128, 128), 128), 128:256] = hot.T.astype(BF)
        return 0

    lax.fori_loop(0, 32, one_hot, 0)

    for a in range(2):
        take(a, 1, 0)
        pass_on(a, 1, 0, 0, 1, 0)
        take(a, 3, 0)
        pass_on(a, 3, 0, 0, -1, 1)
    for a in range(2):
        both_ways(a, 1)
        both_ways(a, 3)
    for a in range(2):
        take(a, 0, 1)
        pass_on(a, 0, 1, 1, 1, 0)
        take(a, 0, 3)
        pass_on(a, 0, 3, 1, -1, 1)
    for a in range(2):
        take(a, 2, 0)
        both_ways(a, 2)
    e_loc.wait()
    e_sib.wait()
    for a in range(2):
        multiply(a, 0, 0, True)
        for first, second in ((1, 0), (3, 0), (0, 1), (0, 3), (2, 0)):
            multiply(a, first, second)

    q_loc.wait()
    for dxh in range(2):
        for dz in range(4):
            if dxh or dz:
                src = ((xh + dxh) % 2) * 4 + mod4(z - dz)
                arrived(qb.at[src], qrecv.at[dxh, dz])

    def prepare(b, _):
        block = qb[b, 0:256, :]
        low = lanes_of((256, 128)) < 64
        zero = jnp.zeros_like(block)
        xs[b, 0:256, :] = jnp.where(low, block, zero)
        xs[b, 256:512, :] = jnp.where(low, zero, block)
        turned = block.T
        xt[b, 0:64, 0:256] = turned[0:64] * jnp.asarray(0.125, BF)
        xt[b, 64:128, 256:512] = turned[64:128]
        xt[b, 0:64, 256:512] = jnp.zeros((64, 256), BF)
        xt[b, 64:128, 0:256] = jnp.zeros((64, 256), BF)
        xt[b, 128:256, :] = jnp.zeros((128, 512), BF)
        ids = qb[b, 256:272, :].astype(F32)
        ids = jnp.concatenate([ids[0:1], ids[1:2]], axis=1)
        row = lax.broadcasted_iota(jnp.int32, (16, 256), 0)
        differs = (row < 4) & (row.astype(F32) != ids)
        xt[b, 128:144, 0:256] = jnp.where(differs, NEG, 0.0).astype(BF)
        seg = eseg[...].astype(F32)
        low_id, high_id = jnp.min(ids, axis=1, keepdims=True), jnp.max(ids, axis=1, keepdims=True)
        begin = jnp.sum(jnp.where(seg < low_id, 1.0, 0.0), axis=(0, 1), keepdims=True)
        end = jnp.sum(jnp.where(seg <= high_id, 1.0, 0.0), axis=(0, 1), keepdims=True)
        begin = jnp.floor(begin * (1.0 / 128)) * 128.0
        count = jnp.floor((end - begin + (KB - 1)) * (1.0 / KB))
        begin = jnp.minimum(begin, 4096.0 - count * KB)
        spans[pl.ds(b, 1), :] = jnp.where(lanes_of((1, 128)) == 0, begin, count).astype(jnp.int32)
        return 0

    for first in (1, 3, 2):
        for a in range(2):
            take(a, first, 1)
            pass_on(a, first, 1, 1, 1, 0)
            take(a, first, 3)
            pass_on(a, first, 3, 1, -1, 1)
            multiply(a, first, 1)
            multiply(a, first, 3)
        if first != 2:
            lax.fori_loop(0 if first == 1 else 4, 4 if first == 1 else 8, prepare, 0)
    saved = [
        pltpu.make_async_copy(xt, xt_out, save.at[8]),
        pltpu.make_async_copy(xs, xs_out, save.at[9]),
    ]
    for copy in saved:
        copy.start()
    for first in (0, 1, 3, 2):
        for a in range(2):
            take(a, first, 2)
            multiply(a, first, 2)

    for j in range(4):
        tile = pl.ds((j // 2) * 128, 128)
        odd = j % 2 == 1
        kvs[j] = halves(acc[0, :, tile], acc[1, :, tile], odd, not odd).astype(BF)

    ex = (c + 2 - xh) % 2
    tx = c * 2 + x % 2
    here = c == xh

    def kv_copy(dz, core):
        hz = mod4(z + dz)
        part = pl.ds(core * 256, 256)
        return remote(
            kvs.at[hz, part], kvb.at[t, part], ksend.at[dz, core], krecv.at[ex, dz], dev(tx, hz, core, y)
        )

    def kv_local(core):
        part = pl.ds(core * 256, 256)
        return pltpu.make_async_copy(kvs.at[z, part], kvb.at[t, part], loc.at[4])

    k_sent = [kv_copy(dz, core) for dz in (2, 1, 3) for core in range(2)]
    for copy in k_sent:
        copy.start()
    for core in range(2):
        local = jnp.logical_and(here, c == core)

        @pl.when(local)
        def _():
            kv_local(core).start()

        @pl.when(jnp.logical_not(local))
        def _():
            kv_copy(0, core).start()

    w_save = pltpu.make_async_copy(wg, wg_out, loc.at[3])
    w_save.start()

    mine = pl.ds(pl.multiple_of(c * 256, 256), 256)
    theirs = pl.ds(pl.multiple_of((1 - c) * 256, 256), 256)

    def source(e, dz):
        return ((xh + e) % 2) * 4 + mod4(z - dz)

    f_sent = []

    def hand_over(e, dz):
        src = source(e, dz)
        if e == 0 and dz == 0:

            @pl.when(here)
            def _():
                for core in range(2):

                    @pl.when(c == core)
                    def _():
                        kv_local(core).wait()

            @pl.when(jnp.logical_not(here))
            def _():
                arrived(kvb.at[src, mine], krecv.at[0, 0])
        else:
            arrived(kvb.at[src, mine], krecv.at[e, dz])
        copy = remote(kvb.at[src, mine], kvb.at[src, mine], fsend.at[e, dz], frecv.at[e, dz], sibling)
        copy.start()
        f_sent.append(copy)

    def use(e, dz):
        src = source(e, dz)
        arrived(kvb.at[src, theirs], frecv.at[e, dz])
        block = kvb[src]
        span = pl.ds(pl.multiple_of(src * 512, 512), 512)
        kvx[span, 0:128] = block
        kvt[:, span] = block.T
        for copy in (
            pltpu.make_async_copy(kvx.at[span], kvx_out.at[span], save.at[e * 4 + dz]),
            pltpu.make_async_copy(kvt.at[:, span], kvt_out.at[:, span], save.at[10 + e * 4 + dz]),
        ):
            copy.start()
            saved.append(copy)

    order = [(e, dz) for dz in (0, 1, 3, 2) for e in (0, 1)]
    for i, at in enumerate(order):
        hand_over(*at)
        if i:
            use(*order[i - 1])
    use(*order[-1])

    for copy in sent + q_sent + k_sent + f_sent:
        copy.wait_send()
    for core in range(2):

        @pl.when(jnp.logical_not(jnp.logical_and(here, c == core)))
        def _():
            kv_copy(0, core).wait_send()

    w_save.wait()
    for copy in saved:
        copy.wait()


def attend(
    spans, kvx_in, kvt_in, xt_in, xs_in, dkv_out, dq_out, kvx, kvt, xt, xs, tt, yy, dkv, sem, xt_sem, xs_sem
):
    kvx_copy = pltpu.make_async_copy(kvx_in, kvx, sem.at[0])
    kvt_copy = pltpu.make_async_copy(kvt_in, kvt, sem.at[1])

    def xt_copy(b):
        return pltpu.make_async_copy(xt_in.at[b], xt.at[b], xt_sem.at[b])

    def xs_copy(b):
        return pltpu.make_async_copy(xs_in.at[b], xs.at[b], xs_sem.at[b])

    xt_copy(0).start()
    kvx_copy.start()
    xs_copy(0).start()
    kvt_copy.start()
    for b in range(1, 8):
        xt_copy(b).start()
        xs_copy(b).start()
    dkv[...] = jnp.zeros_like(dkv)
    kvx_copy.wait()

    def one_block(b, _):
        begin, count = spans[b, 0], spans[b, 1]
        xt_copy(b).wait()

        def sweep(step, carry):
            done = 0
            for blocks in (3, 2, 1):
                times = (count - done) // blocks

                def piece(i, value, done=done, blocks=blocks):
                    first = pl.multiple_of(begin + (done + i * blocks) * KB, 128)
                    return step(pl.ds(first, blocks * KB), value)

                carry = lax.fori_loop(0, times, piece, carry)
                done = done + times * blocks
            return carry

        def fold(op, v):
            return op(v.reshape(v.shape[0] // 8, 8, 256), axis=0)

        def scores(rows, top):
            both = jnp.dot(kvx[rows, :], xt[b], preferred_element_type=F32)
            tt[rows, :] = both
            return jnp.maximum(top, fold(jnp.max, both[:, 0:256]))

        top = sweep(scores, jnp.full((8, 256), -3e38, F32))
        top = jnp.max(top, axis=0, keepdims=True)

        def weigh(rows, total):
            e = jnp.exp(tt[rows, 0:256] - top)
            tt[rows, 0:256] = e
            return total + fold(jnp.sum, e)

        total = sweep(weigh, jnp.zeros((8, 256), F32))
        inv = 1.0 / jnp.sum(total, axis=0, keepdims=True)

        def deltas(rows, delta):
            low_p = (tt[rows, 0:256] * inv).astype(BF)
            yy[rows, 256:512] = low_p
            return delta + fold(jnp.sum, low_p.astype(F32) * tt[rows, 256:512])

        delta = sweep(deltas, jnp.zeros((8, 256), F32))
        delta = jnp.sum(delta, axis=0, keepdims=True)
        inv8 = inv * 0.125
        xs_copy(b).wait()

        @pl.when(b == 0)
        def _():
            kvt_copy.wait()

        def grads(rows, dq):
            yy[rows, 0:256] = ((tt[rows, 0:256] * inv8) * (tt[rows, 256:512] - delta)).astype(BF)
            dkv[rows, :] += jnp.dot(yy[rows, :], xs[b], preferred_element_type=F32)
            return dq + jnp.dot(kvt[0:64, rows], yy[rows, 0:256], preferred_element_type=F32)

        dq = sweep(grads, jnp.zeros((64, 256), F32))
        dq_out[b] = jnp.concatenate([dq[:, 0:128], dq[:, 128:256]], axis=0).T.astype(BF)
        return 0

    lax.fori_loop(0, 8, one_block, 0)
    dkv_out[...] = dkv[...].astype(BF).reshape(dkv_out.shape)


def back(
    dkvp, dqp, enc, w,
    enc_out, q_out, w_out,
    encv, wv, po, pb, ps, rb, gt, gs, qg, cs, cr, ms, mr, keep, fin, fsib, ycs, ycr, yms, ymr,
    loc, sib_s, sib_r, dsend, drecv, qsend, qrecv, csend, crecv, msend, mrecv, ysend, yrecv,
):
    x, xh, z, c, y = coords()
    sibling = dev(x, z, 1 - c, y)
    peers = plane_peers(x, z, c, y) + [dev(x, z, c, mod4(y + 1)), dev(x, z, c, mod4(y + 3))]
    greet(peers)
    p_loc = pltpu.make_async_copy(dkvp.at[pl.ds(c * 4, 4)], po, loc.at[0])
    p_loc.start()
    e_loc = pltpu.make_async_copy(enc, encv.at[c], loc.at[1])
    e_loc.start()
    w_loc = pltpu.make_async_copy(w, wv.at[c], loc.at[2])
    w_loc.start()
    q_loc = pltpu.make_async_copy(dqp.at[xh * 4 + z], qg.at[xh * 4 + z], loc.at[3])
    q_loc.start()
    greeted(peers)

    here = c == xh
    p_sib = remote(dkvp.at[pl.ds((1 - c) * 4, 4)], pb, sib_s.at[0], sib_r.at[0], sibling)
    p_sib.start()
    e_sib = remote(enc, encv.at[c], sib_s.at[1], sib_r.at[1], sibling)
    e_sib.start()
    w_sib = remote(w, wv.at[c], sib_s.at[2], sib_r.at[2], sibling)
    w_sib.start()

    def d_copy(dz):
        tz = mod4(z + dz)
        return remote(ps.at[tz], rb.at[z], dsend.at[dz], drecv.at[dz], dev(c * 2 + x % 2, tz, xh, y))

    p_loc.wait()
    p_sib.wait()
    for dz in (2, 1, 3, 0):
        tz = mod4(z + dz)
        ps[tz] = (po[tz].astype(F32) + pb[tz].astype(F32)).astype(BF)
        if dz:
            d_copy(dz).start()
    d_loc = pltpu.make_async_copy(ps.at[z], rb.at[z], loc.at[4])

    @pl.when(here)
    def _():
        d_loc.start()

    @pl.when(jnp.logical_not(here))
    def _():
        d_copy(0).start()

    q_sent = []
    for dxh in (1, 0):
        for dz in (2, 1, 3, 0):
            if dxh or dz:
                tx, tz = (xh + dxh) % 2, mod4(z + dz)
                copy = remote(
                    dqp.at[tx * 4 + tz], qg.at[xh * 4 + z], qsend.at[dxh, dz], qrecv.at[dxh, dz],
                    dev(tx * 2 + x % 2, tz, c, y),
                )
                copy.start()
                q_sent.append(copy)

    for dz in (0, 1, 3, 2):
        j = mod4(z - dz)
        if dz == 0:

            @pl.when(here)
            def _():
                d_loc.wait()

            @pl.when(jnp.logical_not(here))
            def _():
                arrived(rb.at[j], drecv.at[0])
        else:
            arrived(rb.at[j], drecv.at[dz])
        turned = rb[j].T
        keys = pl.ds(pl.multiple_of(j * 64, 64), 64)
        gt[0, keys, :] = turned[0:64]
        gt[1, keys, :] = turned[64:128]

    own_tok = pl.ds(pl.multiple_of(c * 256, 256), 256)
    sib_tok = pl.ds(pl.multiple_of((1 - c) * 256, 256), 256)
    g_sib = remote(gt.at[:, :, sib_tok], gs.at[c], sib_s.at[3], sib_r.at[3], sibling)
    g_sib.start()
    gs_own = pltpu.make_async_copy(gt.at[:, :, own_tok], gs.at[c], loc.at[5])
    gs_own.start()
    e_loc.wait()
    e_sib.wait()

    def product(a, first, second):
        bx, bz = (second, first) if a == 0 else (first, second)
        columns = pl.ds(pl.multiple_of((row_group(mod4(x + bx)) * 4 + mod4(z + bz)) * 256, 256), 256)
        return jnp.dot(gt[a, :, 0:256], encv[0, :, columns], preferred_element_type=F32) + jnp.dot(
            gt[a, :, 256:512], encv[1, :, columns], preferred_element_type=F32
        )

    sent = []

    def neighbour(a, ring, step):
        along_x = (a == 1) == (ring == 0)
        return dev(mod4(x + step), z, c, y) if along_x else dev(x, mod4(z + step), c, y)

    def send_far(a, slot, ring, value):
        for half in range(2):
            cs[a, slot, half] = value[half * 128 : half * 128 + 128].astype(BF)
            at = (a, slot, half)
            copy = remote(cs.at[at], cr.at[at], csend.at[at], crecv.at[at], neighbour(a, ring, 1 - 2 * half))
            copy.start()
            sent.append(copy)

    def send_near(a, slot, ring, values):
        for half in range(2):
            value = values[half]()
            at = (a, slot, half)
            arrived(cr.at[at], crecv.at[at])
            keep_half = pl.ds(half * 128, 128)
            rest = slice(128, 256) if half == 0 else slice(0, 128)
            this = slice(0, 128) if half == 0 else slice(128, 256)
            ms[a, slot, half, pl.ds((1 - half) * 128, 128), :] = value[rest].astype(BF)
            ms[a, slot, half, keep_half, :] = (value[this] + cr[a, slot, half].astype(F32)).astype(BF)
            copy = remote(ms.at[at], mr.at[at], msend.at[at], mrecv.at[at], neighbour(a, ring, 1 - 2 * half))
            copy.start()
            sent.append(copy)

    def collect(a, slot, value):
        for half in range(2):
            at = (a, slot, half)
            arrived(mr.at[at], mrecv.at[at])
            value = value + mr[a, slot, half].astype(F32)
        return value

    def far(slot):
        for a in range(2):
            send_far(a, slot, 0, product(a, 2, slot))

    def near(slot):
        for a in range(2):
            send_near(a, slot, 0, [lambda a=a: product(a, 1, slot), lambda a=a: product(a, 3, slot)])

    def ahead(slot):
        for a in range(2):
            keep[a, slot] = product(a, 0, slot)

    def enc_rows(dy, r):
        group = mod4(y + dy)
        total = None
        for half in range(2):
            for a in range(2):
                term = jnp.dot(wv[half, a, group, r], gs[half, a], preferred_element_type=F32)
                total = term if total is None else total + term
        return total

    def y_send(src, dst, i, step):
        copy = remote(src, dst, ysend.at[i], yrecv.at[i], dev(x, z, c, mod4(y + step)))
        copy.start()
        sent.append(copy)

    def y_far():
        for half in range(2):
            for r in range(2):
                ycs[half, r] = enc_rows(2, 2 * half + r).astype(BF)
            y_send(ycs.at[half], ycr.at[half], half, 1 - 2 * half)

    def y_free():
        for half in range(2):
            for r in range(2):
                yms[half, 1 - half, r] = enc_rows(1 + 2 * half, 2 * (1 - half) + r).astype(BF)
            y_send(yms.at[half, 1 - half], ymr.at[half, 1 - half], 2 + half, 1 - 2 * half)

    def y_near():
        for half in range(2):
            for r in range(2):
                value = enc_rows(1 + 2 * half, 2 * half + r)
                if r == 0:
                    arrived(ycr.at[half], yrecv.at[half])
                yms[half, half, r] = (value + ycr[half, r].astype(F32)).astype(BF)
            y_send(yms.at[half, half], ymr.at[half, half], 4 + half, 1 - 2 * half)

    far(2)
    gs_own.wait()
    g_sib.wait()
    w_loc.wait()
    w_sib.wait()
    y_far()
    far(1)
    near(2)
    y_free()
    far(3)
    near(1)
    ahead(2)
    far(0)
    near(3)
    y_near()
    for a in range(2):
        send_far(a, 4, 1, collect(a, 2, keep[a, 2]))
    near(0)
    ahead(1)
    ahead(3)
    ahead(0)

    q_loc.wait()
    for dxh in range(2):
        for dz in range(4):
            if dxh or dz:
                src = ((xh + dxh) % 2) * 4 + mod4(z - dz)
                arrived(qg.at[src], qrecv.at[dxh, dz])
    q_out[...] = qg[...]

    for a in range(2):
        for slot in (1, 3):
            keep[a, slot] = collect(a, slot, keep[a, slot])
    for a in range(2):
        send_near(a, 4, 1, [lambda a=a: keep[a, 1], lambda a=a: keep[a, 3]])

    for r in range(4):
        total = enc_rows(0, r).astype(BF).astype(F32)
        for half in range(2):
            if r == 0:
                arrived(ymr.at[half, 1 - half], yrecv.at[2 + half])
                arrived(ymr.at[half, half], yrecv.at[4 + half])
            total = total + ymr[half, r // 2, r % 2].astype(F32)
        enc_out[pl.ds(r * 256, 256), :] = total.astype(BF)

    for a in range(2):
        fin[a] = collect(a, 4, collect(a, 0, keep[a, 0]))
    mine = pl.ds(pl.multiple_of(c * 128, 128), 128)
    theirs = pl.ds(pl.multiple_of((1 - c) * 128, 128), 128)
    f_sib = remote(fin.at[:, :, theirs], fsib, sib_s.at[4], sib_r.at[4], sibling)
    f_sib.start()
    w_out[:, pl.ds(pl.multiple_of(c * 256, 256), 256), :] = fin[:, :, mine]
    for copy in q_sent + sent + [d_copy(dz) for dz in (1, 2, 3)]:
        copy.wait_send()

    @pl.when(jnp.logical_not(here))
    def _():
        d_copy(0).wait_send()

    f_sib.wait()
    w_out[:, pl.ds(pl.multiple_of((1 - c) * 256, 256), 256), :] = fsib[...]


def finish(enc_t, qg, w_t, enc_out, q_out, w_out):
    enc_out[...] = enc_t[...].T
    for i in range(4):
        tile = pl.ds(i * 128, 128)
        even, odd = qg[2 * i].astype(F32), qg[2 * i + 1].astype(F32)
        q_out[0:128, tile] = halves(even, odd, False, True).astype(BF)
        q_out[128:256, tile] = halves(even, odd, True, False).astype(BF)
    for a in range(2):
        w_out[a] = w_t[a].T


VM = pl.BlockSpec(memory_space=pltpu.VMEM)
ANY = pl.BlockSpec(memory_space=pl.ANY)
DMA = pltpu.SemaphoreType.DMA


def params(collective_id=None):
    if collective_id is None:
        return pltpu.CompilerParams(vmem_limit_bytes=60 << 20)
    return pltpu.CompilerParams(
        collective_id=collective_id, has_side_effects=True, vmem_limit_bytes=60 << 20
    )


def body(enc_out, dec_query, ctx_grad, kv_weight, enc_seg, dec_seg):
    enc = enc_out[0]
    eseg = enc_seg.reshape(32, 128)
    dseg = dec_seg.reshape(2, 128)
    shape = jax.ShapeDtypeStruct
    wg, kvx, kvt, xt, xs, spans = pl.pallas_call(
        front,
        out_shape=(
            shape((2, 4, 4, 256, 256), BF),
            shape((4096, 256), BF),
            shape((128, 4096), BF),
            shape((8, 256, 512), BF),
            shape((8, 512, 128), BF),
            shape((8, 128), jnp.int32),
        ),
        in_specs=[ANY, VM, VM, ANY, VM, VM],
        out_specs=(ANY, ANY, ANY, ANY, ANY, VM),
        scratch_shapes=[
            pltpu.VMEM((2, 256, 4096), BF),
            pltpu.VMEM((2, 4, 4, 256, 256), BF),
            pltpu.VMEM((2, 512, 256), F32),
            pltpu.VMEM((4, 512, 128), BF),
            pltpu.VMEM((8, 512, 128), BF),
            pltpu.VMEM((8, 272, 128), BF),
            pltpu.VMEM((8, 272, 128), BF),
            pltpu.VMEM((4096, 256), BF),
            pltpu.VMEM((128, 4096), BF),
            pltpu.VMEM((8, 256, 512), BF),
            pltpu.VMEM((8, 512, 128), BF),
            DMA((5,)), DMA((18,)), DMA((2,)), DMA((2,)),
            DMA((2, 4, 4, 2)), DMA((2, 4, 4, 2)),
            DMA((2, 4)), DMA((2, 4)),
            DMA((4, 2)), DMA((2, 4)),
            DMA((2, 4)), DMA((2, 4)),
        ],
        compiler_params=params(1),
        name="front",
    )(enc, dec_query[0], ctx_grad[0], kv_weight, dseg, eseg)

    dkvp, dqp = pl.pallas_call(
        attend,
        out_shape=(shape((8, 512, 128), BF), shape((8, 128, 128), BF)),
        in_specs=[pl.BlockSpec(memory_space=pltpu.SMEM), ANY, ANY, ANY, ANY],
        out_specs=(VM, VM),
        scratch_shapes=[
            pltpu.VMEM((4096, 256), BF),
            pltpu.VMEM((128, 4096), BF),
            pltpu.VMEM((8, 256, 512), BF),
            pltpu.VMEM((8, 512, 128), BF),
            pltpu.VMEM((4096, 512), F32),
            pltpu.VMEM((4096, 512), BF),
            pltpu.VMEM((4096, 128), F32),
            DMA((2,)), DMA((8,)), DMA((8,)),
        ],
        compiler_params=params(),
        name="attend",
    )(spans, kvx, kvt, xt, xs)

    enc_t, qg, w_t = pl.pallas_call(
        back,
        out_shape=(shape((1024, 256), BF), shape((8, 128, 128), BF), shape((2, 512, 128), F32)),
        in_specs=[ANY, ANY, ANY, ANY],
        out_specs=(VM, VM, VM),
        scratch_shapes=[
            pltpu.VMEM((2, 256, 4096), BF),
            pltpu.VMEM((2, 2, 4, 4, 256, 256), BF),
            pltpu.VMEM((4, 512, 128), BF),
            pltpu.VMEM((4, 512, 128), BF),
            pltpu.VMEM((4, 512, 128), BF),
            pltpu.VMEM((4, 512, 128), BF),
            pltpu.VMEM((2, 256, 512), BF),
            pltpu.VMEM((2, 2, 256, 256), BF),
            pltpu.VMEM((8, 128, 128), BF),
            pltpu.VMEM((2, 5, 2, 128, 256), BF),
            pltpu.VMEM((2, 5, 2, 128, 256), BF),
            pltpu.VMEM((2, 5, 2, 256, 256), BF),
            pltpu.VMEM((2, 5, 2, 256, 256), BF),
            pltpu.VMEM((2, 4, 256, 256), F32),
            pltpu.VMEM((2, 256, 256), F32),
            pltpu.VMEM((2, 256, 128), F32),
            pltpu.VMEM((2, 2, 256, 256), BF),
            pltpu.VMEM((2, 2, 256, 256), BF),
            pltpu.VMEM((2, 2, 2, 256, 256), BF),
            pltpu.VMEM((2, 2, 2, 256, 256), BF),
            DMA((6,)), DMA((5,)), DMA((5,)),
            DMA((4,)), DMA((4,)),
            DMA((2, 4)), DMA((2, 4)),
            DMA((2, 5, 2)), DMA((2, 5, 2)),
            DMA((2, 5, 2)), DMA((2, 5, 2)),
            DMA((6,)), DMA((6,)),
        ],
        compiler_params=params(2),
        name="back",
    )(dkvp, dqp, enc, wg)

    enc_grad, q_grad, w_grad = pl.pallas_call(
        finish,
        out_shape=(shape((256, 1024), BF), shape((256, 512), BF), shape((2, 128, 512), F32)),
        in_specs=[VM] * 3,
        out_specs=(VM, VM, VM),
        compiler_params=params(),
        name="finish",
    )(enc_t, qg, w_t)
    return enc_grad[None], q_grad[None], w_grad


def solution(mesh):
    placed = (
        P("dp", "seq", None),
        P("dp", "seq", "mp"),
        P("dp", "seq", "mp"),
        P(None, ("dp", "seq"), "mp"),
        P("dp", None),
        P("dp", "seq"),
    )
    return jax.shard_map(
        body,
        mesh=mesh,
        in_specs=placed,
        out_specs=(P("dp", "seq", "mp"), P("dp", "seq", "mp"), P(None, ("dp", "seq"), "mp")),
        check_vma=False,
    )
```

```python
import functools

import jax
import jax.numpy as jnp
from jax import lax
from jax.experimental import pallas as pl
from jax.experimental.pallas import tpu as pltpu
from jax.sharding import PartitionSpec as P

MESH = pl.DeviceIdType.MESH
BF = jnp.bfloat16
F32 = jnp.float32
NEG = -1e30
KB = 256


def coords():
    dp, seq, y = lax.axis_index("dp"), lax.axis_index("seq"), lax.axis_index("mp")
    xh = seq // 8
    return xh * 2 + dp, xh, (seq // 2) % 4, seq % 2, y


def dev(x, z, core, y):
    return (x % 2, (x // 2) * 8 + z * 2 + core, y)


def row_group(x):
    return (x % 2) * 2 + x // 2


def mod4(v):
    return (v + 4) % 4


def remote(src, dst, send, recv, device):
    return pltpu.make_async_remote_copy(
        src_ref=src, dst_ref=dst, send_sem=send, recv_sem=recv, device_id=device, device_id_type=MESH
    )


def arrived(dst, sem):
    pltpu.make_async_copy(dst, dst, sem).wait()


def greet(peers):
    for peer in peers:
        pl.semaphore_signal(pltpu.get_barrier_semaphore(), inc=1, device_id=peer, device_id_type=MESH)


def greeted(peers):
    pl.semaphore_wait(pltpu.get_barrier_semaphore(), len(peers))


def plane_peers(x, z, c, y):
    peers = [dev(x, z, 1 - c, y), dev(mod4(x + 1), z, c, y), dev(mod4(x + 3), z, c, y)]
    for dx in (0, 2):
        for dz in range(4):
            if dx or dz:
                peers += [dev(mod4(x + dx), mod4(z + dz), core, y) for core in range(2)]
    return peers


def lanes_of(shape):
    return lax.broadcasted_iota(jnp.int32, shape, 1)


def halves(first, second, shift_first, shift_second):
    first = pltpu.roll(first, 64, 1) if shift_first else first
    second = pltpu.roll(second, 64, 1) if shift_second else second
    return jnp.where(lanes_of(first.shape) < 64, first, second)


def front(
    enc, q, do, w, dseg, eseg,
    wg_out, kvx_out, kvt_out, xt_out, xs_out, spans,
    encv, wg, acc, kvs, kvb, qs, qb, kvx, kvt, xt, xs,
    loc, save, sib_s, sib_r, ws, wr, qsend, qrecv, ksend, krecv, fsend, frecv,
):
    x, xh, z, c, y = coords()
    me = row_group(x)
    t = xh * 4 + z
    sibling = dev(x, z, 1 - c, y)
    peers = plane_peers(x, z, c, y)
    greet(peers)

    own = pl.multiple_of(c * 256, 256)
    other = pl.multiple_of((1 - c) * 256, 256)
    rows = pl.ds(pl.multiple_of(c * 128, 128), 128)
    w_loc = pltpu.make_async_copy(w.at[:, :, pl.ds(own, 256)], wg.at[:, me, z, rows], loc.at[0])
    w_loc.start()
    e_loc = pltpu.make_async_copy(enc, encv.at[c], loc.at[1])
    e_loc.start()

    ids = dseg[...].astype(F32)
    row = lax.broadcasted_iota(jnp.int32, (16, 128), 0)
    id_rows = jnp.where(row == 0, ids[0:1], jnp.where(row == 1, ids[1:2], 0.0)).astype(BF)
    for h in range(8):
        tile = pl.ds((h // 2) * 128, 128)
        odd = h % 2 == 1
        qs[h, 0:256, :] = halves(q[:, tile].astype(F32), do[:, tile].astype(F32), odd, not odd).astype(BF)
        qs[h, 256:272, :] = id_rows
    q_loc = pltpu.make_async_copy(qs.at[t], qb.at[t], loc.at[2])
    q_loc.start()
    greeted(peers)

    w_sib = remote(w.at[:, :, pl.ds(other, 256)], wg.at[:, me, z, rows], sib_s.at[0], sib_r.at[0], sibling)
    w_sib.start()
    q_sent = []
    for dxh in (1, 0):
        for dz in (2, 1, 3, 0):
            if dxh == 0 and dz == 0:
                continue
            hx, hz = (xh + dxh) % 2, mod4(z + dz)
            copy = remote(
                qs.at[hx * 4 + hz], qb.at[t], qsend.at[dxh, dz], qrecv.at[dxh, dz],
                dev(mod4(x + 2 * dxh), hz, c, y),
            )
            copy.start()
            q_sent.append(copy)
    e_sib = remote(enc, encv.at[c], sib_s.at[1], sib_r.at[1], sibling)
    e_sib.start()
    w_loc.wait()
    w_sib.wait()

    def place(a, first, second):
        bx, bz = (first, second) if a == 0 else (second, first)
        return row_group(mod4(x - bx)), mod4(z - bz)

    def block_of(a, first, second, half=None):
        group, bz = place(a, first, second)
        block = wg.at[a, group, bz]
        return block if half is None else block.at[pl.ds(half * 128, 128)]

    sent = []

    def pass_on(a, first, second, ring, step, half=None):
        block = block_of(a, first, second, half)
        to_first, to_second = (first + step) % 4 if ring == 0 else first, (second + step) % 4 if ring else second
        sem = (a, to_first, to_second, half or 0)
        along_x = (a == 0) == (ring == 0)
        target = dev(mod4(x + step), z, c, y) if along_x else dev(x, mod4(z + step), c, y)
        copy = remote(block, block, ws.at[sem], wr.at[sem], target)
        copy.start()
        sent.append(copy)

    def take(a, first, second):
        if second == 2 or (first == 2 and second == 0):
            for half in range(2):
                arrived(block_of(a, first, second, half), wr.at[a, first, second, half])
        else:
            arrived(block_of(a, first, second), wr.at[a, first, second, 0])

    def multiply(a, first, second, fresh=False):
        group, bz = place(a, first, second)
        columns = pl.ds(pl.multiple_of((group * 4 + bz) * 256, 256), 256)
        for half in range(2):
            term = jnp.dot(encv[half, :, columns], wg[a, group, bz], preferred_element_type=F32)
            if fresh:
                acc[a, pl.ds(half * 256, 256), :] = term
            else:
                acc[a, pl.ds(half * 256, 256), :] += term

    def both_ways(a, first):
        pass_on(a, first, 0, 1, 1)
        pass_on(a, first, 0, 1, -1)

    for step in (1, -1):
        for a in range(2):
            pass_on(a, 0, 0, 0, step)
    for a in range(2):
        both_ways(a, 0)

    def one_hot(i, _):
        seg = eseg[pl.ds(i, 1), :].astype(F32)
        row = lax.broadcasted_iota(jnp.int32, (128, 128), 0).astype(F32)
        hot = jnp.where(row == seg, 1.0, 0.0)
        kvx[pl.ds(pl.multiple_of(i * 128, 128), 128), 128:256] = hot.T.astype(BF)
        return 0

    lax.fori_loop(0, 32, one_hot, 0)

    for a in range(2):
        take(a, 1, 0)
        pass_on(a, 1, 0, 0, 1, 0)
        take(a, 3, 0)
        pass_on(a, 3, 0, 0, -1, 1)
    for a in range(2):
        both_ways(a, 1)
        both_ways(a, 3)
    for a in range(2):
        take(a, 0, 1)
        pass_on(a, 0, 1, 1, 1, 0)
        take(a, 0, 3)
        pass_on(a, 0, 3, 1, -1, 1)
    for a in range(2):
        take(a, 2, 0)
        both_ways(a, 2)
    e_loc.wait()
    e_sib.wait()
    for a in range(2):
        multiply(a, 0, 0, True)
        for first, second in ((1, 0), (3, 0), (0, 1), (0, 3), (2, 0)):
            multiply(a, first, second)

    q_loc.wait()
    for dxh in range(2):
        for dz in range(4):
            if dxh or dz:
                src = ((xh + dxh) % 2) * 4 + mod4(z - dz)
                arrived(qb.at[src], qrecv.at[dxh, dz])

    def prepare(b, _):
        block = qb[b, 0:256, :]
        low = lanes_of((256, 128)) < 64
        zero = jnp.zeros_like(block)
        xs[b, 0:256, :] = jnp.where(low, block, zero)
        xs[b, 256:512, :] = jnp.where(low, zero, block)
        turned = block.T
        xt[b, 0:64, 0:256] = turned[0:64] * jnp.asarray(0.125, BF)
        xt[b, 64:128, 256:512] = turned[64:128]
        xt[b, 0:64, 256:512] = jnp.zeros((64, 256), BF)
        xt[b, 64:128, 0:256] = jnp.zeros((64, 256), BF)
        xt[b, 128:256, :] = jnp.zeros((128, 512), BF)
        ids = qb[b, 256:272, :].astype(F32)
        ids = jnp.concatenate([ids[0:1], ids[1:2]], axis=1)
        row = lax.broadcasted_iota(jnp.int32, (16, 256), 0)
        differs = (row < 4) & (row.astype(F32) != ids)
        xt[b, 128:144, 0:256] = jnp.where(differs, NEG, 0.0).astype(BF)
        seg = eseg[...].astype(F32)
        low_id, high_id = jnp.min(ids, axis=1, keepdims=True), jnp.max(ids, axis=1, keepdims=True)
        begin = jnp.sum(jnp.where(seg < low_id, 1.0, 0.0), axis=(0, 1), keepdims=True)
        end = jnp.sum(jnp.where(seg <= high_id, 1.0, 0.0), axis=(0, 1), keepdims=True)
        begin = jnp.floor(begin * (1.0 / 128)) * 128.0
        count = jnp.floor((end - begin + (KB - 1)) * (1.0 / KB))
        begin = jnp.minimum(begin, 4096.0 - count * KB)
        spans[pl.ds(b, 1), :] = jnp.where(lanes_of((1, 128)) == 0, begin, count).astype(jnp.int32)
        return 0

    for first in (1, 3, 2):
        for a in range(2):
            take(a, first, 1)
            pass_on(a, first, 1, 1, 1, 0)
            take(a, first, 3)
            pass_on(a, first, 3, 1, -1, 1)
            multiply(a, first, 1)
            multiply(a, first, 3)
        if first != 2:
            lax.fori_loop(0 if first == 1 else 4, 4 if first == 1 else 8, prepare, 0)
    saved = [
        pltpu.make_async_copy(xt, xt_out, save.at[8]),
        pltpu.make_async_copy(xs, xs_out, save.at[9]),
    ]
    for copy in saved:
        copy.start()
    for first in (0, 1, 3, 2):
        for a in range(2):
            take(a, first, 2)
            multiply(a, first, 2)

    for j in range(4):
        tile = pl.ds((j // 2) * 128, 128)
        odd = j % 2 == 1
        kvs[j] = halves(acc[0, :, tile], acc[1, :, tile], odd, not odd).astype(BF)

    ex = (c + 2 - xh) % 2
    tx = c * 2 + x % 2
    here = c == xh

    def kv_copy(dz, core):
        hz = mod4(z + dz)
        part = pl.ds(core * 256, 256)
        return remote(
            kvs.at[hz, part], kvb.at[t, part], ksend.at[dz, core], krecv.at[ex, dz], dev(tx, hz, core, y)
        )

    def kv_local(core):
        part = pl.ds(core * 256, 256)
        return pltpu.make_async_copy(kvs.at[z, part], kvb.at[t, part], loc.at[4])

    k_sent = [kv_copy(dz, core) for dz in (2, 1, 3) for core in range(2)]
    for copy in k_sent:
        copy.start()
    for core in range(2):
        local = jnp.logical_and(here, c == core)

        @pl.when(local)
        def _():
            kv_local(core).start()

        @pl.when(jnp.logical_not(local))
        def _():
            kv_copy(0, core).start()

    w_save = pltpu.make_async_copy(wg, wg_out, loc.at[3])
    w_save.start()

    mine = pl.ds(pl.multiple_of(c * 256, 256), 256)
    theirs = pl.ds(pl.multiple_of((1 - c) * 256, 256), 256)

    def source(e, dz):
        return ((xh + e) % 2) * 4 + mod4(z - dz)

    f_sent = []

    def hand_over(e, dz):
        src = source(e, dz)
        if e == 0 and dz == 0:

            @pl.when(here)
            def _():
                for core in range(2):

                    @pl.when(c == core)
                    def _():
                        kv_local(core).wait()

            @pl.when(jnp.logical_not(here))
            def _():
                arrived(kvb.at[src, mine], krecv.at[0, 0])
        else:
            arrived(kvb.at[src, mine], krecv.at[e, dz])
        copy = remote(kvb.at[src, mine], kvb.at[src, mine], fsend.at[e, dz], frecv.at[e, dz], sibling)
        copy.start()
        f_sent.append(copy)

    def use(e, dz):
        src = source(e, dz)
        arrived(kvb.at[src, theirs], frecv.at[e, dz])
        block = kvb[src]
        span = pl.ds(pl.multiple_of(src * 512, 512), 512)
        kvx[span, 0:128] = block
        kvt[:, span] = block.T
        for copy in (
            pltpu.make_async_copy(kvx.at[span], kvx_out.at[span], save.at[e * 4 + dz]),
            pltpu.make_async_copy(kvt.at[:, span], kvt_out.at[:, span], save.at[10 + e * 4 + dz]),
        ):
            copy.start()
            saved.append(copy)

    order = [(e, dz) for dz in (0, 1, 3, 2) for e in (0, 1)]
    for i, at in enumerate(order):
        hand_over(*at)
        if i:
            use(*order[i - 1])
    use(*order[-1])

    for copy in sent + q_sent + k_sent + f_sent:
        copy.wait_send()
    for core in range(2):

        @pl.when(jnp.logical_not(jnp.logical_and(here, c == core)))
        def _():
            kv_copy(0, core).wait_send()

    w_save.wait()
    for copy in saved:
        copy.wait()


def attend(
    spans, kvx_in, kvt_in, xt_in, xs_in, dkv_out, dq_out, kvx, kvt, xt, xs, tt, low_ps, dkv, sem, xt_sem, xs_sem
):
    kvx_copy = pltpu.make_async_copy(kvx_in, kvx, sem.at[0])
    kvt_copy = pltpu.make_async_copy(kvt_in, kvt, sem.at[1])

    def xt_copy(b):
        return pltpu.make_async_copy(xt_in.at[b], xt.at[b], xt_sem.at[b])

    def xs_copy(b):
        return pltpu.make_async_copy(xs_in.at[b], xs.at[b], xs_sem.at[b])

    xt_copy(0).start()
    kvx_copy.start()
    xs_copy(0).start()
    kvt_copy.start()
    for b in range(1, 8):
        xt_copy(b).start()
        xs_copy(b).start()
    dkv[...] = jnp.zeros_like(dkv)
    kvx_copy.wait()

    def one_block(b, _):
        begin, count = spans[b, 0], spans[b, 1]
        xt_copy(b).wait()

        def sweep(step, carry):
            done = 0
            for blocks in (8, 3, 2, 1):
                times = (count - done) // blocks

                def piece(i, value, done=done, blocks=blocks):
                    first = pl.multiple_of(begin + (done + i * blocks) * KB, 128)
                    return step(first, blocks * KB, value)

                carry = lax.fori_loop(0, times, piece, carry)
                done = done + times * blocks
            return carry

        def fold(op, v):
            return op(v.reshape(v.shape[0] // 8, 8, 256), axis=0)

        def scores(first, length, top):
            rows = pl.ds(first, length)
            both = jnp.dot(kvx[rows, :], xt[b], preferred_element_type=F32)
            tt[rows, :] = both
            return jnp.maximum(top, fold(jnp.max, both[:, 0:256]))

        top = sweep(scores, jnp.full((8, 256), -3e38, F32))
        top = jnp.max(top, axis=0, keepdims=True)

        def weigh(first, length, total):
            rows = pl.ds(first, length)
            e = jnp.exp(tt[rows, 0:256] - top)
            tt[rows, 0:256] = e
            return total + fold(jnp.sum, e)

        total = sweep(weigh, jnp.zeros((8, 256), F32))
        inv = 1.0 / jnp.sum(total, axis=0, keepdims=True)

        def deltas(first, length, delta):
            rows = pl.ds(first, length)
            low_p = (tt[rows, 0:256] * inv).astype(BF)
            low_ps[rows, :] = low_p
            return delta + fold(jnp.sum, low_p.astype(F32) * tt[rows, 256:512])

        delta = sweep(deltas, jnp.zeros((8, 256), F32))
        delta = jnp.sum(delta, axis=0, keepdims=True)
        inv8 = inv * 0.125
        xs_copy(b).wait()

        @pl.when(b == 0)
        def _():
            kvt_copy.wait()

        def grads(first, length, dq):
            for part in range(0, length, KB):
                rows = pl.ds(pl.multiple_of(first + part, 128), KB)
                ds = ((tt[rows, 0:256] * inv8) * (tt[rows, 256:512] - delta)).astype(BF)
                dkv[rows, :] += jnp.dot(ds, xs[b, 0:256], preferred_element_type=F32) + jnp.dot(
                    low_ps[rows, :], xs[b, 256:512], preferred_element_type=F32
                )
                dq = dq + jnp.dot(kvt[0:64, rows], ds, preferred_element_type=F32)
            return dq

        dq = sweep(grads, jnp.zeros((64, 256), F32))
        dq_out[b] = jnp.concatenate([dq[:, 0:128], dq[:, 128:256]], axis=0).T.astype(BF)
        return 0

    lax.fori_loop(0, 8, one_block, 0)
    dkv_out[...] = dkv[...].astype(BF).reshape(dkv_out.shape)


def back(
    dkvp, dqp, enc, w,
    enc_out, q_out, w_out,
    encv, wv, po, pb, ps, rb, gt, gs, qg, cs, cr, ms, mr, keep, fin, fsib, ycs, ycr, yms, ymr,
    loc, sib_s, sib_r, dsend, drecv, qsend, qrecv, csend, crecv, msend, mrecv, ysend, yrecv,
):
    x, xh, z, c, y = coords()
    sibling = dev(x, z, 1 - c, y)
    peers = plane_peers(x, z, c, y) + [dev(x, z, c, mod4(y + 1)), dev(x, z, c, mod4(y + 3))]
    greet(peers)
    p_loc = pltpu.make_async_copy(dkvp.at[pl.ds(c * 4, 4)], po, loc.at[0])
    p_loc.start()
    e_loc = pltpu.make_async_copy(enc, encv.at[c], loc.at[1])
    e_loc.start()
    w_loc = pltpu.make_async_copy(w, wv.at[c], loc.at[2])
    w_loc.start()
    q_loc = pltpu.make_async_copy(dqp.at[xh * 4 + z], qg.at[xh * 4 + z], loc.at[3])
    q_loc.start()
    greeted(peers)

    here = c == xh
    p_sib = remote(dkvp.at[pl.ds((1 - c) * 4, 4)], pb, sib_s.at[0], sib_r.at[0], sibling)
    p_sib.start()
    e_sib = remote(enc, encv.at[c], sib_s.at[1], sib_r.at[1], sibling)
    e_sib.start()
    w_sib = remote(w, wv.at[c], sib_s.at[2], sib_r.at[2], sibling)
    w_sib.start()

    def d_copy(dz):
        tz = mod4(z + dz)
        return remote(ps.at[tz], rb.at[z], dsend.at[dz], drecv.at[dz], dev(c * 2 + x % 2, tz, xh, y))

    p_loc.wait()
    p_sib.wait()
    for dz in (2, 1, 3, 0):
        tz = mod4(z + dz)
        ps[tz] = (po[tz].astype(F32) + pb[tz].astype(F32)).astype(BF)
        if dz:
            d_copy(dz).start()
    d_loc = pltpu.make_async_copy(ps.at[z], rb.at[z], loc.at[4])

    @pl.when(here)
    def _():
        d_loc.start()

    @pl.when(jnp.logical_not(here))
    def _():
        d_copy(0).start()

    q_sent = []
    for dxh in (1, 0):
        for dz in (2, 1, 3, 0):
            if dxh or dz:
                tx, tz = (xh + dxh) % 2, mod4(z + dz)
                copy = remote(
                    dqp.at[tx * 4 + tz], qg.at[xh * 4 + z], qsend.at[dxh, dz], qrecv.at[dxh, dz],
                    dev(tx * 2 + x % 2, tz, c, y),
                )
                copy.start()
                q_sent.append(copy)

    for dz in (0, 1, 3, 2):
        j = mod4(z - dz)
        if dz == 0:

            @pl.when(here)
            def _():
                d_loc.wait()

            @pl.when(jnp.logical_not(here))
            def _():
                arrived(rb.at[j], drecv.at[0])
        else:
            arrived(rb.at[j], drecv.at[dz])
        turned = rb[j].T
        keys = pl.ds(pl.multiple_of(j * 64, 64), 64)
        gt[0, keys, :] = turned[0:64]
        gt[1, keys, :] = turned[64:128]

    own_tok = pl.ds(pl.multiple_of(c * 256, 256), 256)
    sib_tok = pl.ds(pl.multiple_of((1 - c) * 256, 256), 256)
    g_sib = remote(gt.at[:, :, sib_tok], gs.at[c], sib_s.at[3], sib_r.at[3], sibling)
    g_sib.start()
    gs_own = pltpu.make_async_copy(gt.at[:, :, own_tok], gs.at[c], loc.at[5])
    gs_own.start()
    e_loc.wait()
    e_sib.wait()

    def product(a, first, second):
        bx, bz = (second, first) if a == 0 else (first, second)
        columns = pl.ds(pl.multiple_of((row_group(mod4(x + bx)) * 4 + mod4(z + bz)) * 256, 256), 256)
        return jnp.dot(gt[a, :, 0:256], encv[0, :, columns], preferred_element_type=F32) + jnp.dot(
            gt[a, :, 256:512], encv[1, :, columns], preferred_element_type=F32
        )

    sent = []

    def neighbour(a, ring, step):
        along_x = (a == 1) == (ring == 0)
        return dev(mod4(x + step), z, c, y) if along_x else dev(x, mod4(z + step), c, y)

    def send_far(a, slot, ring, value):
        for half in range(2):
            cs[a, slot, half] = value[half * 128 : half * 128 + 128].astype(BF)
            at = (a, slot, half)
            copy = remote(cs.at[at], cr.at[at], csend.at[at], crecv.at[at], neighbour(a, ring, 1 - 2 * half))
            copy.start()
            sent.append(copy)

    def send_near(a, slot, ring, values):
        for half in range(2):
            value = values[half]()
            at = (a, slot, half)
            arrived(cr.at[at], crecv.at[at])
            keep_half = pl.ds(half * 128, 128)
            rest = slice(128, 256) if half == 0 else slice(0, 128)
            this = slice(0, 128) if half == 0 else slice(128, 256)
            ms[a, slot, half, pl.ds((1 - half) * 128, 128), :] = value[rest].astype(BF)
            ms[a, slot, half, keep_half, :] = (value[this] + cr[a, slot, half].astype(F32)).astype(BF)
            copy = remote(ms.at[at], mr.at[at], msend.at[at], mrecv.at[at], neighbour(a, ring, 1 - 2 * half))
            copy.start()
            sent.append(copy)

    def collect(a, slot, value):
        for half in range(2):
            at = (a, slot, half)
            arrived(mr.at[at], mrecv.at[at])
            value = value + mr[a, slot, half].astype(F32)
        return value

    def far(slot):
        for a in range(2):
            send_far(a, slot, 0, product(a, 2, slot))

    def near(slot):
        for a in range(2):
            send_near(a, slot, 0, [lambda a=a: product(a, 1, slot), lambda a=a: product(a, 3, slot)])

    def ahead(slot):
        for a in range(2):
            keep[a, slot] = product(a, 0, slot)

    def enc_rows(dy, r):
        group = mod4(y + dy)
        total = None
        for half in range(2):
            for a in range(2):
                term = jnp.dot(wv[half, a, group, r], gs[half, a], preferred_element_type=F32)
                total = term if total is None else total + term
        return total

    def y_send(src, dst, i, step):
        copy = remote(src, dst, ysend.at[i], yrecv.at[i], dev(x, z, c, mod4(y + step)))
        copy.start()
        sent.append(copy)

    def y_far():
        for half in range(2):
            for r in range(2):
                ycs[half, r] = enc_rows(2, 2 * half + r).astype(BF)
            y_send(ycs.at[half], ycr.at[half], half, 1 - 2 * half)

    def y_free():
        for half in range(2):
            for r in range(2):
                yms[half, 1 - half, r] = enc_rows(1 + 2 * half, 2 * (1 - half) + r).astype(BF)
            y_send(yms.at[half, 1 - half], ymr.at[half, 1 - half], 2 + half, 1 - 2 * half)

    def y_near():
        for half in range(2):
            for r in range(2):
                value = enc_rows(1 + 2 * half, 2 * half + r)
                if r == 0:
                    arrived(ycr.at[half], yrecv.at[half])
                yms[half, half, r] = (value + ycr[half, r].astype(F32)).astype(BF)
            y_send(yms.at[half, half], ymr.at[half, half], 4 + half, 1 - 2 * half)

    far(2)
    gs_own.wait()
    g_sib.wait()
    w_loc.wait()
    w_sib.wait()
    y_far()
    far(1)
    near(2)
    y_free()
    far(3)
    near(1)
    ahead(2)
    far(0)
    near(3)
    y_near()
    for a in range(2):
        send_far(a, 4, 1, collect(a, 2, keep[a, 2]))
    near(0)
    ahead(1)
    ahead(3)
    ahead(0)

    q_loc.wait()
    for dxh in range(2):
        for dz in range(4):
            if dxh or dz:
                src = ((xh + dxh) % 2) * 4 + mod4(z - dz)
                arrived(qg.at[src], qrecv.at[dxh, dz])
    for i in range(4):
        tile = pl.ds(i * 128, 128)
        even, odd = qg[2 * i].astype(F32), qg[2 * i + 1].astype(F32)
        q_out[0:128, tile] = halves(even, odd, False, True).astype(BF)
        q_out[128:256, tile] = halves(even, odd, True, False).astype(BF)

    for a in range(2):
        for slot in (1, 3):
            keep[a, slot] = collect(a, slot, keep[a, slot])
    for a in range(2):
        send_near(a, 4, 1, [lambda a=a: keep[a, 1], lambda a=a: keep[a, 3]])

    for r in range(4):
        total = enc_rows(0, r).astype(BF).astype(F32)
        for half in range(2):
            if r == 0:
                arrived(ymr.at[half, 1 - half], yrecv.at[2 + half])
                arrived(ymr.at[half, half], yrecv.at[4 + half])
            total = total + ymr[half, r // 2, r % 2].astype(F32)
        enc_out[:, pl.ds(r * 256, 256)] = total.T.astype(BF)

    for a in range(2):
        fin[a] = collect(a, 4, collect(a, 0, keep[a, 0])).T
    mine = pl.ds(pl.multiple_of(c * 128, 128), 128)
    theirs = pl.ds(pl.multiple_of((1 - c) * 128, 128), 128)
    f_sib = remote(fin.at[:, theirs], fsib, sib_s.at[4], sib_r.at[4], sibling)
    f_sib.start()
    w_out[:, :, pl.ds(pl.multiple_of(c * 256, 256), 256)] = fin[:, mine]
    for copy in q_sent + sent + [d_copy(dz) for dz in (1, 2, 3)]:
        copy.wait_send()

    @pl.when(jnp.logical_not(here))
    def _():
        d_copy(0).wait_send()

    f_sib.wait()
    w_out[:, :, pl.ds(pl.multiple_of((1 - c) * 256, 256), 256)] = fsib[...]


def finish(*refs):
    given, results, held, (load, store) = refs[0:3], refs[3:6], refs[6:9], refs[9:11]
    parts = []
    for i in range(3):
        rows = given[i].shape[-2] // 4
        for k in range(4):
            at = (slice(None),) * (len(given[i].shape) - 2) + (pl.ds(k * rows, rows),)
            parts.append(
                (
                    pltpu.make_async_copy(given[i].at[at], held[i].at[at], load.at[i, k]),
                    pltpu.make_async_copy(held[i].at[at], results[i].at[at], store.at[i, k]),
                )
            )
    for first, _ in parts:
        first.start()
    for first, second in parts:
        first.wait()
        second.start()
    for _, second in parts:
        second.wait()


VM = pl.BlockSpec(memory_space=pltpu.VMEM)
ANY = pl.BlockSpec(memory_space=pl.ANY)
DMA = pltpu.SemaphoreType.DMA


def params(collective_id=None):
    if collective_id is None:
        return pltpu.CompilerParams(vmem_limit_bytes=60 << 20)
    return pltpu.CompilerParams(
        collective_id=collective_id, has_side_effects=True, vmem_limit_bytes=60 << 20
    )


def body(enc_out, dec_query, ctx_grad, kv_weight, enc_seg, dec_seg):
    enc = enc_out[0]
    eseg = enc_seg.reshape(32, 128)
    dseg = dec_seg.reshape(2, 128)
    shape = jax.ShapeDtypeStruct
    wg, kvx, kvt, xt, xs, spans = pl.pallas_call(
        front,
        out_shape=(
            shape((2, 4, 4, 256, 256), BF),
            shape((4096, 256), BF),
            shape((128, 4096), BF),
            shape((8, 256, 512), BF),
            shape((8, 512, 128), BF),
            shape((8, 128), jnp.int32),
        ),
        in_specs=[ANY, VM, VM, ANY, VM, VM],
        out_specs=(ANY, ANY, ANY, ANY, ANY, VM),
        scratch_shapes=[
            pltpu.VMEM((2, 256, 4096), BF),
            pltpu.VMEM((2, 4, 4, 256, 256), BF),
            pltpu.VMEM((2, 512, 256), F32),
            pltpu.VMEM((4, 512, 128), BF),
            pltpu.VMEM((8, 512, 128), BF),
            pltpu.VMEM((8, 272, 128), BF),
            pltpu.VMEM((8, 272, 128), BF),
            pltpu.VMEM((4096, 256), BF),
            pltpu.VMEM((128, 4096), BF),
            pltpu.VMEM((8, 256, 512), BF),
            pltpu.VMEM((8, 512, 128), BF),
            DMA((5,)), DMA((18,)), DMA((2,)), DMA((2,)),
            DMA((2, 4, 4, 2)), DMA((2, 4, 4, 2)),
            DMA((2, 4)), DMA((2, 4)),
            DMA((4, 2)), DMA((2, 4)),
            DMA((2, 4)), DMA((2, 4)),
        ],
        compiler_params=params(1),
        name="front",
    )(enc, dec_query[0], ctx_grad[0], kv_weight, dseg, eseg)

    dkvp, dqp = pl.pallas_call(
        attend,
        out_shape=(shape((8, 512, 128), BF), shape((8, 128, 128), BF)),
        in_specs=[pl.BlockSpec(memory_space=pltpu.SMEM), ANY, ANY, ANY, ANY],
        out_specs=(VM, VM),
        scratch_shapes=[
            pltpu.VMEM((4096, 256), BF),
            pltpu.VMEM((128, 4096), BF),
            pltpu.VMEM((8, 256, 512), BF),
            pltpu.VMEM((8, 512, 128), BF),
            pltpu.VMEM((4096, 512), F32),
            pltpu.VMEM((4096, 256), BF),
            pltpu.VMEM((4096, 128), F32),
            DMA((2,)), DMA((8,)), DMA((8,)),
        ],
        compiler_params=params(),
        name="attend",
    )(spans, kvx, kvt, xt, xs)

    grads = pl.pallas_call(
        back,
        out_shape=(shape((256, 1024), BF), shape((256, 512), BF), shape((2, 128, 512), F32)),
        in_specs=[ANY, ANY, ANY, ANY],
        out_specs=(VM, VM, VM),
        scratch_shapes=[
            pltpu.VMEM((2, 256, 4096), BF),
            pltpu.VMEM((2, 2, 4, 4, 256, 256), BF),
            pltpu.VMEM((4, 512, 128), BF),
            pltpu.VMEM((4, 512, 128), BF),
            pltpu.VMEM((4, 512, 128), BF),
            pltpu.VMEM((4, 512, 128), BF),
            pltpu.VMEM((2, 256, 512), BF),
            pltpu.VMEM((2, 2, 256, 256), BF),
            pltpu.VMEM((8, 128, 128), BF),
            pltpu.VMEM((2, 5, 2, 128, 256), BF),
            pltpu.VMEM((2, 5, 2, 128, 256), BF),
            pltpu.VMEM((2, 5, 2, 256, 256), BF),
            pltpu.VMEM((2, 5, 2, 256, 256), BF),
            pltpu.VMEM((2, 4, 256, 256), F32),
            pltpu.VMEM((2, 256, 256), F32),
            pltpu.VMEM((2, 128, 256), F32),
            pltpu.VMEM((2, 2, 256, 256), BF),
            pltpu.VMEM((2, 2, 256, 256), BF),
            pltpu.VMEM((2, 2, 2, 256, 256), BF),
            pltpu.VMEM((2, 2, 2, 256, 256), BF),
            DMA((6,)), DMA((5,)), DMA((5,)),
            DMA((4,)), DMA((4,)),
            DMA((2, 4)), DMA((2, 4)),
            DMA((2, 5, 2)), DMA((2, 5, 2)),
            DMA((2, 5, 2)), DMA((2, 5, 2)),
            DMA((6,)), DMA((6,)),
        ],
        compiler_params=params(2),
        name="back",
    )(dkvp, dqp, enc, wg)

    enc_grad, q_grad, w_grad = pl.pallas_call(
        finish,
        out_shape=(shape((256, 1024), BF), shape((256, 512), BF), shape((2, 128, 512), F32)),
        in_specs=[ANY] * 3,
        out_specs=(ANY, ANY, ANY),
        scratch_shapes=[
            pltpu.VMEM((256, 1024), BF), pltpu.VMEM((256, 512), BF), pltpu.VMEM((2, 128, 512), F32),
            DMA((3, 4)), DMA((3, 4)),
        ],
        compiler_params=params(),
        name="finish",
    )(*grads)
    return enc_grad[None], q_grad[None], w_grad


def solution(mesh):
    placed = (
        P("dp", "seq", None),
        P("dp", "seq", "mp"),
        P("dp", "seq", "mp"),
        P(None, ("dp", "seq"), "mp"),
        P("dp", None),
        P("dp", "seq"),
    )
    return jax.shard_map(
        body,
        mesh=mesh,
        in_specs=placed,
        out_specs=(P("dp", "seq", "mp"), P("dp", "seq", "mp"), P(None, ("dp", "seq"), "mp")),
        check_vma=False,
    )
```

```python
import functools

import jax
import jax.numpy as jnp
from jax import lax
from jax.experimental import pallas as pl
from jax.experimental.pallas import tpu as pltpu
from jax.sharding import PartitionSpec as P

MESH = pl.DeviceIdType.MESH
BF = jnp.bfloat16
F32 = jnp.float32
NEG = -1e30
KB = 256


def coords():
    dp, seq, y = lax.axis_index("dp"), lax.axis_index("seq"), lax.axis_index("mp")
    xh = seq // 8
    return xh * 2 + dp, xh, (seq // 2) % 4, seq % 2, y


def dev(x, z, core, y):
    return (x % 2, (x // 2) * 8 + z * 2 + core, y)


def row_group(x):
    return (x % 2) * 2 + x // 2


def swap(v):
    return (v % 2) * 2 + v // 2


def mod4(v):
    return (v + 4) % 4


def remote(src, dst, send, recv, device):
    return pltpu.make_async_remote_copy(
        src_ref=src, dst_ref=dst, send_sem=send, recv_sem=recv, device_id=device, device_id_type=MESH
    )


def arrived(dst, sem):
    pltpu.make_async_copy(dst, dst, sem).wait()


def greet(peers):
    for peer in peers:
        pl.semaphore_signal(pltpu.get_barrier_semaphore(), inc=1, device_id=peer, device_id_type=MESH)


def greeted(peers):
    pl.semaphore_wait(pltpu.get_barrier_semaphore(), len(peers))


def plane_peers(x, z, c, y, other_cores):
    peers = [dev(x, z, 1 - c, y), dev(mod4(x + 1), z, c, y), dev(mod4(x + 3), z, c, y)]
    for dx, core in [(0, c), (2, c)] + other_cores:
        for dz in range(4):
            if dx or dz:
                peers.append(dev(mod4(x + dx), mod4(z + dz), core, y))
    return peers


def lanes_of(shape):
    return lax.broadcasted_iota(jnp.int32, shape, 1)


def halves(first, second, shift_first, shift_second):
    first = pltpu.roll(first, 64, 1) if shift_first else first
    second = pltpu.roll(second, 64, 1) if shift_second else second
    return jnp.where(lanes_of(first.shape) < 64, first, second)


def front(
    enc, q_in, do_in, w, dseg, eseg,
    wg_out, kvx_out, kvt_out, xt_out, xs_out, spans,
    encv, wg, acc, kvs, kvb, q, do, qs, qb, kvx, kvt, xt, xs,
    loc, save, sib_s, sib_r, ws, wr, qsend, qrecv, ksend, krecv, fsend, frecv,
):
    x, xh, z, c, y = coords()
    me = row_group(x)
    t = xh * 4 + z
    sibling = dev(x, z, 1 - c, y)
    peers = plane_peers(x, z, c, y, [(0, 1 - c), (2, 1 - c)])
    q_in_copy = pltpu.make_async_copy(q_in, q, loc.at[5])
    do_in_copy = pltpu.make_async_copy(do_in, do, loc.at[6])
    q_in_copy.start()
    do_in_copy.start()
    greet(peers)

    own = pl.multiple_of(c * 256, 256)
    other = pl.multiple_of((1 - c) * 256, 256)
    rows = pl.ds(pl.multiple_of(c * 128, 128), 128)
    w_loc = [
        pltpu.make_async_copy(
            w.at[:, :, pl.ds(own + 128 * part, 128)], wg.at[:, part, me, z, rows], loc.at[7 * part]
        )
        for part in range(2)
    ]
    for copy in w_loc:
        copy.start()
    e_loc = pltpu.make_async_copy(enc, encv.at[c], loc.at[1])
    e_loc.start()

    ids = dseg[...].astype(F32)
    row = lax.broadcasted_iota(jnp.int32, (16, 128), 0)
    id_rows = jnp.where(row == 0, ids[0:1], jnp.where(row == 1, ids[1:2], 0.0)).astype(BF)
    q_in_copy.wait()
    do_in_copy.wait()
    for h in range(8):
        tile = pl.ds((h // 2) * 128, 128)
        odd = h % 2 == 1
        qs[h, 0:256, :] = halves(q[:, tile].astype(F32), do[:, tile].astype(F32), odd, not odd).astype(BF)
        qs[h, 256:272, :] = id_rows
    q_loc = pltpu.make_async_copy(qs.at[xh * 4 + swap(z)], qb.at[t], loc.at[2])
    q_loc.start()
    greeted(peers)

    w_sib = [
        remote(
            w.at[:, :, pl.ds(other + 128 * part, 128)], wg.at[:, part, me, z, rows],
            sib_s.at[2 * part], sib_r.at[2 * part], sibling,
        )
        for part in range(2)
    ]
    for copy in w_sib:
        copy.start()
    q_sent = []
    for dxh in (1, 0):
        for dz in (2, 1, 3, 0):
            if dxh == 0 and dz == 0:
                continue
            hx, hz = (xh + dxh) % 2, mod4(z + dz)
            copy = remote(
                qs.at[hx * 4 + swap(hz)], qb.at[t], qsend.at[dxh, dz], qrecv.at[dxh, dz],
                dev(mod4(x + 2 * dxh), hz, c, y),
            )
            copy.start()
            q_sent.append(copy)
    e_sib = remote(enc, encv.at[c], sib_s.at[1], sib_r.at[1], sibling)
    e_sib.start()
    for copy in w_loc + w_sib:
        copy.wait()

    def place(a, first, second):
        bx, bz = (first, second) if a == 0 else (second, first)
        return row_group(mod4(x - bx)), mod4(z - bz)

    def block_of(part, a, first, second, half=None):
        group, bz = place(a, first, second)
        block = wg.at[a, part, group, bz]
        return block if half is None else block.at[pl.ds(half * 128, 128)]

    sent = []

    def pass_on(part, a, first, second, ring, step, half=None):
        block = block_of(part, a, first, second, half)
        to_first, to_second = (first + step) % 4 if ring == 0 else first, (second + step) % 4 if ring else second
        sem = (part, a, to_first, to_second, half or 0)
        along_x = (a == 0) == (ring == 0)
        target = dev(mod4(x + step), z, c, y) if along_x else dev(x, mod4(z + step), c, y)
        copy = remote(block, block, ws.at[sem], wr.at[sem], target)
        copy.start()
        sent.append(copy)

    def take(part, a, first, second):
        if second == 2 or (first == 2 and second == 0):
            for half in range(2):
                arrived(block_of(part, a, first, second, half), wr.at[part, a, first, second, half])
        else:
            arrived(block_of(part, a, first, second), wr.at[part, a, first, second, 0])

    def multiply(part, dx, dz, fresh=False):
        group, bz = place(0, dx, dz)
        columns = pl.ds(pl.multiple_of((group * 4 + bz) * 256, 256), 256)
        both = jnp.concatenate([wg[0, part, group, bz], wg[1, part, group, bz]], axis=1)
        for half in range(2):
            term = jnp.dot(encv[half, :, columns], both, preferred_element_type=F32)
            if fresh:
                acc[part, pl.ds(half * 256, 256), :] = term
            else:
                acc[part, pl.ds(half * 256, 256), :] += term

    def both_ways(part, a, first):
        pass_on(part, a, first, 0, 1, 1)
        pass_on(part, a, first, 0, 1, -1)

    def own_first(part):
        for step in (1, -1):
            for a in range(2):
                pass_on(part, a, 0, 0, 0, step)

    def own_second(part):
        for a in range(2):
            both_ways(part, a, 0)

    def near_first(part):
        for a in range(2):
            take(part, a, 1, 0)
            pass_on(part, a, 1, 0, 0, 1, 0)
            take(part, a, 3, 0)
            pass_on(part, a, 3, 0, 0, -1, 1)
        for a in range(2):
            both_ways(part, a, 1)
            both_ways(part, a, 3)

    def near_second(part, first):
        for a in range(2):
            take(part, a, first, 1)
            pass_on(part, a, first, 1, 1, 1, 0)
            take(part, a, first, 3)
            pass_on(part, a, first, 3, 1, -1, 1)

    def far_first(part):
        for a in range(2):
            take(part, a, 2, 0)
            both_ways(part, a, 2)

    own_first(0)
    own_second(0)
    own_first(1)

    def one_hot(i, _):
        seg = eseg[pl.ds(i, 1), :].astype(F32)
        row = lax.broadcasted_iota(jnp.int32, (128, 128), 0).astype(F32)
        hot = jnp.where(row == seg, 1.0, 0.0)
        kvx[pl.ds(pl.multiple_of(i * 128, 128), 128), 128:256] = hot.T.astype(BF)
        return 0

    lax.fori_loop(0, 32, one_hot, 0)

    near_first(0)
    own_second(1)
    near_second(0, 0)
    near_first(1)
    far_first(0)
    near_second(1, 0)
    far_first(1)
    e_loc.wait()
    e_sib.wait()

    def multiply_near(part):
        multiply(part, 0, 0, True)
        for d in (1, 3):
            multiply(part, d, 0)
            multiply(part, 0, d)

    def multiply_diagonal(part):
        for dx in (1, 3):
            for dz in (1, 3):
                multiply(part, dx, dz)

    multiply_near(0)

    q_loc.wait()
    for dxh in range(2):
        for dz in range(4):
            if dxh or dz:
                src = ((xh + dxh) % 2) * 4 + mod4(z - dz)
                arrived(qb.at[src], qrecv.at[dxh, dz])

    def prepare(b, _):
        block = qb[b, 0:256, :]
        low = lanes_of((256, 128)) < 64
        zero = jnp.zeros_like(block)
        xs[b, 0:256, :] = jnp.where(low, block, zero)
        xs[b, 256:512, :] = jnp.where(low, zero, block)
        turned = block.T
        xt[b, 0:64, 0:256] = turned[0:64] * jnp.asarray(0.125, BF)
        xt[b, 64:128, 256:512] = turned[64:128]
        xt[b, 0:64, 256:512] = jnp.zeros((64, 256), BF)
        xt[b, 64:128, 0:256] = jnp.zeros((64, 256), BF)
        xt[b, 128:256, :] = jnp.zeros((128, 512), BF)
        ids = qb[b, 256:272, :].astype(F32)
        ids = jnp.concatenate([ids[0:1], ids[1:2]], axis=1)
        row = lax.broadcasted_iota(jnp.int32, (16, 256), 0)
        differs = (row < 4) & (row.astype(F32) != ids)
        xt[b, 128:144, 0:256] = jnp.where(differs, NEG, 0.0).astype(BF)
        seg = eseg[...].astype(F32)
        low_id, high_id = jnp.min(ids, axis=1, keepdims=True), jnp.max(ids, axis=1, keepdims=True)
        begin = jnp.sum(jnp.where(seg < low_id, 1.0, 0.0), axis=(0, 1), keepdims=True)
        end = jnp.sum(jnp.where(seg <= high_id, 1.0, 0.0), axis=(0, 1), keepdims=True)
        begin = jnp.floor(begin * (1.0 / 128)) * 128.0
        count = jnp.floor((end - begin + (KB - 1)) * (1.0 / KB))
        begin = jnp.minimum(begin, 4096.0 - count * KB)
        spans[pl.ds(b, 1), :] = jnp.where(lanes_of((1, 128)) == 0, begin, count).astype(jnp.int32)
        return 0

    lax.fori_loop(0, 4, prepare, 0)
    for first in (1, 3, 2):
        near_second(0, first)
    multiply_near(1)
    for first in (1, 3, 2):
        near_second(1, first)
    multiply_diagonal(0)

    ex = (c + 2 - xh) % 2
    tx = c * 2 + x % 2
    here = c == xh

    def kv_copy(head, core):
        rows_of = pl.ds(core * 256, 256)
        return remote(
            kvs.at[head, rows_of], kvb.at[t, rows_of], ksend.at[head, core], krecv.at[ex, z],
            dev(tx, swap(head), core, y),
        )

    def kv_local(core):
        rows_of = pl.ds(core * 256, 256)
        return pltpu.make_async_copy(kvs.at[swap(z), rows_of], kvb.at[t, rows_of], loc.at[4])

    def stays(head, core):
        return jnp.logical_and(here, jnp.logical_and(z == swap(head), c == core))

    def last_part(part):
        for dx, dz in ((2, 0), (0, 2), (1, 2), (3, 2), (2, 1), (2, 3), (2, 2)):
            if dz == 2:
                take(part, 0, dx, dz)
            if dx == 2:
                take(part, 1, dz, dx)
            multiply(part, dx, dz)
        for i in range(2):
            head = 2 * part + i
            keys, values = acc[part, :, 0:128], acc[part, :, 128:256]
            kvs[head] = halves(keys, values, i == 1, i == 0).astype(BF)
            for core in range(2):
                local = stays(head, core)

                @pl.when(local)
                def _():
                    kv_local(core).start()

                @pl.when(jnp.logical_not(local))
                def _():
                    kv_copy(head, core).start()

    last_part(0)
    multiply_diagonal(1)
    last_part(1)
    lax.fori_loop(4, 8, prepare, 0)
    saved = [
        pltpu.make_async_copy(xt, xt_out, save.at[8]),
        pltpu.make_async_copy(xs, xs_out, save.at[9]),
    ]
    for copy in saved:
        copy.start()

    w_save = pltpu.make_async_copy(wg, wg_out, loc.at[3])
    w_save.start()

    mine = pl.ds(pl.multiple_of(c * 256, 256), 256)
    theirs = pl.ds(pl.multiple_of((1 - c) * 256, 256), 256)

    def source(e, dz):
        return ((xh + e) % 2) * 4 + mod4(z - dz)

    f_sent = []

    def hand_over(e, dz):
        src = source(e, dz)
        if e == 0 and dz == 0:

            @pl.when(here)
            def _():
                for core in range(2):

                    @pl.when(c == core)
                    def _():
                        kv_local(core).wait()

            @pl.when(jnp.logical_not(here))
            def _():
                arrived(kvb.at[src, mine], krecv.at[0, z])
        else:
            arrived(kvb.at[src, mine], krecv.at[e, mod4(z - dz)])
        copy = remote(kvb.at[src, mine], kvb.at[src, mine], fsend.at[e, dz], frecv.at[e, dz], sibling)
        copy.start()
        f_sent.append(copy)

    def use(e, dz):
        src = source(e, dz)
        arrived(kvb.at[src, theirs], frecv.at[e, dz])
        block = kvb[src]
        span = pl.ds(pl.multiple_of(src * 512, 512), 512)
        kvx[span, 0:128] = block
        kvt[:, span] = block.T
        for copy in (
            pltpu.make_async_copy(kvx.at[span], kvx_out.at[span], save.at[e * 4 + dz]),
            pltpu.make_async_copy(kvt.at[:, span], kvt_out.at[:, span], save.at[10 + e * 4 + dz]),
        ):
            copy.start()
            saved.append(copy)

    order = [(e, dz) for dz in (0, 1, 3, 2) for e in (0, 1)]
    for i, at in enumerate(order):
        hand_over(*at)
        if i:
            use(*order[i - 1])
    use(*order[-1])

    for copy in sent + q_sent + f_sent:
        copy.wait_send()
    for head in range(4):
        for core in range(2):

            @pl.when(jnp.logical_not(stays(head, core)))
            def _():
                kv_copy(head, core).wait_send()

    w_save.wait()
    for copy in saved:
        copy.wait()


def attend(
    spans, kvx_in, kvt_in, xt_in, xs_in, dkv_res, dq_res,
    kvx, kvt, xt, xs, tt, low_ps, dkv, dkv_out, dq_out, sem, xt_sem, xs_sem, dkv_sem, dq_sem,
):
    kvx_copy = pltpu.make_async_copy(kvx_in, kvx, sem.at[0])
    kvt_copy = pltpu.make_async_copy(kvt_in, kvt, sem.at[1])

    def xt_copy(b):
        return pltpu.make_async_copy(xt_in.at[b], xt.at[b], xt_sem.at[b])

    def xs_copy(b):
        return pltpu.make_async_copy(xs_in.at[b], xs.at[b], xs_sem.at[b])

    xt_copy(0).start()
    kvx_copy.start()
    xs_copy(0).start()
    kvt_copy.start()
    for b in range(1, 8):
        xt_copy(b).start()
        xs_copy(b).start()
    dkv[...] = jnp.zeros_like(dkv)
    kvx_copy.wait()

    def one_block(b, _):
        begin, count = spans[b, 0], spans[b, 1]
        xt_copy(b).wait()

        def sweep(step, carry):
            done = 0
            for blocks in (8, 3, 2, 1):
                times = (count - done) // blocks

                def piece(i, value, done=done, blocks=blocks):
                    first = pl.multiple_of(begin + (done + i * blocks) * KB, 128)
                    return step(first, blocks * KB, value)

                carry = lax.fori_loop(0, times, piece, carry)
                done = done + times * blocks
            return carry

        def fold(op, v):
            return op(v.reshape(v.shape[0] // 8, 8, 256), axis=0)

        def scores(first, length, top):
            rows = pl.ds(first, length)
            both = jnp.dot(kvx[rows, :], xt[b], preferred_element_type=F32)
            tt[rows, :] = both
            return jnp.maximum(top, fold(jnp.max, both[:, 0:256]))

        top = sweep(scores, jnp.full((8, 256), -3e38, F32))
        top = jnp.max(top, axis=0, keepdims=True)

        def weigh(first, length, total):
            rows = pl.ds(first, length)
            e = jnp.exp(tt[rows, 0:256] - top)
            tt[rows, 0:256] = e
            return total + fold(jnp.sum, e)

        total = sweep(weigh, jnp.zeros((8, 256), F32))
        inv = 1.0 / jnp.sum(total, axis=0, keepdims=True)

        def deltas(first, length, delta):
            rows = pl.ds(first, length)
            low_p = (tt[rows, 0:256] * inv).astype(BF)
            low_ps[rows, :] = low_p
            return delta + fold(jnp.sum, low_p.astype(F32) * tt[rows, 256:512])

        delta = sweep(deltas, jnp.zeros((8, 256), F32))
        delta = jnp.sum(delta, axis=0, keepdims=True)
        inv8 = inv * 0.125
        xs_copy(b).wait()

        @pl.when(b == 0)
        def _():
            kvt_copy.wait()

        def grads(first, length, dq):
            for part in range(0, length, KB):
                rows = pl.ds(pl.multiple_of(first + part, 128), KB)
                ds = ((tt[rows, 0:256] * inv8) * (tt[rows, 256:512] - delta)).astype(BF)
                dkv[rows, :] += jnp.dot(ds, xs[b, 0:256], preferred_element_type=F32) + jnp.dot(
                    low_ps[rows, :], xs[b, 256:512], preferred_element_type=F32
                )
                dq = dq + jnp.dot(kvt[0:64, rows], ds, preferred_element_type=F32)
            return dq

        dq = sweep(grads, jnp.zeros((64, 256), F32))
        dq_out[b] = jnp.concatenate([dq[:, 0:128], dq[:, 128:256]], axis=0).T.astype(BF)
        dq_copy(b).start()
        return 0

    def dq_copy(b):
        return pltpu.make_async_copy(dq_out.at[b], dq_res.at[b], dq_sem.at[b])

    lax.fori_loop(0, 8, one_block, 0)
    saved = []
    for t in range(8):
        dkv_out[t] = dkv[pl.ds(t * 512, 512), :].astype(BF)
        saved.append(pltpu.make_async_copy(dkv_out.at[t], dkv_res.at[t], dkv_sem.at[t]))
        saved[t].start()
    for t in range(8):
        saved[t].wait()
        dq_copy(t).wait()


def back(
    dkvp, dqp, enc, w,
    enc_res, q_res, w_res,
    enc_out, q_out, encv, wv, po, pb, ps, rb, gt, gs, qg, cs, cr, ms, mr, keep, fin, fsib, ycs, ycr, yms, ymr,
    loc, sib_s, sib_r, dsend, drecv, qsend, qrecv, csend, crecv, msend, mrecv, ysend, yrecv,
):
    x, xh, z, c, y = coords()
    sibling = dev(x, z, 1 - c, y)
    peers = [dev(x, z, c, mod4(y + 1)), dev(x, z, c, mod4(y + 3))]
    peers += plane_peers(x, z, c, y, [(2, 1 - c)])
    greet(peers)
    p_loc = pltpu.make_async_copy(dkvp.at[pl.ds(c * 4, 4)], po, loc.at[0])
    p_loc.start()
    e_loc = pltpu.make_async_copy(enc, encv.at[c], loc.at[1])
    e_loc.start()
    w_loc = pltpu.make_async_copy(w, wv.at[c], loc.at[2])
    w_loc.start()
    q_loc = pltpu.make_async_copy(dqp.at[xh * 4 + z], qg.at[xh * 4 + swap(z)], loc.at[3])
    q_loc.start()
    greeted(peers)

    here = c == xh
    p_sib = remote(dkvp.at[pl.ds((1 - c) * 4, 4)], pb, sib_s.at[0], sib_r.at[0], sibling)
    p_sib.start()
    e_sib = remote(enc, encv.at[c], sib_s.at[1], sib_r.at[1], sibling)
    e_sib.start()
    w_sib = remote(w, wv.at[c], sib_s.at[2], sib_r.at[2], sibling)
    w_sib.start()

    def d_copy(dz):
        tz = mod4(z + dz)
        return remote(ps.at[tz], rb.at[z], dsend.at[dz], drecv.at[dz], dev(c * 2 + x % 2, tz, xh, y))

    p_loc.wait()
    p_sib.wait()
    for dz in (2, 1, 3, 0):
        tz = mod4(z + dz)
        ps[tz] = (po[tz].astype(F32) + pb[tz].astype(F32)).astype(BF)
        if dz:
            d_copy(dz).start()
    d_loc = pltpu.make_async_copy(ps.at[z], rb.at[z], loc.at[4])

    @pl.when(here)
    def _():
        d_loc.start()

    @pl.when(jnp.logical_not(here))
    def _():
        d_copy(0).start()

    q_sent = []
    for dxh in (1, 0):
        for dz in (2, 1, 3, 0):
            if dxh or dz:
                tx, tz = (xh + dxh) % 2, mod4(z + dz)
                copy = remote(
                    dqp.at[tx * 4 + tz], qg.at[xh * 4 + swap(z)], qsend.at[dxh, dz], qrecv.at[dxh, dz],
                    dev(tx * 2 + x % 2, tz, c, y),
                )
                copy.start()
                q_sent.append(copy)

    for dz in (0, 1, 3, 2):
        j = mod4(z - dz)
        if dz == 0:

            @pl.when(here)
            def _():
                d_loc.wait()

            @pl.when(jnp.logical_not(here))
            def _():
                arrived(rb.at[j], drecv.at[0])
        else:
            arrived(rb.at[j], drecv.at[dz])
        turned = rb[j].T
        keys = pl.ds(pl.multiple_of(swap(j) * 64, 64), 64)
        gt[0, keys, :] = turned[0:64]
        gt[1, keys, :] = turned[64:128]

    own_tok = pl.ds(pl.multiple_of(c * 256, 256), 256)
    sib_tok = pl.ds(pl.multiple_of((1 - c) * 256, 256), 256)
    g_sib = remote(gt.at[:, :, sib_tok], gs.at[c], sib_s.at[3], sib_r.at[3], sibling)
    g_sib.start()
    gs_own = pltpu.make_async_copy(gt.at[:, :, own_tok], gs.at[c], loc.at[5])
    gs_own.start()
    e_loc.wait()
    e_sib.wait()

    def product(a, first, second):
        bx, bz = (second, first) if a == 0 else (first, second)
        columns = pl.ds(pl.multiple_of((row_group(mod4(x + bx)) * 4 + mod4(z + bz)) * 256, 256), 256)
        return jnp.dot(gt[a, :, 0:256], encv[0, :, columns], preferred_element_type=F32) + jnp.dot(
            gt[a, :, 256:512], encv[1, :, columns], preferred_element_type=F32
        )

    sent = []

    def neighbour(a, ring, step):
        along_x = (a == 1) == (ring == 0)
        return dev(mod4(x + step), z, c, y) if along_x else dev(x, mod4(z + step), c, y)

    def send_far(a, slot, ring, value):
        for half in range(2):
            cs[a, slot, half] = value[half * 128 : half * 128 + 128].astype(BF)
            at = (a, slot, half)
            copy = remote(cs.at[at], cr.at[at], csend.at[at], crecv.at[at], neighbour(a, ring, 1 - 2 * half))
            copy.start()
            sent.append(copy)

    def send_near(a, slot, ring, values):
        for half in range(2):
            value = values[half]()
            at = (a, slot, half)
            arrived(cr.at[at], crecv.at[at])
            keep_half = pl.ds(half * 128, 128)
            rest = slice(128, 256) if half == 0 else slice(0, 128)
            this = slice(0, 128) if half == 0 else slice(128, 256)
            ms[a, slot, half, pl.ds((1 - half) * 128, 128), :] = value[rest].astype(BF)
            ms[a, slot, half, keep_half, :] = (value[this] + cr[a, slot, half].astype(F32)).astype(BF)
            copy = remote(ms.at[at], mr.at[at], msend.at[at], mrecv.at[at], neighbour(a, ring, 1 - 2 * half))
            copy.start()
            sent.append(copy)

    def collect(a, slot, value):
        for half in range(2):
            at = (a, slot, half)
            arrived(mr.at[at], mrecv.at[at])
            value = value + mr[a, slot, half].astype(F32)
        return value

    def far(slot):
        for a in range(2):
            send_far(a, slot, 0, product(a, 2, slot))

    def near(slot):
        for a in range(2):
            send_near(a, slot, 0, [lambda a=a: product(a, 1, slot), lambda a=a: product(a, 3, slot)])

    def ahead(slot):
        for a in range(2):
            keep[a, slot] = product(a, 0, slot)

    def enc_rows(dy, r):
        group = mod4(y + dy)
        total = None
        for half in range(2):
            for a in range(2):
                weights = jnp.concatenate([wv[half, a, 0, group, r], wv[half, a, 1, group, r]], axis=1)
                term = jnp.dot(weights, gs[half, a], preferred_element_type=F32)
                total = term if total is None else total + term
        return total

    def y_send(src, dst, i, step):
        copy = remote(src, dst, ysend.at[i], yrecv.at[i], dev(x, z, c, mod4(y + step)))
        copy.start()
        sent.append(copy)

    def y_far():
        for half in range(2):
            for r in range(2):
                ycs[half, r] = enc_rows(2, 2 * half + r).astype(BF)
            y_send(ycs.at[half], ycr.at[half], half, 1 - 2 * half)

    def y_free():
        for half in range(2):
            for r in range(2):
                yms[half, 1 - half, r] = enc_rows(1 + 2 * half, 2 * (1 - half) + r).astype(BF)
            y_send(yms.at[half, 1 - half], ymr.at[half, 1 - half], 2 + half, 1 - 2 * half)

    def y_near():
        for half in range(2):
            for r in range(2):
                value = enc_rows(1 + 2 * half, 2 * half + r)
                if r == 0:
                    arrived(ycr.at[half], yrecv.at[half])
                yms[half, half, r] = (value + ycr[half, r].astype(F32)).astype(BF)
            y_send(yms.at[half, half], ymr.at[half, half], 4 + half, 1 - 2 * half)

    far(2)
    gs_own.wait()
    g_sib.wait()
    w_loc.wait()
    w_sib.wait()
    y_far()
    far(1)
    near(2)
    y_free()
    far(3)
    near(1)
    ahead(2)
    far(0)
    near(3)
    y_near()
    for a in range(2):
        send_far(a, 4, 1, collect(a, 2, keep[a, 2]))
    near(0)
    ahead(1)
    ahead(3)
    ahead(0)

    q_loc.wait()
    for dxh in range(2):
        for dz in range(4):
            if dxh or dz:
                src = ((xh + dxh) % 2) * 4 + swap(mod4(z - dz))
                arrived(qg.at[src], qrecv.at[dxh, dz])
    for i in range(4):
        tile = pl.ds(i * 128, 128)
        even, odd = qg[2 * i].astype(F32), qg[2 * i + 1].astype(F32)
        q_out[0:128, tile] = halves(even, odd, False, True).astype(BF)
        q_out[128:256, tile] = halves(even, odd, True, False).astype(BF)
    q_save = pltpu.make_async_copy(q_out, q_res, loc.at[6])
    q_save.start()

    for a in range(2):
        for slot in (1, 3):
            keep[a, slot] = collect(a, slot, keep[a, slot])
    for a in range(2):
        send_near(a, 4, 1, [lambda a=a: keep[a, 1], lambda a=a: keep[a, 3]])

    for r in range(4):
        total = enc_rows(0, r).astype(BF).astype(F32)
        for half in range(2):
            if r == 0:
                arrived(ymr.at[half, 1 - half], yrecv.at[2 + half])
                arrived(ymr.at[half, half], yrecv.at[4 + half])
            total = total + ymr[half, r // 2, r % 2].astype(F32)
        enc_out[:, pl.ds(r * 256, 256)] = total.T.astype(BF)
    enc_save = pltpu.make_async_copy(enc_out, enc_res, loc.at[7])
    enc_save.start()

    for a in range(2):
        fin[a] = collect(a, 4, collect(a, 0, keep[a, 0])).T
    mine = pl.ds(pl.multiple_of(c * 128, 128), 128)
    theirs = pl.ds(pl.multiple_of((1 - c) * 128, 128), 128)
    f_sib = remote(fin.at[:, theirs], fsib, sib_s.at[4], sib_r.at[4], sibling)
    f_sib.start()
    w_own = pltpu.make_async_copy(
        fin.at[:, mine], w_res.at[:, :, pl.ds(pl.multiple_of(c * 256, 256), 256)], loc.at[8]
    )
    w_own.start()
    f_sib.wait()
    w_other = pltpu.make_async_copy(
        fsib, w_res.at[:, :, pl.ds(pl.multiple_of((1 - c) * 256, 256), 256)], loc.at[9]
    )
    w_other.start()
    for copy in q_sent + sent + [d_copy(dz) for dz in (1, 2, 3)]:
        copy.wait_send()

    @pl.when(jnp.logical_not(here))
    def _():
        d_copy(0).wait_send()

    for copy in (enc_save, q_save, w_own, w_other):
        copy.wait()


def finish(*refs):
    given, results, held, (load, store) = refs[0:3], refs[3:6], refs[6:9], refs[9:11]
    parts = []
    for i in range(3):
        rows = given[i].shape[-2] // 4
        for k in range(4):
            at = (slice(None),) * (len(given[i].shape) - 2) + (pl.ds(k * rows, rows),)
            parts.append(
                (
                    pltpu.make_async_copy(given[i].at[at], held[i].at[at], load.at[i, k]),
                    pltpu.make_async_copy(held[i].at[at], results[i].at[at], store.at[i, k]),
                )
            )
    for first, _ in parts:
        first.start()
    for first, second in parts:
        first.wait()
        second.start()
    for _, second in parts:
        second.wait()


VM = pl.BlockSpec(memory_space=pltpu.VMEM)
ANY = pl.BlockSpec(memory_space=pl.ANY)
DMA = pltpu.SemaphoreType.DMA


def params(collective_id=None):
    if collective_id is None:
        return pltpu.CompilerParams(vmem_limit_bytes=60 << 20)
    return pltpu.CompilerParams(
        collective_id=collective_id, has_side_effects=True, vmem_limit_bytes=60 << 20
    )


def body(enc_out, dec_query, ctx_grad, kv_weight, enc_seg, dec_seg):
    enc = enc_out[0]
    eseg = enc_seg.reshape(32, 128)
    dseg = dec_seg.reshape(2, 128)
    shape = jax.ShapeDtypeStruct
    wg, kvx, kvt, xt, xs, spans = pl.pallas_call(
        front,
        out_shape=(
            shape((2, 2, 4, 4, 256, 128), BF),
            shape((4096, 256), BF),
            shape((128, 4096), BF),
            shape((8, 256, 512), BF),
            shape((8, 512, 128), BF),
            shape((8, 128), jnp.int32),
        ),
        in_specs=[ANY, ANY, ANY, ANY, VM, VM],
        out_specs=(ANY, ANY, ANY, ANY, ANY, VM),
        scratch_shapes=[
            pltpu.VMEM((2, 256, 4096), BF),
            pltpu.VMEM((2, 2, 4, 4, 256, 128), BF),
            pltpu.VMEM((2, 512, 256), F32),
            pltpu.VMEM((4, 512, 128), BF),
            pltpu.VMEM((8, 512, 128), BF),
            pltpu.VMEM((256, 512), BF),
            pltpu.VMEM((256, 512), BF),
            pltpu.VMEM((8, 272, 128), BF),
            pltpu.VMEM((8, 272, 128), BF),
            pltpu.VMEM((4096, 256), BF),
            pltpu.VMEM((128, 4096), BF),
            pltpu.VMEM((8, 256, 512), BF),
            pltpu.VMEM((8, 512, 128), BF),
            DMA((8,)), DMA((18,)), DMA((3,)), DMA((3,)),
            DMA((2, 2, 4, 4, 2)), DMA((2, 2, 4, 4, 2)),
            DMA((2, 4)), DMA((2, 4)),
            DMA((4, 2)), DMA((2, 4)),
            DMA((2, 4)), DMA((2, 4)),
        ],
        compiler_params=params(1),
        name="front",
    )(enc, dec_query[0], ctx_grad[0], kv_weight, dseg, eseg)

    dkvp, dqp = pl.pallas_call(
        attend,
        out_shape=(shape((8, 512, 128), BF), shape((8, 128, 128), BF)),
        in_specs=[pl.BlockSpec(memory_space=pltpu.SMEM), ANY, ANY, ANY, ANY],
        out_specs=(ANY, ANY),
        scratch_shapes=[
            pltpu.VMEM((4096, 256), BF),
            pltpu.VMEM((128, 4096), BF),
            pltpu.VMEM((8, 256, 512), BF),
            pltpu.VMEM((8, 512, 128), BF),
            pltpu.VMEM((4096, 512), F32),
            pltpu.VMEM((4096, 256), BF),
            pltpu.VMEM((4096, 128), F32),
            pltpu.VMEM((8, 512, 128), BF),
            pltpu.VMEM((8, 128, 128), BF),
            DMA((2,)), DMA((8,)), DMA((8,)), DMA((8,)), DMA((8,)),
        ],
        compiler_params=params(),
        name="attend",
    )(spans, kvx, kvt, xt, xs)

    grads = pl.pallas_call(
        back,
        out_shape=(shape((256, 1024), BF), shape((256, 512), BF), shape((2, 128, 512), F32)),
        in_specs=[ANY, ANY, ANY, ANY],
        out_specs=(ANY, ANY, ANY),
        scratch_shapes=[
            pltpu.VMEM((256, 1024), BF),
            pltpu.VMEM((256, 512), BF),
            pltpu.VMEM((2, 256, 4096), BF),
            pltpu.VMEM((2, 2, 2, 4, 4, 256, 128), BF),
            pltpu.VMEM((4, 512, 128), BF),
            pltpu.VMEM((4, 512, 128), BF),
            pltpu.VMEM((4, 512, 128), BF),
            pltpu.VMEM((4, 512, 128), BF),
            pltpu.VMEM((2, 256, 512), BF),
            pltpu.VMEM((2, 2, 256, 256), BF),
            pltpu.VMEM((8, 128, 128), BF),
            pltpu.VMEM((2, 5, 2, 128, 256), BF),
            pltpu.VMEM((2, 5, 2, 128, 256), BF),
            pltpu.VMEM((2, 5, 2, 256, 256), BF),
            pltpu.VMEM((2, 5, 2, 256, 256), BF),
            pltpu.VMEM((2, 4, 256, 256), F32),
            pltpu.VMEM((2, 256, 256), F32),
            pltpu.VMEM((2, 128, 256), F32),
            pltpu.VMEM((2, 2, 256, 256), BF),
            pltpu.VMEM((2, 2, 256, 256), BF),
            pltpu.VMEM((2, 2, 2, 256, 256), BF),
            pltpu.VMEM((2, 2, 2, 256, 256), BF),
            DMA((10,)), DMA((5,)), DMA((5,)),
            DMA((4,)), DMA((4,)),
            DMA((2, 4)), DMA((2, 4)),
            DMA((2, 5, 2)), DMA((2, 5, 2)),
            DMA((2, 5, 2)), DMA((2, 5, 2)),
            DMA((6,)), DMA((6,)),
        ],
        compiler_params=params(2),
        name="back",
    )(dkvp, dqp, enc, wg)

    enc_grad, q_grad, w_grad = pl.pallas_call(
        finish,
        out_shape=(shape((256, 1024), BF), shape((256, 512), BF), shape((2, 128, 512), F32)),
        in_specs=[ANY] * 3,
        out_specs=(ANY, ANY, ANY),
        scratch_shapes=[
            pltpu.VMEM((256, 1024), BF), pltpu.VMEM((256, 512), BF), pltpu.VMEM((2, 128, 512), F32),
            DMA((3, 4)), DMA((3, 4)),
        ],
        compiler_params=params(),
        name="finish",
    )(*grads)
    return enc_grad[None], q_grad[None], w_grad


def solution(mesh):
    placed = (
        P("dp", "seq", None),
        P("dp", "seq", "mp"),
        P("dp", "seq", "mp"),
        P(None, ("dp", "seq"), "mp"),
        P("dp", None),
        P("dp", "seq"),
    )
    return jax.shard_map(
        body,
        mesh=mesh,
        in_specs=placed,
        out_specs=(P("dp", "seq", "mp"), P("dp", "seq", "mp"), P(None, ("dp", "seq"), "mp")),
        check_vma=False,
    )
```

```python
import functools

import jax
import jax.numpy as jnp
from jax import lax
from jax.experimental import pallas as pl
from jax.experimental.pallas import tpu as pltpu
from jax.sharding import PartitionSpec as P

MESH = pl.DeviceIdType.MESH
BF = jnp.bfloat16
F32 = jnp.float32
NEG = -1e30
KB = 256


def coords():
    dp, seq, y = lax.axis_index("dp"), lax.axis_index("seq"), lax.axis_index("mp")
    xh = seq // 8
    return xh * 2 + dp, xh, (seq // 2) % 4, seq % 2, y


def dev(x, z, core, y):
    return (x % 2, (x // 2) * 8 + z * 2 + core, y)


def row_group(x):
    return (x % 2) * 2 + x // 2


def swap(v):
    return (v % 2) * 2 + v // 2


def mod4(v):
    return (v + 4) % 4


def remote(src, dst, send, recv, device):
    return pltpu.make_async_remote_copy(
        src_ref=src, dst_ref=dst, send_sem=send, recv_sem=recv, device_id=device, device_id_type=MESH
    )


def arrived(dst, sem):
    pltpu.make_async_copy(dst, dst, sem).wait()


def greet(peers):
    for peer in peers:
        pl.semaphore_signal(pltpu.get_barrier_semaphore(), inc=1, device_id=peer, device_id_type=MESH)


def greeted(peers):
    pl.semaphore_wait(pltpu.get_barrier_semaphore(), len(peers))


def plane_peers(x, z, c, y, other_cores):
    peers = [dev(x, z, 1 - c, y), dev(mod4(x + 1), z, c, y), dev(mod4(x + 3), z, c, y)]
    for dx, core in [(0, c), (2, c)] + other_cores:
        for dz in range(4):
            if dx or dz:
                peers.append(dev(mod4(x + dx), mod4(z + dz), core, y))
    return peers


def lanes_of(shape):
    return lax.broadcasted_iota(jnp.int32, shape, 1)


def halves(first, second, shift_first, shift_second):
    first = pltpu.roll(first, 64, 1) if shift_first else first
    second = pltpu.roll(second, 64, 1) if shift_second else second
    return jnp.where(lanes_of(first.shape) < 64, first, second)


def front(
    enc, q_in, do_in, w, dseg_in, eseg_in,
    wg_out, kvx_out, kvt_out, xt_out, xs_out, spans_out,
    encv, wg, acc, kvs, kvb, q, do, dseg, eseg, qs, qb, kvx, kvt, xt, xs, spans,
    loc, save, sib_s, sib_r, ws, wr, qsend, qrecv, ksend, krecv, fsend, frecv,
):
    x, xh, z, c, y = coords()
    me = row_group(x)
    t = xh * 4 + z
    sibling = dev(x, z, 1 - c, y)
    peers = plane_peers(x, z, c, y, [(0, 1 - c), (2, 1 - c)])
    q_in_copy = pltpu.make_async_copy(q_in, q, loc.at[5])
    do_in_copy = pltpu.make_async_copy(do_in, do, loc.at[6])
    dseg_copy = pltpu.make_async_copy(dseg_in, dseg, loc.at[8])
    eseg_copy = pltpu.make_async_copy(eseg_in, eseg, loc.at[9])
    for copy in (q_in_copy, do_in_copy, dseg_copy, eseg_copy):
        copy.start()
    greet(peers)

    own = pl.multiple_of(c * 256, 256)
    other = pl.multiple_of((1 - c) * 256, 256)
    rows = pl.ds(pl.multiple_of(c * 128, 128), 128)
    w_loc = [
        pltpu.make_async_copy(
            w.at[:, :, pl.ds(own + 128 * part, 128)], wg.at[:, part, me, z, rows], loc.at[7 * part]
        )
        for part in range(2)
    ]
    for copy in w_loc:
        copy.start()
    e_loc = pltpu.make_async_copy(enc, encv.at[c], loc.at[1])
    e_loc.start()

    dseg_copy.wait()
    eseg_copy.wait()
    ids = dseg[...].astype(F32)
    row = lax.broadcasted_iota(jnp.int32, (16, 128), 0)
    id_rows = jnp.where(row == 0, ids[0:1], jnp.where(row == 1, ids[1:2], 0.0)).astype(BF)
    q_in_copy.wait()
    do_in_copy.wait()
    for h in range(8):
        tile = pl.ds((h // 2) * 128, 128)
        odd = h % 2 == 1
        qs[h, 0:256, :] = halves(q[:, tile].astype(F32), do[:, tile].astype(F32), odd, not odd).astype(BF)
        qs[h, 256:272, :] = id_rows
    q_loc = pltpu.make_async_copy(qs.at[xh * 4 + swap(z)], qb.at[t], loc.at[2])
    q_loc.start()
    greeted(peers)

    w_sib = [
        remote(
            w.at[:, :, pl.ds(other + 128 * part, 128)], wg.at[:, part, me, z, rows],
            sib_s.at[2 * part], sib_r.at[2 * part], sibling,
        )
        for part in range(2)
    ]
    for copy in w_sib:
        copy.start()
    q_sent = []
    for dxh in (1, 0):
        for dz in (2, 1, 3, 0):
            if dxh == 0 and dz == 0:
                continue
            hx, hz = (xh + dxh) % 2, mod4(z + dz)
            copy = remote(
                qs.at[hx * 4 + swap(hz)], qb.at[t], qsend.at[dxh, dz], qrecv.at[dxh, dz],
                dev(mod4(x + 2 * dxh), hz, c, y),
            )
            copy.start()
            q_sent.append(copy)
    e_sib = remote(enc, encv.at[c], sib_s.at[1], sib_r.at[1], sibling)
    e_sib.start()
    for copy in w_loc + w_sib:
        copy.wait()

    def place(a, first, second):
        bx, bz = (first, second) if a == 0 else (second, first)
        return row_group(mod4(x - bx)), mod4(z - bz)

    def block_of(part, a, first, second, half=None):
        group, bz = place(a, first, second)
        block = wg.at[a, part, group, bz]
        return block if half is None else block.at[pl.ds(half * 128, 128)]

    sent = []

    def pass_on(part, a, first, second, ring, step, half=None):
        block = block_of(part, a, first, second, half)
        to_first, to_second = (first + step) % 4 if ring == 0 else first, (second + step) % 4 if ring else second
        sem = (part, a, to_first, to_second, half or 0)
        along_x = (a == 0) == (ring == 0)
        target = dev(mod4(x + step), z, c, y) if along_x else dev(x, mod4(z + step), c, y)
        copy = remote(block, block, ws.at[sem], wr.at[sem], target)
        copy.start()
        sent.append(copy)

    def take(part, a, first, second):
        if second == 2 or (first == 2 and second == 0):
            for half in range(2):
                arrived(block_of(part, a, first, second, half), wr.at[part, a, first, second, half])
        else:
            arrived(block_of(part, a, first, second), wr.at[part, a, first, second, 0])

    def multiply(part, dx, dz, fresh=False):
        group, bz = place(0, dx, dz)
        columns = pl.ds(pl.multiple_of((group * 4 + bz) * 256, 256), 256)
        both = jnp.concatenate([wg[0, part, group, bz], wg[1, part, group, bz]], axis=1)
        for half in range(2):
            term = jnp.dot(encv[half, :, columns], both, preferred_element_type=F32)
            if fresh:
                acc[part, pl.ds(half * 256, 256), :] = term
            else:
                acc[part, pl.ds(half * 256, 256), :] += term

    def both_ways(part, a, first):
        pass_on(part, a, first, 0, 1, 1)
        pass_on(part, a, first, 0, 1, -1)

    def own_first(part):
        for step in (1, -1):
            for a in range(2):
                pass_on(part, a, 0, 0, 0, step)

    def own_second(part):
        for a in range(2):
            both_ways(part, a, 0)

    def near_first(part):
        for a in range(2):
            take(part, a, 1, 0)
            pass_on(part, a, 1, 0, 0, 1, 0)
            take(part, a, 3, 0)
            pass_on(part, a, 3, 0, 0, -1, 1)
        for a in range(2):
            both_ways(part, a, 1)
            both_ways(part, a, 3)

    def near_second(part, first):
        for a in range(2):
            take(part, a, first, 1)
            pass_on(part, a, first, 1, 1, 1, 0)
            take(part, a, first, 3)
            pass_on(part, a, first, 3, 1, -1, 1)

    def far_first(part):
        for a in range(2):
            take(part, a, 2, 0)
            both_ways(part, a, 2)

    own_first(0)
    own_second(0)
    own_first(1)

    def one_hot(i, _):
        seg = eseg[pl.ds(i, 1), :].astype(F32)
        row = lax.broadcasted_iota(jnp.int32, (128, 128), 0).astype(F32)
        hot = jnp.where(row == seg, 1.0, 0.0)
        kvx[pl.ds(pl.multiple_of(i * 128, 128), 128), 128:256] = hot.T.astype(BF)
        return 0

    lax.fori_loop(0, 32, one_hot, 0)

    near_first(0)
    own_second(1)
    near_second(0, 0)
    near_first(1)
    far_first(0)
    near_second(1, 0)
    far_first(1)
    e_loc.wait()
    e_sib.wait()

    def multiply_near(part):
        multiply(part, 0, 0, True)
        for d in (1, 3):
            multiply(part, d, 0)
            multiply(part, 0, d)

    def multiply_diagonal(part):
        for dx in (1, 3):
            for dz in (1, 3):
                multiply(part, dx, dz)

    multiply_near(0)

    q_loc.wait()
    for dxh in range(2):
        for dz in range(4):
            if dxh or dz:
                src = ((xh + dxh) % 2) * 4 + mod4(z - dz)
                arrived(qb.at[src], qrecv.at[dxh, dz])

    def prepare(b, _):
        block = qb[b, 0:256, :]
        low = lanes_of((256, 128)) < 64
        zero = jnp.zeros_like(block)
        xs[b, 0:256, :] = jnp.where(low, block, zero)
        xs[b, 256:512, :] = jnp.where(low, zero, block)
        turned = block.T
        xt[b, 0:64, 0:256] = turned[0:64] * jnp.asarray(0.125, BF)
        xt[b, 64:128, 256:512] = turned[64:128]
        xt[b, 0:64, 256:512] = jnp.zeros((64, 256), BF)
        xt[b, 64:128, 0:256] = jnp.zeros((64, 256), BF)
        xt[b, 128:256, :] = jnp.zeros((128, 512), BF)
        ids = qb[b, 256:272, :].astype(F32)
        ids = jnp.concatenate([ids[0:1], ids[1:2]], axis=1)
        row = lax.broadcasted_iota(jnp.int32, (16, 256), 0)
        differs = (row < 4) & (row.astype(F32) != ids)
        xt[b, 128:144, 0:256] = jnp.where(differs, NEG, 0.0).astype(BF)
        seg = eseg[...].astype(F32)
        low_id, high_id = jnp.min(ids, axis=1, keepdims=True), jnp.max(ids, axis=1, keepdims=True)
        begin = jnp.sum(jnp.where(seg < low_id, 1.0, 0.0), axis=(0, 1), keepdims=True)
        end = jnp.sum(jnp.where(seg <= high_id, 1.0, 0.0), axis=(0, 1), keepdims=True)
        begin = jnp.floor(begin * (1.0 / 128)) * 128.0
        count = jnp.floor((end - begin + (KB - 1)) * (1.0 / KB))
        begin = jnp.minimum(begin, 4096.0 - count * KB)
        spans[pl.ds(b, 1), :] = jnp.where(lanes_of((1, 128)) == 0, begin, count).astype(jnp.int32)
        return 0

    lax.fori_loop(0, 4, prepare, 0)
    for first in (1, 3, 2):
        near_second(0, first)
    multiply_near(1)
    for first in (1, 3, 2):
        near_second(1, first)
    multiply_diagonal(0)

    ex = (c + 2 - xh) % 2
    tx = c * 2 + x % 2
    here = c == xh

    def kv_copy(head, core):
        rows_of = pl.ds(core * 256, 256)
        return remote(
            kvs.at[head, rows_of], kvb.at[t, rows_of], ksend.at[head, core], krecv.at[ex, z],
            dev(tx, swap(head), core, y),
        )

    def kv_local(core):
        rows_of = pl.ds(core * 256, 256)
        return pltpu.make_async_copy(kvs.at[swap(z), rows_of], kvb.at[t, rows_of], loc.at[4])

    def stays(head, core):
        return jnp.logical_and(here, jnp.logical_and(z == swap(head), c == core))

    def last_part(part):
        for dx, dz in ((2, 0), (0, 2), (1, 2), (3, 2), (2, 1), (2, 3), (2, 2)):
            if dz == 2:
                take(part, 0, dx, dz)
            if dx == 2:
                take(part, 1, dz, dx)
            multiply(part, dx, dz)
        for i in range(2):
            head = 2 * part + i
            keys, values = acc[part, :, 0:128], acc[part, :, 128:256]
            kvs[head] = halves(keys, values, i == 1, i == 0).astype(BF)
            for core in range(2):
                local = stays(head, core)

                @pl.when(local)
                def _():
                    kv_local(core).start()

                @pl.when(jnp.logical_not(local))
                def _():
                    kv_copy(head, core).start()

    last_part(0)
    multiply_diagonal(1)
    last_part(1)
    lax.fori_loop(4, 8, prepare, 0)
    saved = [
        pltpu.make_async_copy(xt, xt_out, save.at[8]),
        pltpu.make_async_copy(xs, xs_out, save.at[9]),
        pltpu.make_async_copy(spans, spans_out, save.at[18]),
    ]
    for copy in saved:
        copy.start()

    w_save = pltpu.make_async_copy(wg, wg_out, loc.at[3])
    w_save.start()

    mine = pl.ds(pl.multiple_of(c * 256, 256), 256)
    theirs = pl.ds(pl.multiple_of((1 - c) * 256, 256), 256)

    def source(e, dz):
        return ((xh + e) % 2) * 4 + mod4(z - dz)

    f_sent = []

    def hand_over(e, dz):
        src = source(e, dz)
        if e == 0 and dz == 0:

            @pl.when(here)
            def _():
                for core in range(2):

                    @pl.when(c == core)
                    def _():
                        kv_local(core).wait()

            @pl.when(jnp.logical_not(here))
            def _():
                arrived(kvb.at[src, mine], krecv.at[0, z])
        else:
            arrived(kvb.at[src, mine], krecv.at[e, mod4(z - dz)])
        copy = remote(kvb.at[src, mine], kvb.at[src, mine], fsend.at[e, dz], frecv.at[e, dz], sibling)
        copy.start()
        f_sent.append(copy)

    def use(e, dz):
        src = source(e, dz)
        arrived(kvb.at[src, theirs], frecv.at[e, dz])
        block = kvb[src]
        span = pl.ds(pl.multiple_of(src * 512, 512), 512)
        kvx[span, 0:128] = block
        kvt[:, span] = block.T
        for copy in (
            pltpu.make_async_copy(kvx.at[span], kvx_out.at[span], save.at[e * 4 + dz]),
            pltpu.make_async_copy(kvt.at[:, span], kvt_out.at[:, span], save.at[10 + e * 4 + dz]),
        ):
            copy.start()
            saved.append(copy)

    order = [(e, dz) for dz in (0, 1, 3, 2) for e in (0, 1)]
    for i, at in enumerate(order):
        hand_over(*at)
        if i:
            use(*order[i - 1])
    use(*order[-1])

    for copy in sent + q_sent + f_sent:
        copy.wait_send()
    for head in range(4):
        for core in range(2):

            @pl.when(jnp.logical_not(stays(head, core)))
            def _():
                kv_copy(head, core).wait_send()

    w_save.wait()
    for copy in saved:
        copy.wait()


def attend(
    spans_in, kvx_in, kvt_in, xt_in, xs_in, dkv_res, dq_res,
    spans, kvx, kvt, xt, xs, tt, low_ps, dkv, dkv_out, dq_out, sem, xt_sem, xs_sem, dkv_sem, dq_sem,
):
    kvx_copy = pltpu.make_async_copy(kvx_in, kvx, sem.at[0])
    kvt_copy = pltpu.make_async_copy(kvt_in, kvt, sem.at[1])

    def xt_copy(b):
        return pltpu.make_async_copy(xt_in.at[b], xt.at[b], xt_sem.at[b])

    def xs_copy(b):
        return pltpu.make_async_copy(xs_in.at[b], xs.at[b], xs_sem.at[b])

    spans_copy = pltpu.make_async_copy(spans_in, spans, sem.at[2])
    spans_copy.start()
    xt_copy(0).start()
    kvx_copy.start()
    xs_copy(0).start()
    kvt_copy.start()
    for b in range(1, 8):
        xt_copy(b).start()
        xs_copy(b).start()
    dkv[...] = jnp.zeros_like(dkv)
    spans_copy.wait()
    kvx_copy.wait()

    def one_block(b, _):
        begin, count = spans[b, 0], spans[b, 1]
        xt_copy(b).wait()

        def sweep(step, carry):
            done = 0
            for blocks in (8, 3, 2, 1):
                times = (count - done) // blocks

                def piece(i, value, done=done, blocks=blocks):
                    first = pl.multiple_of(begin + (done + i * blocks) * KB, 128)
                    return step(first, blocks * KB, value)

                carry = lax.fori_loop(0, times, piece, carry)
                done = done + times * blocks
            return carry

        def fold(op, v):
            return op(v.reshape(v.shape[0] // 8, 8, 256), axis=0)

        def scores(first, length, top):
            rows = pl.ds(first, length)
            both = jnp.dot(kvx[rows, :], xt[b], preferred_element_type=F32)
            tt[rows, :] = both
            return jnp.maximum(top, fold(jnp.max, both[:, 0:256]))

        top = sweep(scores, jnp.full((8, 256), -3e38, F32))
        top = jnp.max(top, axis=0, keepdims=True)

        def weigh(first, length, total):
            rows = pl.ds(first, length)
            e = jnp.exp(tt[rows, 0:256] - top)
            tt[rows, 0:256] = e
            return total + fold(jnp.sum, e)

        total = sweep(weigh, jnp.zeros((8, 256), F32))
        inv = 1.0 / jnp.sum(total, axis=0, keepdims=True)

        def deltas(first, length, delta):
            rows = pl.ds(first, length)
            low_p = (tt[rows, 0:256] * inv).astype(BF)
            low_ps[rows, :] = low_p
            return delta + fold(jnp.sum, low_p.astype(F32) * tt[rows, 256:512])

        delta = sweep(deltas, jnp.zeros((8, 256), F32))
        delta = jnp.sum(delta, axis=0, keepdims=True)
        inv8 = inv * 0.125
        xs_copy(b).wait()

        @pl.when(b == 0)
        def _():
            kvt_copy.wait()

        def grads(first, length, dq):
            for part in range(0, length, KB):
                rows = pl.ds(pl.multiple_of(first + part, 128), KB)
                ds = ((tt[rows, 0:256] * inv8) * (tt[rows, 256:512] - delta)).astype(BF)
                dkv[rows, :] += jnp.dot(ds, xs[b, 0:256], preferred_element_type=F32) + jnp.dot(
                    low_ps[rows, :], xs[b, 256:512], preferred_element_type=F32
                )
                dq = dq + jnp.dot(kvt[0:64, rows], ds, preferred_element_type=F32)
            return dq

        dq = sweep(grads, jnp.zeros((64, 256), F32))
        dq_out[b] = jnp.concatenate([dq[:, 0:128], dq[:, 128:256]], axis=0).T.astype(BF)
        dq_copy(b).start()
        return 0

    def dq_copy(b):
        return pltpu.make_async_copy(dq_out.at[b], dq_res.at[b], dq_sem.at[b])

    lax.fori_loop(0, 8, one_block, 0)
    saved = []
    for t in range(8):
        dkv_out[t] = dkv[pl.ds(t * 512, 512), :].astype(BF)
        saved.append(pltpu.make_async_copy(dkv_out.at[t], dkv_res.at[t], dkv_sem.at[t]))
        saved[t].start()
    for t in range(8):
        saved[t].wait()
        dq_copy(t).wait()


def back(
    dkvp, dqp, enc, w,
    enc_res, q_res, w_res,
    enc_out, q_out, encv, wv, po, pb, ps, rb, gt, gs, qg, cs, cr, ms, mr, keep, fin, fsib, ycs, ycr, yms, ymr,
    loc, sib_s, sib_r, dsend, drecv, qsend, qrecv, csend, crecv, msend, mrecv, ysend, yrecv,
):
    x, xh, z, c, y = coords()
    sibling = dev(x, z, 1 - c, y)
    peers = [dev(x, z, c, mod4(y + 1)), dev(x, z, c, mod4(y + 3))]
    peers += plane_peers(x, z, c, y, [(2, 1 - c)])
    greet(peers)
    p_loc = pltpu.make_async_copy(dkvp.at[pl.ds(c * 4, 4)], po, loc.at[0])
    p_loc.start()
    e_loc = pltpu.make_async_copy(enc, encv.at[c], loc.at[1])
    e_loc.start()
    w_loc = pltpu.make_async_copy(w, wv.at[c], loc.at[2])
    w_loc.start()
    q_loc = pltpu.make_async_copy(dqp.at[xh * 4 + z], qg.at[xh * 4 + swap(z)], loc.at[3])
    q_loc.start()
    greeted(peers)

    here = c == xh
    p_sib = []
    for i, dz in enumerate((2, 1, 3, 0)):
        tz = mod4(z + dz)
        p_sib.append(remote(dkvp.at[(1 - c) * 4 + tz], pb.at[tz], sib_s.at[5 + i], sib_r.at[5 + i], sibling))
        p_sib[i].start()
    e_sib = remote(enc, encv.at[c], sib_s.at[1], sib_r.at[1], sibling)
    e_sib.start()
    w_sib = remote(w, wv.at[c], sib_s.at[2], sib_r.at[2], sibling)
    w_sib.start()

    def d_copy(dz):
        tz = mod4(z + dz)
        return remote(ps.at[tz], rb.at[z], dsend.at[dz], drecv.at[dz], dev(c * 2 + x % 2, tz, xh, y))

    p_loc.wait()
    for i, dz in enumerate((2, 1, 3, 0)):
        tz = mod4(z + dz)
        p_sib[i].wait()
        ps[tz] = (po[tz].astype(F32) + pb[tz].astype(F32)).astype(BF)
        if dz:
            d_copy(dz).start()
    d_loc = pltpu.make_async_copy(ps.at[z], rb.at[z], loc.at[4])

    @pl.when(here)
    def _():
        d_loc.start()

    @pl.when(jnp.logical_not(here))
    def _():
        d_copy(0).start()

    q_sent = []
    for dxh in (1, 0):
        for dz in (2, 1, 3, 0):
            if dxh or dz:
                tx, tz = (xh + dxh) % 2, mod4(z + dz)
                copy = remote(
                    dqp.at[tx * 4 + tz], qg.at[xh * 4 + swap(z)], qsend.at[dxh, dz], qrecv.at[dxh, dz],
                    dev(tx * 2 + x % 2, tz, c, y),
                )
                copy.start()
                q_sent.append(copy)

    for dz in (0, 1, 3, 2):
        j = mod4(z - dz)
        if dz == 0:

            @pl.when(here)
            def _():
                d_loc.wait()

            @pl.when(jnp.logical_not(here))
            def _():
                arrived(rb.at[j], drecv.at[0])
        else:
            arrived(rb.at[j], drecv.at[dz])
        turned = rb[j].T
        keys = pl.ds(pl.multiple_of(swap(j) * 64, 64), 64)
        gt[0, keys, :] = turned[0:64]
        gt[1, keys, :] = turned[64:128]

    own_tok = pl.ds(pl.multiple_of(c * 256, 256), 256)
    sib_tok = pl.ds(pl.multiple_of((1 - c) * 256, 256), 256)
    g_sib = remote(gt.at[:, :, sib_tok], gs.at[c], sib_s.at[3], sib_r.at[3], sibling)
    g_sib.start()
    gs_own = pltpu.make_async_copy(gt.at[:, :, own_tok], gs.at[c], loc.at[5])
    gs_own.start()
    e_loc.wait()
    e_sib.wait()

    def product(a, first, second):
        bx, bz = (second, first) if a == 0 else (first, second)
        columns = pl.ds(pl.multiple_of((row_group(mod4(x + bx)) * 4 + mod4(z + bz)) * 256, 256), 256)
        return jnp.dot(gt[a, :, 0:256], encv[0, :, columns], preferred_element_type=F32) + jnp.dot(
            gt[a, :, 256:512], encv[1, :, columns], preferred_element_type=F32
        )

    sent = []

    def neighbour(a, ring, step):
        along_x = (a == 1) == (ring == 0)
        return dev(mod4(x + step), z, c, y) if along_x else dev(x, mod4(z + step), c, y)

    def send_far(a, slot, ring, value):
        for half in range(2):
            cs[a, slot, half] = value[half * 128 : half * 128 + 128].astype(BF)
            at = (a, slot, half)
            copy = remote(cs.at[at], cr.at[at], csend.at[at], crecv.at[at], neighbour(a, ring, 1 - 2 * half))
            copy.start()
            sent.append(copy)

    def send_near(a, slot, ring, values):
        for half in range(2):
            value = values[half]()
            at = (a, slot, half)
            arrived(cr.at[at], crecv.at[at])
            keep_half = pl.ds(half * 128, 128)
            rest = slice(128, 256) if half == 0 else slice(0, 128)
            this = slice(0, 128) if half == 0 else slice(128, 256)
            ms[a, slot, half, pl.ds((1 - half) * 128, 128), :] = value[rest].astype(BF)
            ms[a, slot, half, keep_half, :] = (value[this] + cr[a, slot, half].astype(F32)).astype(BF)
            copy = remote(ms.at[at], mr.at[at], msend.at[at], mrecv.at[at], neighbour(a, ring, 1 - 2 * half))
            copy.start()
            sent.append(copy)

    def collect(a, slot, value):
        for half in range(2):
            at = (a, slot, half)
            arrived(mr.at[at], mrecv.at[at])
            value = value + mr[a, slot, half].astype(F32)
        return value

    def far(slot):
        for a in range(2):
            send_far(a, slot, 0, product(a, 2, slot))

    def near(slot):
        for a in range(2):
            send_near(a, slot, 0, [lambda a=a: product(a, 1, slot), lambda a=a: product(a, 3, slot)])

    def ahead(slot):
        for a in range(2):
            keep[a, slot] = product(a, 0, slot)

    def enc_rows(dy, r):
        group = mod4(y + dy)
        total = None
        for half in range(2):
            for a in range(2):
                weights = jnp.concatenate([wv[half, a, 0, group, r], wv[half, a, 1, group, r]], axis=1)
                term = jnp.dot(weights, gs[half, a], preferred_element_type=F32)
                total = term if total is None else total + term
        return total

    def y_send(src, dst, i, step):
        copy = remote(src, dst, ysend.at[i], yrecv.at[i], dev(x, z, c, mod4(y + step)))
        copy.start()
        sent.append(copy)

    def y_far():
        for half in range(2):
            for r in range(2):
                ycs[half, r] = enc_rows(2, 2 * half + r).astype(BF)
            y_send(ycs.at[half], ycr.at[half], half, 1 - 2 * half)

    def y_free():
        for half in range(2):
            for r in range(2):
                yms[half, 1 - half, r] = enc_rows(1 + 2 * half, 2 * (1 - half) + r).astype(BF)
            y_send(yms.at[half, 1 - half], ymr.at[half, 1 - half], 2 + half, 1 - 2 * half)

    def y_near():
        for half in range(2):
            for r in range(2):
                value = enc_rows(1 + 2 * half, 2 * half + r)
                if r == 0:
                    arrived(ycr.at[half], yrecv.at[half])
                yms[half, half, r] = (value + ycr[half, r].astype(F32)).astype(BF)
            y_send(yms.at[half, half], ymr.at[half, half], 4 + half, 1 - 2 * half)

    far(2)
    gs_own.wait()
    g_sib.wait()
    w_loc.wait()
    w_sib.wait()
    y_far()
    far(1)
    near(2)
    y_free()
    far(3)
    near(1)
    ahead(2)
    far(0)
    near(3)
    y_near()
    for a in range(2):
        send_far(a, 4, 1, collect(a, 2, keep[a, 2]))
    near(0)
    ahead(1)
    ahead(3)
    ahead(0)

    q_loc.wait()
    for dxh in range(2):
        for dz in range(4):
            if dxh or dz:
                src = ((xh + dxh) % 2) * 4 + swap(mod4(z - dz))
                arrived(qg.at[src], qrecv.at[dxh, dz])
    for i in range(4):
        tile = pl.ds(i * 128, 128)
        even, odd = qg[2 * i].astype(F32), qg[2 * i + 1].astype(F32)
        q_out[0:128, tile] = halves(even, odd, False, True).astype(BF)
        q_out[128:256, tile] = halves(even, odd, True, False).astype(BF)
    q_save = pltpu.make_async_copy(q_out, q_res, loc.at[6])
    q_save.start()

    for a in range(2):
        for slot in (1, 3):
            keep[a, slot] = collect(a, slot, keep[a, slot])
    for a in range(2):
        send_near(a, 4, 1, [lambda a=a: keep[a, 1], lambda a=a: keep[a, 3]])

    for r in range(4):
        total = enc_rows(0, r).astype(BF).astype(F32)
        for half in range(2):
            if r == 0:
                arrived(ymr.at[half, 1 - half], yrecv.at[2 + half])
                arrived(ymr.at[half, half], yrecv.at[4 + half])
            total = total + ymr[half, r // 2, r % 2].astype(F32)
        enc_out[:, pl.ds(r * 256, 256)] = total.T.astype(BF)
    enc_save = pltpu.make_async_copy(enc_out, enc_res, loc.at[7])
    enc_save.start()

    for a in range(2):
        fin[a] = collect(a, 4, collect(a, 0, keep[a, 0])).T
    mine = pl.ds(pl.multiple_of(c * 128, 128), 128)
    theirs = pl.ds(pl.multiple_of((1 - c) * 128, 128), 128)
    f_sib = remote(fin.at[:, theirs], fsib, sib_s.at[4], sib_r.at[4], sibling)
    f_sib.start()
    w_own = pltpu.make_async_copy(
        fin.at[:, mine], w_res.at[:, :, pl.ds(pl.multiple_of(c * 256, 256), 256)], loc.at[8]
    )
    w_own.start()
    f_sib.wait()
    w_other = pltpu.make_async_copy(
        fsib, w_res.at[:, :, pl.ds(pl.multiple_of((1 - c) * 256, 256), 256)], loc.at[9]
    )
    w_other.start()
    for copy in q_sent + sent + [d_copy(dz) for dz in (1, 2, 3)]:
        copy.wait_send()

    @pl.when(jnp.logical_not(here))
    def _():
        d_copy(0).wait_send()

    for copy in (enc_save, q_save, w_own, w_other):
        copy.wait()


def finish(*refs):
    given, results, held, (load, store) = refs[0:3], refs[3:6], refs[6:9], refs[9:11]
    parts = []
    for i in range(3):
        rows = given[i].shape[-2] // 4
        for k in range(4):
            at = (slice(None),) * (len(given[i].shape) - 2) + (pl.ds(k * rows, rows),)
            parts.append(
                (
                    pltpu.make_async_copy(given[i].at[at], held[i].at[at], load.at[i, k]),
                    pltpu.make_async_copy(held[i].at[at], results[i].at[at], store.at[i, k]),
                )
            )
    for first, _ in parts:
        first.start()
    for first, second in parts:
        first.wait()
        second.start()
    for _, second in parts:
        second.wait()


VM = pl.BlockSpec(memory_space=pltpu.VMEM)
ANY = pl.BlockSpec(memory_space=pl.ANY)
DMA = pltpu.SemaphoreType.DMA


def params(collective_id=None):
    if collective_id is None:
        return pltpu.CompilerParams(vmem_limit_bytes=60 << 20)
    return pltpu.CompilerParams(
        collective_id=collective_id, has_side_effects=True, vmem_limit_bytes=60 << 20
    )


def body(enc_out, dec_query, ctx_grad, kv_weight, enc_seg, dec_seg):
    enc = enc_out[0]
    eseg = enc_seg.reshape(32, 128)
    dseg = dec_seg.reshape(2, 128)
    shape = jax.ShapeDtypeStruct
    wg, kvx, kvt, xt, xs, spans = pl.pallas_call(
        front,
        out_shape=(
            shape((2, 2, 4, 4, 256, 128), BF),
            shape((4096, 256), BF),
            shape((128, 4096), BF),
            shape((8, 256, 512), BF),
            shape((8, 512, 128), BF),
            shape((8, 128), jnp.int32),
        ),
        in_specs=[ANY] * 6,
        out_specs=(ANY,) * 6,
        scratch_shapes=[
            pltpu.VMEM((2, 256, 4096), BF),
            pltpu.VMEM((2, 2, 4, 4, 256, 128), BF),
            pltpu.VMEM((2, 512, 256), F32),
            pltpu.VMEM((4, 512, 128), BF),
            pltpu.VMEM((8, 512, 128), BF),
            pltpu.VMEM((256, 512), BF),
            pltpu.VMEM((256, 512), BF),
            pltpu.VMEM((2, 128), jnp.int32),
            pltpu.VMEM((32, 128), jnp.int32),
            pltpu.VMEM((8, 272, 128), BF),
            pltpu.VMEM((8, 272, 128), BF),
            pltpu.VMEM((4096, 256), BF),
            pltpu.VMEM((128, 4096), BF),
            pltpu.VMEM((8, 256, 512), BF),
            pltpu.VMEM((8, 512, 128), BF),
            pltpu.VMEM((8, 128), jnp.int32),
            DMA((10,)), DMA((19,)), DMA((3,)), DMA((3,)),
            DMA((2, 2, 4, 4, 2)), DMA((2, 2, 4, 4, 2)),
            DMA((2, 4)), DMA((2, 4)),
            DMA((4, 2)), DMA((2, 4)),
            DMA((2, 4)), DMA((2, 4)),
        ],
        compiler_params=params(1),
        name="front",
    )(enc, dec_query[0], ctx_grad[0], kv_weight, dseg, eseg)

    dkvp, dqp = pl.pallas_call(
        attend,
        out_shape=(shape((8, 512, 128), BF), shape((8, 128, 128), BF)),
        in_specs=[ANY] * 5,
        out_specs=(ANY, ANY),
        scratch_shapes=[
            pltpu.SMEM((8, 128), jnp.int32),
            pltpu.VMEM((4096, 256), BF),
            pltpu.VMEM((128, 4096), BF),
            pltpu.VMEM((8, 256, 512), BF),
            pltpu.VMEM((8, 512, 128), BF),
            pltpu.VMEM((4096, 512), F32),
            pltpu.VMEM((4096, 256), BF),
            pltpu.VMEM((4096, 128), F32),
            pltpu.VMEM((8, 512, 128), BF),
            pltpu.VMEM((8, 128, 128), BF),
            DMA((3,)), DMA((8,)), DMA((8,)), DMA((8,)), DMA((8,)),
        ],
        compiler_params=params(),
        name="attend",
    )(spans, kvx, kvt, xt, xs)

    grads = pl.pallas_call(
        back,
        out_shape=(shape((256, 1024), BF), shape((256, 512), BF), shape((2, 128, 512), F32)),
        in_specs=[ANY, ANY, ANY, ANY],
        out_specs=(ANY, ANY, ANY),
        scratch_shapes=[
            pltpu.VMEM((256, 1024), BF),
            pltpu.VMEM((256, 512), BF),
            pltpu.VMEM((2, 256, 4096), BF),
            pltpu.VMEM((2, 2, 2, 4, 4, 256, 128), BF),
            pltpu.VMEM((4, 512, 128), BF),
            pltpu.VMEM((4, 512, 128), BF),
            pltpu.VMEM((4, 512, 128), BF),
            pltpu.VMEM((4, 512, 128), BF),
            pltpu.VMEM((2, 256, 512), BF),
            pltpu.VMEM((2, 2, 256, 256), BF),
            pltpu.VMEM((8, 128, 128), BF),
            pltpu.VMEM((2, 5, 2, 128, 256), BF),
            pltpu.VMEM((2, 5, 2, 128, 256), BF),
            pltpu.VMEM((2, 5, 2, 256, 256), BF),
            pltpu.VMEM((2, 5, 2, 256, 256), BF),
            pltpu.VMEM((2, 4, 256, 256), F32),
            pltpu.VMEM((2, 256, 256), F32),
            pltpu.VMEM((2, 128, 256), F32),
            pltpu.VMEM((2, 2, 256, 256), BF),
            pltpu.VMEM((2, 2, 256, 256), BF),
            pltpu.VMEM((2, 2, 2, 256, 256), BF),
            pltpu.VMEM((2, 2, 2, 256, 256), BF),
            DMA((10,)), DMA((9,)), DMA((9,)),
            DMA((4,)), DMA((4,)),
            DMA((2, 4)), DMA((2, 4)),
            DMA((2, 5, 2)), DMA((2, 5, 2)),
            DMA((2, 5, 2)), DMA((2, 5, 2)),
            DMA((6,)), DMA((6,)),
        ],
        compiler_params=params(2),
        name="back",
    )(dkvp, dqp, enc, wg)

    enc_grad, q_grad, w_grad = pl.pallas_call(
        finish,
        out_shape=(shape((256, 1024), BF), shape((256, 512), BF), shape((2, 128, 512), F32)),
        in_specs=[ANY] * 3,
        out_specs=(ANY, ANY, ANY),
        scratch_shapes=[
            pltpu.VMEM((256, 1024), BF), pltpu.VMEM((256, 512), BF), pltpu.VMEM((2, 128, 512), F32),
            DMA((3, 4)), DMA((3, 4)),
        ],
        compiler_params=params(),
        name="finish",
    )(*grads)
    return enc_grad[None], q_grad[None], w_grad


def solution(mesh):
    placed = (
        P("dp", "seq", None),
        P("dp", "seq", "mp"),
        P("dp", "seq", "mp"),
        P(None, ("dp", "seq"), "mp"),
        P("dp", None),
        P("dp", "seq"),
    )
    return jax.shard_map(
        body,
        mesh=mesh,
        in_specs=placed,
        out_specs=(P("dp", "seq", "mp"), P("dp", "seq", "mp"), P(None, ("dp", "seq"), "mp")),
        check_vma=False,
    )
```

```python
import functools

import jax
import jax.numpy as jnp
from jax import lax
from jax.experimental import pallas as pl
from jax.experimental.pallas import tpu as pltpu
from jax.sharding import PartitionSpec as P

MESH = pl.DeviceIdType.MESH
BF = jnp.bfloat16
F32 = jnp.float32
NEG = -1e30
KB = 256


def coords():
    dp, seq, y = lax.axis_index("dp"), lax.axis_index("seq"), lax.axis_index("mp")
    xh = seq // 8
    return xh * 2 + dp, xh, (seq // 2) % 4, seq % 2, y


def dev(x, z, core, y):
    return (x % 2, (x // 2) * 8 + z * 2 + core, y)


def row_group(x):
    return (x % 2) * 2 + x // 2


def swap(v):
    return (v % 2) * 2 + v // 2


def mod4(v):
    return (v + 4) % 4


def remote(src, dst, send, recv, device):
    return pltpu.make_async_remote_copy(
        src_ref=src, dst_ref=dst, send_sem=send, recv_sem=recv, device_id=device, device_id_type=MESH
    )


def arrived(dst, sem):
    pltpu.make_async_copy(dst, dst, sem).wait()


def greet(peers):
    for peer in peers:
        pl.semaphore_signal(pltpu.get_barrier_semaphore(), inc=1, device_id=peer, device_id_type=MESH)


def greeted(peers):
    pl.semaphore_wait(pltpu.get_barrier_semaphore(), len(peers))


def plane_peers(x, z, c, y, other_cores):
    peers = [dev(x, z, 1 - c, y), dev(mod4(x + 1), z, c, y), dev(mod4(x + 3), z, c, y)]
    for dx, core in [(0, c), (2, c)] + other_cores:
        for dz in range(4):
            if dx or dz:
                peers.append(dev(mod4(x + dx), mod4(z + dz), core, y))
    return peers


def lanes_of(shape):
    return lax.broadcasted_iota(jnp.int32, shape, 1)


def halves(first, second, shift_first, shift_second):
    first = pltpu.roll(first, 64, 1) if shift_first else first
    second = pltpu.roll(second, 64, 1) if shift_second else second
    return jnp.where(lanes_of(first.shape) < 64, first, second)


def front(
    enc, q_in, do_in, w, dseg_in, eseg_in,
    wg_out, kvx_out, kvt_out, xt_out, xs_out, spans_out,
    encv, wg, acc, kvs, kvb, q, do, dseg, eseg, qs, qb, kvx, kvt, xt, xs, spans,
    loc, save, sib_s, sib_r, ws, wr, qsend, qrecv, ksend, krecv, fsend, frecv,
):
    x, xh, z, c, y = coords()
    me = row_group(x)
    t = xh * 4 + z
    sibling = dev(x, z, 1 - c, y)
    peers = plane_peers(x, z, c, y, [(0, 1 - c), (2, 1 - c)])
    q_in_copy = pltpu.make_async_copy(q_in, q, loc.at[5])
    do_in_copy = pltpu.make_async_copy(do_in, do, loc.at[6])
    dseg_copy = pltpu.make_async_copy(dseg_in, dseg, loc.at[8])
    eseg_copy = pltpu.make_async_copy(eseg_in, eseg, loc.at[9])
    for copy in (q_in_copy, do_in_copy, dseg_copy, eseg_copy):
        copy.start()
    greet(peers)

    own = pl.multiple_of(c * 256, 256)
    other = pl.multiple_of((1 - c) * 256, 256)
    rows = pl.ds(pl.multiple_of(c * 128, 128), 128)
    w_loc = [
        pltpu.make_async_copy(
            w.at[:, :, pl.ds(own + 128 * part, 128)], wg.at[:, part, me, z, rows], loc.at[7 * part]
        )
        for part in range(2)
    ]
    for copy in w_loc:
        copy.start()
    e_loc = pltpu.make_async_copy(enc, encv.at[c], loc.at[1])
    e_loc.start()

    dseg_copy.wait()
    eseg_copy.wait()
    ids = dseg[...].astype(F32)
    row = lax.broadcasted_iota(jnp.int32, (16, 128), 0)
    id_rows = jnp.where(row == 0, ids[0:1], jnp.where(row == 1, ids[1:2], 0.0)).astype(BF)
    q_in_copy.wait()
    do_in_copy.wait()
    for h in range(8):
        tile = pl.ds((h // 2) * 128, 128)
        odd = h % 2 == 1
        qs[h, 0:256, :] = halves(q[:, tile].astype(F32), do[:, tile].astype(F32), odd, not odd).astype(BF)
        qs[h, 256:272, :] = id_rows
    q_loc = pltpu.make_async_copy(qs.at[xh * 4 + swap(z)], qb.at[t], loc.at[2])
    q_loc.start()
    greeted(peers)

    w_sib = [
        remote(
            w.at[:, :, pl.ds(other + 128 * part, 128)], wg.at[:, part, me, z, rows],
            sib_s.at[2 * part], sib_r.at[2 * part], sibling,
        )
        for part in range(2)
    ]
    for copy in w_sib:
        copy.start()
    q_sent = []
    for dxh in (1, 0):
        for dz in (2, 1, 3, 0):
            if dxh == 0 and dz == 0:
                continue
            hx, hz = (xh + dxh) % 2, mod4(z + dz)
            copy = remote(
                qs.at[hx * 4 + swap(hz)], qb.at[t], qsend.at[dxh, dz], qrecv.at[dxh, dz],
                dev(mod4(x + 2 * dxh), hz, c, y),
            )
            copy.start()
            q_sent.append(copy)
    e_sib = remote(enc, encv.at[c], sib_s.at[1], sib_r.at[1], sibling)
    e_sib.start()
    for copy in w_loc + w_sib:
        copy.wait()

    def place(a, first, second):
        bx, bz = (first, second) if a == 0 else (second, first)
        return row_group(mod4(x - bx)), mod4(z - bz)

    def block_of(part, a, first, second, half=None):
        group, bz = place(a, first, second)
        block = wg.at[a, part, group, bz]
        return block if half is None else block.at[pl.ds(half * 128, 128)]

    sent = []

    def pass_on(part, a, first, second, ring, step, half=None):
        block = block_of(part, a, first, second, half)
        to_first, to_second = (first + step) % 4 if ring == 0 else first, (second + step) % 4 if ring else second
        sem = (part, a, to_first, to_second, half or 0)
        along_x = (a == 0) == (ring == 0)
        target = dev(mod4(x + step), z, c, y) if along_x else dev(x, mod4(z + step), c, y)
        copy = remote(block, block, ws.at[sem], wr.at[sem], target)
        copy.start()
        sent.append(copy)

    def take(part, a, first, second):
        if second == 2 or (first == 2 and second == 0):
            for half in range(2):
                arrived(block_of(part, a, first, second, half), wr.at[part, a, first, second, half])
        else:
            arrived(block_of(part, a, first, second), wr.at[part, a, first, second, 0])

    def multiply(part, dx, dz, fresh=False):
        group, bz = place(0, dx, dz)
        columns = pl.ds(pl.multiple_of((group * 4 + bz) * 256, 256), 256)
        both = jnp.concatenate([wg[0, part, group, bz], wg[1, part, group, bz]], axis=1)
        for half in range(2):
            term = jnp.dot(encv[half, :, columns], both, preferred_element_type=F32)
            if fresh:
                acc[part, pl.ds(half * 256, 256), :] = term
            else:
                acc[part, pl.ds(half * 256, 256), :] += term

    def both_ways(part, a, first):
        pass_on(part, a, first, 0, 1, 1)
        pass_on(part, a, first, 0, 1, -1)

    def own_first(part):
        for step in (1, -1):
            for a in range(2):
                pass_on(part, a, 0, 0, 0, step)

    def own_second(part):
        for a in range(2):
            both_ways(part, a, 0)

    def near_first(part):
        for a in range(2):
            take(part, a, 1, 0)
            pass_on(part, a, 1, 0, 0, 1, 0)
            take(part, a, 3, 0)
            pass_on(part, a, 3, 0, 0, -1, 1)
        for a in range(2):
            both_ways(part, a, 1)
            both_ways(part, a, 3)

    def near_second(part, first):
        for a in range(2):
            take(part, a, first, 1)
            pass_on(part, a, first, 1, 1, 1, 0)
            take(part, a, first, 3)
            pass_on(part, a, first, 3, 1, -1, 1)

    def far_first(part):
        for a in range(2):
            take(part, a, 2, 0)
            both_ways(part, a, 2)

    own_first(0)
    own_second(0)
    own_first(1)

    def one_hot(i, _):
        seg = eseg[pl.ds(i, 1), :].astype(F32)
        row = lax.broadcasted_iota(jnp.int32, (128, 128), 0).astype(F32)
        hot = jnp.where(row == seg, 1.0, 0.0)
        kvx[pl.ds(pl.multiple_of(i * 128, 128), 128), 128:256] = hot.T.astype(BF)
        return 0

    lax.fori_loop(0, 32, one_hot, 0)

    near_first(0)
    own_second(1)
    near_second(0, 0)
    near_first(1)
    far_first(0)
    near_second(1, 0)
    far_first(1)
    e_loc.wait()
    e_sib.wait()

    def multiply_near(part):
        multiply(part, 0, 0, True)
        for d in (1, 3):
            multiply(part, d, 0)
            multiply(part, 0, d)

    def multiply_diagonal(part):
        for dx in (1, 3):
            for dz in (1, 3):
                multiply(part, dx, dz)

    multiply_near(0)

    q_loc.wait()
    for dxh in range(2):
        for dz in range(4):
            if dxh or dz:
                src = ((xh + dxh) % 2) * 4 + mod4(z - dz)
                arrived(qb.at[src], qrecv.at[dxh, dz])

    def prepare(b, _):
        block = qb[b, 0:256, :]
        low = lanes_of((256, 128)) < 64
        zero = jnp.zeros_like(block)
        xs[b, 0:256, :] = jnp.where(low, block, zero)
        xs[b, 256:512, :] = jnp.where(low, zero, block)
        turned = block.T
        xt[b, 0:64, 0:256] = turned[0:64] * jnp.asarray(0.125, BF)
        xt[b, 64:128, 256:512] = turned[64:128]
        xt[b, 0:64, 256:512] = jnp.zeros((64, 256), BF)
        xt[b, 64:128, 0:256] = jnp.zeros((64, 256), BF)
        xt[b, 128:256, :] = jnp.zeros((128, 512), BF)
        ids = qb[b, 256:272, :].astype(F32)
        ids = jnp.concatenate([ids[0:1], ids[1:2]], axis=1)
        row = lax.broadcasted_iota(jnp.int32, (16, 256), 0)
        differs = (row < 4) & (row.astype(F32) != ids)
        xt[b, 128:144, 0:256] = jnp.where(differs, NEG, 0.0).astype(BF)
        seg = eseg[...].astype(F32)
        low_id, high_id = jnp.min(ids, axis=1, keepdims=True), jnp.max(ids, axis=1, keepdims=True)
        begin = jnp.sum(jnp.where(seg < low_id, 1.0, 0.0), axis=(0, 1), keepdims=True)
        end = jnp.sum(jnp.where(seg <= high_id, 1.0, 0.0), axis=(0, 1), keepdims=True)
        begin = jnp.floor(begin * (1.0 / 128)) * 128.0
        count = jnp.floor((end - begin + (KB - 1)) * (1.0 / KB))
        begin = jnp.minimum(begin, 4096.0 - count * KB)
        spans[pl.ds(b, 1), :] = jnp.where(lanes_of((1, 128)) == 0, begin, count).astype(jnp.int32)
        return 0

    lax.fori_loop(0, 4, prepare, 0)
    for first in (1, 3, 2):
        near_second(0, first)
    multiply_near(1)
    for first in (1, 3, 2):
        near_second(1, first)
    multiply_diagonal(0)

    ex = (c + 2 - xh) % 2
    tx = c * 2 + x % 2
    here = c == xh

    def kv_copy(head, core):
        rows_of = pl.ds(core * 256, 256)
        return remote(
            kvs.at[head, rows_of], kvb.at[t, rows_of], ksend.at[head, core], krecv.at[ex, z],
            dev(tx, swap(head), core, y),
        )

    def kv_local(core):
        rows_of = pl.ds(core * 256, 256)
        return pltpu.make_async_copy(kvs.at[swap(z), rows_of], kvb.at[t, rows_of], loc.at[4])

    def stays(head, core):
        return jnp.logical_and(here, jnp.logical_and(z == swap(head), c == core))

    def last_part(part):
        for dx, dz in ((2, 0), (0, 2), (1, 2), (3, 2), (2, 1), (2, 3), (2, 2)):
            if dz == 2:
                take(part, 0, dx, dz)
            if dx == 2:
                take(part, 1, dz, dx)
            multiply(part, dx, dz)
        for i in range(2):
            head = 2 * part + i
            keys, values = acc[part, :, 0:128], acc[part, :, 128:256]
            kvs[head] = halves(keys, values, i == 1, i == 0).astype(BF)
            for core in range(2):
                local = stays(head, core)

                @pl.when(local)
                def _():
                    kv_local(core).start()

                @pl.when(jnp.logical_not(local))
                def _():
                    kv_copy(head, core).start()

    last_part(0)
    multiply_diagonal(1)
    last_part(1)
    lax.fori_loop(4, 8, prepare, 0)
    saved = [
        pltpu.make_async_copy(xt, xt_out, save.at[8]),
        pltpu.make_async_copy(xs, xs_out, save.at[9]),
        pltpu.make_async_copy(spans, spans_out, save.at[18]),
    ]
    for copy in saved:
        copy.start()

    w_save = pltpu.make_async_copy(wg, wg_out, loc.at[3])
    w_save.start()

    mine = pl.ds(pl.multiple_of(c * 256, 256), 256)
    theirs = pl.ds(pl.multiple_of((1 - c) * 256, 256), 256)

    def source(e, dz):
        return ((xh + e) % 2) * 4 + mod4(z - dz)

    f_sent = []

    def hand_over(e, dz):
        src = source(e, dz)
        if e == 0 and dz == 0:

            @pl.when(here)
            def _():
                for core in range(2):

                    @pl.when(c == core)
                    def _():
                        kv_local(core).wait()

            @pl.when(jnp.logical_not(here))
            def _():
                arrived(kvb.at[src, mine], krecv.at[0, z])
        else:
            arrived(kvb.at[src, mine], krecv.at[e, mod4(z - dz)])
        copy = remote(kvb.at[src, mine], kvb.at[src, mine], fsend.at[e, dz], frecv.at[e, dz], sibling)
        copy.start()
        f_sent.append(copy)

    def use(e, dz):
        src = source(e, dz)
        arrived(kvb.at[src, theirs], frecv.at[e, dz])
        block = kvb[src]
        span = pl.ds(pl.multiple_of(src * 512, 512), 512)
        kvx[span, 0:128] = block
        kvt[:, span] = block.T
        for copy in (
            pltpu.make_async_copy(kvx.at[span], kvx_out.at[span], save.at[e * 4 + dz]),
            pltpu.make_async_copy(kvt.at[:, span], kvt_out.at[:, span], save.at[10 + e * 4 + dz]),
        ):
            copy.start()
            saved.append(copy)

    for copy in sent + q_sent:
        copy.wait_send()
    order = [(e, dz) for dz in (0, 1, 3, 2) for e in (0, 1)]
    for i, at in enumerate(order):
        hand_over(*at)
        if i:
            use(*order[i - 1])
    use(*order[-1])

    for copy in f_sent:
        copy.wait_send()
    for head in range(4):
        for core in range(2):

            @pl.when(jnp.logical_not(stays(head, core)))
            def _():
                kv_copy(head, core).wait_send()

    w_save.wait()
    for copy in saved:
        copy.wait()


def attend(
    spans_in, kvx_in, kvt_in, xt_in, xs_in, dkv_res, dq_res,
    spans, kvx, kvt, xt, xs, tt, low_ps, dkv, dkv_out, dq_out, sem, xt_sem, xs_sem, dkv_sem, dq_sem,
):
    kvx_copy = pltpu.make_async_copy(kvx_in, kvx, sem.at[0])
    kvt_copy = pltpu.make_async_copy(kvt_in, kvt, sem.at[1])

    def xt_copy(b):
        return pltpu.make_async_copy(xt_in.at[b], xt.at[b], xt_sem.at[b])

    def xs_copy(b):
        return pltpu.make_async_copy(xs_in.at[b], xs.at[b], xs_sem.at[b])

    spans_copy = pltpu.make_async_copy(spans_in, spans, sem.at[2])
    spans_copy.start()
    xt_copy(0).start()
    kvx_copy.start()
    xs_copy(0).start()
    kvt_copy.start()
    for b in range(1, 8):
        xt_copy(b).start()
        xs_copy(b).start()
    dkv[...] = jnp.zeros_like(dkv)
    spans_copy.wait()
    kvx_copy.wait()

    def one_block(b, _):
        begin, count = spans[b, 0], spans[b, 1]
        xt_copy(b).wait()

        def sweep(step, carry):
            done = 0
            for blocks in (8, 3, 2, 1):
                times = (count - done) // blocks

                def piece(i, value, done=done, blocks=blocks):
                    first = pl.multiple_of(begin + (done + i * blocks) * KB, 128)
                    return step(first, blocks * KB, value)

                carry = lax.fori_loop(0, times, piece, carry)
                done = done + times * blocks
            return carry

        def fold(op, v):
            return op(v.reshape(v.shape[0] // 8, 8, 256), axis=0)

        def scores(first, length, top):
            rows = pl.ds(first, length)
            both = jnp.dot(kvx[rows, :], xt[b], preferred_element_type=F32)
            tt[rows, :] = both
            return jnp.maximum(top, fold(jnp.max, both[:, 0:256]))

        top = sweep(scores, jnp.full((8, 256), -3e38, F32))
        top = jnp.max(top, axis=0, keepdims=True)

        def weigh(first, length, total):
            rows = pl.ds(first, length)
            e = jnp.exp(tt[rows, 0:256] - top)
            tt[rows, 0:256] = e
            return total + fold(jnp.sum, e)

        total = sweep(weigh, jnp.zeros((8, 256), F32))
        inv = 1.0 / jnp.sum(total, axis=0, keepdims=True)

        def deltas(first, length, delta):
            rows = pl.ds(first, length)
            low_p = (tt[rows, 0:256] * inv).astype(BF)
            low_ps[rows, :] = low_p
            return delta + fold(jnp.sum, low_p.astype(F32) * tt[rows, 256:512])

        delta = sweep(deltas, jnp.zeros((8, 256), F32))
        delta = jnp.sum(delta, axis=0, keepdims=True)
        inv8 = inv * 0.125
        xs_copy(b).wait()

        @pl.when(b == 0)
        def _():
            kvt_copy.wait()

        def grads(first, length, dq):
            for part in range(0, length, KB):
                rows = pl.ds(pl.multiple_of(first + part, 128), KB)
                ds = ((tt[rows, 0:256] * inv8) * (tt[rows, 256:512] - delta)).astype(BF)
                dkv[rows, :] += jnp.dot(ds, xs[b, 0:256], preferred_element_type=F32) + jnp.dot(
                    low_ps[rows, :], xs[b, 256:512], preferred_element_type=F32
                )
                dq = dq + jnp.dot(kvt[0:64, rows], ds, preferred_element_type=F32)
            return dq

        dq = sweep(grads, jnp.zeros((64, 256), F32))
        dq_out[b] = jnp.concatenate([dq[:, 0:128], dq[:, 128:256]], axis=0).T.astype(BF)
        dq_copy(b).start()
        return 0

    def dq_copy(b):
        return pltpu.make_async_copy(dq_out.at[b], dq_res.at[b], dq_sem.at[b])

    lax.fori_loop(0, 8, one_block, 0)
    saved = []
    for t in range(8):
        dkv_out[t] = dkv[pl.ds(t * 512, 512), :].astype(BF)
        saved.append(pltpu.make_async_copy(dkv_out.at[t], dkv_res.at[t], dkv_sem.at[t]))
        saved[t].start()
    for t in range(8):
        saved[t].wait()
        dq_copy(t).wait()


def back(
    dkvp, dqp, enc, w,
    enc_res, q_res, w_res,
    enc_out, q_out, encv, wv, po, pb, ps, rb, gt, gs, qg, cs, cr, ms, mr, keep, fin, fsib, ycs, ycr, yms, ymr,
    loc, sib_s, sib_r, dsend, drecv, qsend, qrecv, csend, crecv, msend, mrecv, ysend, yrecv,
):
    x, xh, z, c, y = coords()
    sibling = dev(x, z, 1 - c, y)
    peers = [dev(x, z, c, mod4(y + 1)), dev(x, z, c, mod4(y + 3))]
    peers += plane_peers(x, z, c, y, [(2, 1 - c)])
    greet(peers)
    p_loc = pltpu.make_async_copy(dkvp.at[pl.ds(c * 4, 4)], po, loc.at[0])
    p_loc.start()
    tokens = pl.ds(pl.multiple_of(c * 256, 256), 256)
    e_loc = pltpu.make_async_copy(enc, encv.at[tokens], loc.at[1])
    e_loc.start()
    w_loc = pltpu.make_async_copy(w, wv.at[c], loc.at[2])
    w_loc.start()
    q_loc = pltpu.make_async_copy(dqp.at[xh * 4 + z], qg.at[xh * 4 + swap(z)], loc.at[3])
    q_loc.start()
    greeted(peers)

    here = c == xh
    p_sib = []
    for i, dz in enumerate((2, 1, 3, 0)):
        tz = mod4(z + dz)
        p_sib.append(remote(dkvp.at[(1 - c) * 4 + tz], pb.at[tz], sib_s.at[5 + i], sib_r.at[5 + i], sibling))
        p_sib[i].start()
    q_sent = []
    for dxh in (1, 0):
        for dz in (2, 1, 3, 0):
            if dxh or dz:
                tx, tz = (xh + dxh) % 2, mod4(z + dz)
                copy = remote(
                    dqp.at[tx * 4 + tz], qg.at[xh * 4 + swap(z)], qsend.at[dxh, dz], qrecv.at[dxh, dz],
                    dev(tx * 2 + x % 2, tz, c, y),
                )
                copy.start()
                q_sent.append(copy)
    e_sib = remote(enc, encv.at[tokens], sib_s.at[1], sib_r.at[1], sibling)
    e_sib.start()
    w_sib = remote(w, wv.at[c], sib_s.at[2], sib_r.at[2], sibling)
    w_sib.start()

    def d_copy(dz):
        tz = mod4(z + dz)
        return remote(ps.at[tz], rb.at[z], dsend.at[dz], drecv.at[dz], dev(c * 2 + x % 2, tz, xh, y))

    p_loc.wait()
    for i, dz in enumerate((2, 1, 3, 0)):
        tz = mod4(z + dz)
        p_sib[i].wait()
        ps[tz] = (po[tz].astype(F32) + pb[tz].astype(F32)).astype(BF)
        if dz:
            d_copy(dz).start()
    d_loc = pltpu.make_async_copy(ps.at[z], rb.at[z], loc.at[4])

    @pl.when(here)
    def _():
        d_loc.start()

    @pl.when(jnp.logical_not(here))
    def _():
        d_copy(0).start()

    for dz in (0, 1, 3, 2):
        j = mod4(z - dz)
        if dz == 0:

            @pl.when(here)
            def _():
                d_loc.wait()

            @pl.when(jnp.logical_not(here))
            def _():
                arrived(rb.at[j], drecv.at[0])
        else:
            arrived(rb.at[j], drecv.at[dz])
        turned = rb[j].T
        keys = pl.ds(pl.multiple_of(swap(j) * 64, 64), 64)
        gt[0, keys, :] = turned[0:64]
        gt[1, keys, :] = turned[64:128]

    own_tok = pl.ds(pl.multiple_of(c * 256, 256), 256)
    sib_tok = pl.ds(pl.multiple_of((1 - c) * 256, 256), 256)
    g_sib = remote(gt.at[:, :, sib_tok], gs.at[c], sib_s.at[3], sib_r.at[3], sibling)
    g_sib.start()
    gs_own = pltpu.make_async_copy(gt.at[:, :, own_tok], gs.at[c], loc.at[5])
    gs_own.start()
    e_loc.wait()
    e_sib.wait()

    def product(a, first, second):
        bx, bz = (second, first) if a == 0 else (first, second)
        columns = pl.ds(pl.multiple_of((row_group(mod4(x + bx)) * 4 + mod4(z + bz)) * 256, 256), 256)
        return jnp.dot(gt[a], encv[:, columns], preferred_element_type=F32)

    sent = []

    def neighbour(a, ring, step):
        along_x = (a == 1) == (ring == 0)
        return dev(mod4(x + step), z, c, y) if along_x else dev(x, mod4(z + step), c, y)

    def send_far(a, slot, ring, value):
        for half in range(2):
            cs[a, slot, half] = value[half * 128 : half * 128 + 128].astype(BF)
            at = (a, slot, half)
            copy = remote(cs.at[at], cr.at[at], csend.at[at], crecv.at[at], neighbour(a, ring, 1 - 2 * half))
            copy.start()
            sent.append(copy)

    def send_near(a, slot, ring, values):
        for half in range(2):
            value = values[half]()
            at = (a, slot, half)
            arrived(cr.at[at], crecv.at[at])
            keep_half = pl.ds(half * 128, 128)
            rest = slice(128, 256) if half == 0 else slice(0, 128)
            this = slice(0, 128) if half == 0 else slice(128, 256)
            ms[a, slot, half, pl.ds((1 - half) * 128, 128), :] = value[rest].astype(BF)
            ms[a, slot, half, keep_half, :] = (value[this] + cr[a, slot, half].astype(F32)).astype(BF)
            copy = remote(ms.at[at], mr.at[at], msend.at[at], mrecv.at[at], neighbour(a, ring, 1 - 2 * half))
            copy.start()
            sent.append(copy)

    def collect(a, slot, value):
        for half in range(2):
            at = (a, slot, half)
            arrived(mr.at[at], mrecv.at[at])
            value = value + mr[a, slot, half].astype(F32)
        return value

    def far(slot):
        for a in range(2):
            send_far(a, slot, 0, product(a, 2, slot))

    def near(slot):
        for a in range(2):
            send_near(a, slot, 0, [lambda a=a: product(a, 1, slot), lambda a=a: product(a, 3, slot)])

    def ahead(slot):
        for a in range(2):
            keep[a, slot] = product(a, 0, slot)

    def enc_rows(dy, r):
        group = mod4(y + dy)
        weights = [wv[half, a, part, group, r] for half in range(2) for a in range(2) for part in range(2)]
        return jnp.dot(
            jnp.concatenate(weights, axis=1), gs[...].reshape(1024, 256), preferred_element_type=F32
        )

    def y_send(src, dst, i, step):
        copy = remote(src, dst, ysend.at[i], yrecv.at[i], dev(x, z, c, mod4(y + step)))
        copy.start()
        sent.append(copy)

    def y_far():
        for half in range(2):
            for r in range(2):
                ycs[half, r] = enc_rows(2, 2 * half + r).astype(BF)
            y_send(ycs.at[half], ycr.at[half], half, 1 - 2 * half)

    def y_free():
        for half in range(2):
            for r in range(2):
                yms[half, 1 - half, r] = enc_rows(1 + 2 * half, 2 * (1 - half) + r).astype(BF)
            y_send(yms.at[half, 1 - half], ymr.at[half, 1 - half], 2 + half, 1 - 2 * half)

    def y_near():
        for half in range(2):
            for r in range(2):
                value = enc_rows(1 + 2 * half, 2 * half + r)
                if r == 0:
                    arrived(ycr.at[half], yrecv.at[half])
                yms[half, half, r] = (value + ycr[half, r].astype(F32)).astype(BF)
            y_send(yms.at[half, half], ymr.at[half, half], 4 + half, 1 - 2 * half)

    far(2)
    gs_own.wait()
    g_sib.wait()
    w_loc.wait()
    w_sib.wait()
    y_far()
    far(1)
    near(2)
    y_free()
    far(3)
    near(1)
    ahead(2)
    far(0)
    near(3)
    y_near()
    for a in range(2):
        send_far(a, 4, 1, collect(a, 2, keep[a, 2]))
    near(0)
    ahead(1)
    ahead(3)
    ahead(0)

    q_loc.wait()
    for dxh in range(2):
        for dz in range(4):
            if dxh or dz:
                src = ((xh + dxh) % 2) * 4 + swap(mod4(z - dz))
                arrived(qg.at[src], qrecv.at[dxh, dz])
    for i in range(4):
        tile = pl.ds(i * 128, 128)
        even, odd = qg[2 * i].astype(F32), qg[2 * i + 1].astype(F32)
        q_out[0:128, tile] = halves(even, odd, False, True).astype(BF)
        q_out[128:256, tile] = halves(even, odd, True, False).astype(BF)
    q_save = pltpu.make_async_copy(q_out, q_res, loc.at[6])
    q_save.start()

    for a in range(2):
        for slot in (1, 3):
            keep[a, slot] = collect(a, slot, keep[a, slot])
    earlier = list(sent)
    for a in range(2):
        send_near(a, 4, 1, [lambda a=a: keep[a, 1], lambda a=a: keep[a, 3]])

    for r in range(4):
        total = enc_rows(0, r).astype(BF).astype(F32)
        for half in range(2):
            if r == 0:
                arrived(ymr.at[half, 1 - half], yrecv.at[2 + half])
                arrived(ymr.at[half, half], yrecv.at[4 + half])
            total = total + ymr[half, r // 2, r % 2].astype(F32)
        enc_out[:, pl.ds(r * 256, 256)] = total.T.astype(BF)
    enc_save = pltpu.make_async_copy(enc_out, enc_res, loc.at[7])
    enc_save.start()

    for copy in q_sent + earlier + [d_copy(dz) for dz in (1, 2, 3)]:
        copy.wait_send()

    @pl.when(jnp.logical_not(here))
    def _():
        d_copy(0).wait_send()

    for a in range(2):
        fin[a] = collect(a, 4, collect(a, 0, keep[a, 0])).T
    mine = pl.ds(pl.multiple_of(c * 128, 128), 128)
    theirs = pl.ds(pl.multiple_of((1 - c) * 128, 128), 128)
    f_sib = remote(fin.at[:, theirs], fsib, sib_s.at[4], sib_r.at[4], sibling)
    f_sib.start()
    w_own = pltpu.make_async_copy(
        fin.at[:, mine], w_res.at[:, :, pl.ds(pl.multiple_of(c * 256, 256), 256)], loc.at[8]
    )
    w_own.start()
    f_sib.wait()
    w_other = pltpu.make_async_copy(
        fsib, w_res.at[:, :, pl.ds(pl.multiple_of((1 - c) * 256, 256), 256)], loc.at[9]
    )
    w_other.start()
    for copy in sent[len(earlier) :]:
        copy.wait_send()
    for copy in (enc_save, q_save, w_own, w_other):
        copy.wait()


def finish(*refs):
    given, results, held, (load, store) = refs[0:3], refs[3:6], refs[6:9], refs[9:11]
    parts = []
    for i in range(3):
        rows = given[i].shape[-2] // 4
        for k in range(4):
            at = (slice(None),) * (len(given[i].shape) - 2) + (pl.ds(k * rows, rows),)
            parts.append(
                (
                    pltpu.make_async_copy(given[i].at[at], held[i].at[at], load.at[i, k]),
                    pltpu.make_async_copy(held[i].at[at], results[i].at[at], store.at[i, k]),
                )
            )
    for first, _ in parts:
        first.start()
    for first, second in parts:
        first.wait()
        second.start()
    for _, second in parts:
        second.wait()


VM = pl.BlockSpec(memory_space=pltpu.VMEM)
ANY = pl.BlockSpec(memory_space=pl.ANY)
DMA = pltpu.SemaphoreType.DMA


def params(collective_id=None):
    if collective_id is None:
        return pltpu.CompilerParams(vmem_limit_bytes=60 << 20)
    return pltpu.CompilerParams(
        collective_id=collective_id, has_side_effects=True, vmem_limit_bytes=60 << 20
    )


def body(enc_out, dec_query, ctx_grad, kv_weight, enc_seg, dec_seg):
    enc = enc_out[0]
    eseg = enc_seg.reshape(32, 128)
    dseg = dec_seg.reshape(2, 128)
    shape = jax.ShapeDtypeStruct
    wg, kvx, kvt, xt, xs, spans = pl.pallas_call(
        front,
        out_shape=(
            shape((2, 2, 4, 4, 256, 128), BF),
            shape((4096, 256), BF),
            shape((128, 4096), BF),
            shape((8, 256, 512), BF),
            shape((8, 512, 128), BF),
            shape((8, 128), jnp.int32),
        ),
        in_specs=[ANY] * 6,
        out_specs=(ANY,) * 6,
        scratch_shapes=[
            pltpu.VMEM((2, 256, 4096), BF),
            pltpu.VMEM((2, 2, 4, 4, 256, 128), BF),
            pltpu.VMEM((2, 512, 256), F32),
            pltpu.VMEM((4, 512, 128), BF),
            pltpu.VMEM((8, 512, 128), BF),
            pltpu.VMEM((256, 512), BF),
            pltpu.VMEM((256, 512), BF),
            pltpu.VMEM((2, 128), jnp.int32),
            pltpu.VMEM((32, 128), jnp.int32),
            pltpu.VMEM((8, 272, 128), BF),
            pltpu.VMEM((8, 272, 128), BF),
            pltpu.VMEM((4096, 256), BF),
            pltpu.VMEM((128, 4096), BF),
            pltpu.VMEM((8, 256, 512), BF),
            pltpu.VMEM((8, 512, 128), BF),
            pltpu.VMEM((8, 128), jnp.int32),
            DMA((10,)), DMA((19,)), DMA((3,)), DMA((3,)),
            DMA((2, 2, 4, 4, 2)), DMA((2, 2, 4, 4, 2)),
            DMA((2, 4)), DMA((2, 4)),
            DMA((4, 2)), DMA((2, 4)),
            DMA((2, 4)), DMA((2, 4)),
        ],
        compiler_params=params(1),
        name="front",
    )(enc, dec_query[0], ctx_grad[0], kv_weight, dseg, eseg)

    dkvp, dqp = pl.pallas_call(
        attend,
        out_shape=(shape((8, 512, 128), BF), shape((8, 128, 128), BF)),
        in_specs=[ANY] * 5,
        out_specs=(ANY, ANY),
        scratch_shapes=[
            pltpu.SMEM((8, 128), jnp.int32),
            pltpu.VMEM((4096, 256), BF),
            pltpu.VMEM((128, 4096), BF),
            pltpu.VMEM((8, 256, 512), BF),
            pltpu.VMEM((8, 512, 128), BF),
            pltpu.VMEM((4096, 512), F32),
            pltpu.VMEM((4096, 256), BF),
            pltpu.VMEM((4096, 128), F32),
            pltpu.VMEM((8, 512, 128), BF),
            pltpu.VMEM((8, 128, 128), BF),
            DMA((3,)), DMA((8,)), DMA((8,)), DMA((8,)), DMA((8,)),
        ],
        compiler_params=params(),
        name="attend",
    )(spans, kvx, kvt, xt, xs)

    grads = pl.pallas_call(
        back,
        out_shape=(shape((256, 1024), BF), shape((256, 512), BF), shape((2, 128, 512), F32)),
        in_specs=[ANY, ANY, ANY, ANY],
        out_specs=(ANY, ANY, ANY),
        scratch_shapes=[
            pltpu.VMEM((256, 1024), BF),
            pltpu.VMEM((256, 512), BF),
            pltpu.VMEM((512, 4096), BF),
            pltpu.VMEM((2, 2, 2, 4, 4, 256, 128), BF),
            pltpu.VMEM((4, 512, 128), BF),
            pltpu.VMEM((4, 512, 128), BF),
            pltpu.VMEM((4, 512, 128), BF),
            pltpu.VMEM((4, 512, 128), BF),
            pltpu.VMEM((2, 256, 512), BF),
            pltpu.VMEM((2, 2, 256, 256), BF),
            pltpu.VMEM((8, 128, 128), BF),
            pltpu.VMEM((2, 5, 2, 128, 256), BF),
            pltpu.VMEM((2, 5, 2, 128, 256), BF),
            pltpu.VMEM((2, 5, 2, 256, 256), BF),
            pltpu.VMEM((2, 5, 2, 256, 256), BF),
            pltpu.VMEM((2, 4, 256, 256), F32),
            pltpu.VMEM((2, 256, 256), F32),
            pltpu.VMEM((2, 128, 256), F32),
            pltpu.VMEM((2, 2, 256, 256), BF),
            pltpu.VMEM((2, 2, 256, 256), BF),
            pltpu.VMEM((2, 2, 2, 256, 256), BF),
            pltpu.VMEM((2, 2, 2, 256, 256), BF),
            DMA((10,)), DMA((9,)), DMA((9,)),
            DMA((4,)), DMA((4,)),
            DMA((2, 4)), DMA((2, 4)),
            DMA((2, 5, 2)), DMA((2, 5, 2)),
            DMA((2, 5, 2)), DMA((2, 5, 2)),
            DMA((6,)), DMA((6,)),
        ],
        compiler_params=params(2),
        name="back",
    )(dkvp, dqp, enc, wg)

    enc_grad, q_grad, w_grad = pl.pallas_call(
        finish,
        out_shape=(shape((256, 1024), BF), shape((256, 512), BF), shape((2, 128, 512), F32)),
        in_specs=[ANY] * 3,
        out_specs=(ANY, ANY, ANY),
        scratch_shapes=[
            pltpu.VMEM((256, 1024), BF), pltpu.VMEM((256, 512), BF), pltpu.VMEM((2, 128, 512), F32),
            DMA((3, 4)), DMA((3, 4)),
        ],
        compiler_params=params(),
        name="finish",
    )(*grads)
    return enc_grad[None], q_grad[None], w_grad


def solution(mesh):
    placed = (
        P("dp", "seq", None),
        P("dp", "seq", "mp"),
        P("dp", "seq", "mp"),
        P(None, ("dp", "seq"), "mp"),
        P("dp", None),
        P("dp", "seq"),
    )
    return jax.shard_map(
        body,
        mesh=mesh,
        in_specs=placed,
        out_specs=(P("dp", "seq", "mp"), P("dp", "seq", "mp"), P(None, ("dp", "seq"), "mp")),
        check_vma=False,
    )
```
